512 devices in a mesh: layer: 4 (over z_lo, core), row: 4 (over z_hi), col: 32 (over x, y).
Axes of the slice: x: 4, y: 8, z: 8 (z_hi: 4, z_lo: 2; z = z_hi * 2 + z_lo), core: 2. Of those that a mesh axis runs over, the one named last changes fastest.
Arguments:
- sources: float32 [8, 256, 16384], P('layer', 'row', 'col'), may hold values from -14 to 14
- conduct: float32 [8, 256, 16384], P('layer', 'row', 'col'), may hold values from 0.5 to 4
- via_cond: float32 [8, 256, 16384], P('layer', 'row', 'col'), may hold values from 0.5 to 4
- via_map: int32 [8, 256, 16384], P('layer', 'row', 'col'), may hold values 0 or 1
- pad_map: int32 [256, 16384], P('row', 'col'), may hold values 0 or 1
- port_tile: int32 [4, 512], replicated, may hold values from 0 to 16383
- pivots: float32 [4, 512, 512], P(None, 'col'), may hold values from -1 to 2, as said below
- coupling: float32 [3, 512, 512], P(None, 'col'), may hold values from -0.109375 to 0.109375
Outputs:
- drop: float32 [8, 256, 16384], P('layer', 'row', 'col')
- ports: float32 [4, 512], replicated
The draws below stay inside these ranges and needn't reach their ends.
Inputs may be any that keep to these rules, and one draw needn't show every extreme that they name: `pivots`: each block is symmetric.
All inputs are finite; a program needn't handle non-finite values. No bound on the sum of `via_map` or of `pad_map` on one device may be relied on, other than what follows from the above.
Results may differ from the reference program's by a relative error of at most 0.00023.
Values sent between devices are 32-bit elements; how exact they have to be, the bound alone decides.
A program may use at most 64 MiB of HBM per device.

```python
import math
import jax
import jax.numpy as jnp
from jax import lax

TILE = 16
PANEL = 512
NPANEL = 4
DEG = 3
ITERS = 2
NL = 8
NR = 256
NC = 16384
NTILES = 16384


def draw_sources(key, part):
    rough_key = jax.random.fold_in(key, 0)
    return jnp.clip(jax.random.normal(rough_key, (NL, NR, NC), jnp.float32), -6.0, 6.0)


def draw_pivots(key, part):
    rough_key, diag_key = jax.random.split(jax.random.fold_in(key, 17))
    spread = jax.random.normal(rough_key, (NPANEL, PANEL, PANEL), jnp.float32) * (0.4 / math.sqrt(PANEL))
    symmetric = (spread + jnp.transpose(spread, (0, 2, 1))) * 0.7071
    leading = jax.random.uniform(diag_key, (NPANEL, PANEL, 1), jnp.float32, 0.5, 1.0)
    identity = (lax_iota_rows() == lax_iota_cols()).astype(jnp.float32)
    return symmetric + identity * leading


def lax_iota_rows():
    return jnp.arange(PANEL, dtype=jnp.int32)[None, :, None]


def lax_iota_cols():
    return jnp.arange(PANEL, dtype=jnp.int32)[None, None, :]


def touch_ends(values, own_key, least, top_value):
    extent = values.shape
    spot = [jax.random.randint(jax.random.fold_in(own_key, axis), (), 0, extent[axis]) for axis in range(len(extent))]
    values = values.at[tuple(spot)].set(least)
    longest = extent.index(max(extent))
    spot[longest] = (spot[longest] + 1) % extent[longest]
    return values.at[tuple(spot)].set(top_value)


def steps_of(key, dims, pieces, least, largest):
    def one(axis_at, blocks):
        draws = jax.random.uniform(jax.random.fold_in(jax.random.fold_in(key, 6), axis_at), (blocks,), jnp.float32, least / len(pieces), largest / len(pieces))
        return jnp.repeat(jnp.exp(draws), dims[axis_at] // blocks).reshape((-1,) + (1,) * (len(dims) - axis_at - 1))

    level = one(*pieces[0])
    for cut in pieces[1:]:
        level = level * one(*cut)
    return level


def noise(stream_key, dims, deviation, limit, cuts=(), held_as=jnp.bfloat16):
    values = jax.random.normal(stream_key, dims, jnp.float32) * deviation
    if len(cuts) > 0:
        values = steps_of(stream_key, dims, cuts, -0.22, 0.18) * values
    return jnp.clip(values, min=-limit, max=limit).astype(held_as)


def setup_inputs(seed: int = 0) -> dict:
    splits = jax.random.split(jax.random.key(seed), 9)
    sources = draw_sources(jax.random.fold_in(splits[8], 71), 0)
    conduct = jnp.clip(jnp.exp(math.log(4.0) - 2.0794415 * jax.random.uniform(splits[1], (NL, NR, NC), jnp.float32) ** steps_of(splits[1], (NL, NR, NC), ((0, 4), (1, 4), (2, 32)), -0.2, 0.2)), 0.5, 4.0)
    via_cond = jnp.clip(jnp.exp(math.log(4.0) - 2.0794415 * jax.random.uniform(splits[2], (NL, NR, NC), jnp.float32) ** steps_of(splits[2], (NL, NR, NC), ((0, 4), (1, 4), (2, 32)), -0.2, 0.2)), 0.5, 4.0)
    via_map = touch_ends((jax.random.randint(splits[3], (NL, NR, NC), 0, 4) < 3).astype(jnp.int32), jax.random.fold_in(splits[3], 1), 0, 1)
    pad_map = touch_ends((jax.random.randint(splits[4], (NR, NC), 0, 16) < 1).astype(jnp.int32), jax.random.fold_in(splits[4], 1), 0, 1)
    port_tile = touch_ends(jax.random.randint(splits[5], (NPANEL, PANEL), 0, NTILES), jax.random.fold_in(splits[5], 1), 0, NTILES - 1).astype(jnp.int32)
    pivots = draw_pivots(jax.random.fold_in(splits[8], 71), 0)
    coupling = noise(splits[7], (NPANEL - 1, PANEL, PANEL), (6 * PANEL) ** -0.5, 0.109375, ((1, 32),), jnp.float32)
    return dict(sources=sources, conduct=conduct, via_cond=via_cond, via_map=via_map, pad_map=pad_map, port_tile=port_tile, pivots=pivots, coupling=coupling)


pad_gain = 8.0
bound_low = 0.1
bound_high = 1.9
restrict_scale = 0.25
prolong_scale = 0.5

def shifted(grown):
    return (grown[2:, 1:-1, 1:-1], grown[:-2, 1:-1, 1:-1], grown[1:-1, 2:, 1:-1], grown[1:-1, :-2, 1:-1], grown[1:-1, 1:-1, 2:], grown[1:-1, 1:-1, :-2])

def apply_grid(field, weights, pad_term):
    result = pad_term * field
    for weight, other in zip(weights, shifted(jnp.pad(field, 1))):
        result = result + weight * (field - other)
    return result

def smooth(resid, weights, pad_term, inverse):
    theta = (bound_high + bound_low) / 2.0
    delta = (bound_high - bound_low) / 2.0
    sigma = theta / delta
    rho = 1.0 / sigma
    change = inverse * resid / theta
    total = change
    for sweep in range(DEG - 1):
        remain = resid - apply_grid(total, weights, pad_term)
        rho_new = 1.0 / (2.0 * sigma - rho)
        change = rho_new * rho * change + 2.0 * rho_new / delta * inverse * remain
        total = total + change
        rho = rho_new
    return total

def coarse(resid, port_tile, pivots, coupling):
    highest = lax.Precision.HIGHEST
    plane = lax.optimization_barrier(jnp.sum(resid, axis=0))
    tiles = plane.reshape(NR // TILE, TILE, NC // TILE, TILE).sum(axis=(1, 3)).reshape(-1)
    rhs = tiles[port_tile] * (restrict_scale / TILE)
    forward = [rhs[0]]
    for section in range(1, NPANEL):
        forward.append(rhs[section] - jnp.dot(coupling[section - 1], forward[-1], precision=highest))
    scaled = [jnp.dot(pivots[section], forward[section], precision=highest) for section in range(NPANEL)]
    results = [scaled[NPANEL - 1]]
    for section in range(NPANEL - 2, -1, -1):
        results.insert(0, scaled[section] - jnp.dot(results[0], coupling[section], precision=highest))
    ports = jnp.stack(results)
    tile_values = jax.ops.segment_sum(ports.reshape(-1), port_tile.reshape(-1).astype(jnp.int32), num_segments=NTILES)
    tile_grid = tile_values.reshape(NR // TILE, 1, NC // TILE, 1)
    field = jnp.broadcast_to(tile_grid, (NR // TILE, TILE, NC // TILE, TILE)).reshape(NR, NC) * prolong_scale
    return (ports, jnp.broadcast_to(field[None], (NL, NR, NC)))

def reference(sources, conduct, via_cond, via_map, pad_map, port_tile, pivots, coupling):
    vertical = via_cond * via_map.astype(jnp.float32)
    near_plane = shifted(jnp.pad(conduct, 1))
    near_vert = shifted(jnp.pad(vertical, 1))
    weights = (jnp.sqrt(vertical * near_vert[0]), jnp.sqrt(vertical * near_vert[1]), jnp.sqrt(conduct * near_plane[2]), jnp.sqrt(conduct * near_plane[3]), jnp.sqrt(conduct * near_plane[4]), jnp.sqrt(conduct * near_plane[5]))
    pad_term = jnp.zeros((NL, NR, NC), jnp.float32).at[NL - 1].set(pad_gain * pad_map.astype(jnp.float32))
    diagonal = pad_term
    for weight in weights:
        diagonal = diagonal + weight
    inverse = 1.0 / diagonal
    drop = jnp.zeros((NL, NR, NC), jnp.float32)
    ports = jnp.zeros((NPANEL, PANEL), jnp.float32)
    for outer in range(ITERS):
        resid = sources - apply_grid(drop, weights, pad_term)
        ports, lifted = coarse(resid, port_tile, pivots, coupling)
        drop = drop + lifted + smooth(resid, weights, pad_term, inverse)
    return (drop, ports)
```

```python
import jax
import jax.numpy as jnp
from jax import lax
from jax.experimental import pallas as pl
from jax.experimental.pallas import tpu as pltpu
from jax.sharding import PartitionSpec as P

F32 = jnp.float32
BF16 = jnp.bfloat16
MESH = pl.DeviceIdType.MESH

TILE = 16
PANEL = 512
NPANEL = 4
NX, NY = 4, 8
NCOL = NX * NY
ROWS, COLS = 64, 512
SHARE = PANEL // NCOL
HALF = SHARE // 2

pad_gain = 8.0
bound_low = 0.1
bound_high = 1.9
restrict_scale = 0.25
prolong_scale = 0.5
theta = (bound_high + bound_low) / 2.0
delta = (bound_high - bound_low) / 2.0
sigma = theta / delta


def iota(shape, axis):
    return lax.broadcasted_iota(jnp.int32, shape, axis)


def pieces(x):
    high = x.astype(BF16).astype(F32)
    rest = x - high
    mid = rest.astype(BF16).astype(F32)
    return high, mid, rest - mid


def stacked(x):
    return jnp.concatenate(pieces(x), axis=0).astype(BF16)


def added(y):
    n = y.shape[0] // 3
    return y[:n] + y[n : 2 * n] + y[2 * n :]


def dot(a, b):
    return lax.dot_general(a, b, (((1,), (0,)), ((), ())), preferred_element_type=F32)


def dot_t(a, b):
    return lax.dot_general(a, b, (((1,), (1,)), ((), ())), preferred_element_type=F32)


def kernel(
    src, cond, via, vmap, pad, pt, piv, coup,
    drop_out, ports_out,
    S, V, INV, DP, VS, Q, T, CH, HSEND, HALO, RSEND, RIM, CSEND, SIDE,
    G, PART, ZSEND, Z, XM, X, CSND, CZ, CXM, CX, SBM, SB, LANES, ROWM, E4, MAPS, LIFT,
    hs, hr, gys, gyr, gxs, gxr, gfs, gfr, gbs, gbr, zs, zr, xs, xr, bs, br,
):
    l, r, c = lax.axis_index("layer"), lax.axis_index("row"), lax.axis_index("col")
    core = lax.rem(l, 2)
    x, y = c // NY, lax.rem(c, NY)

    def at_col(px, py):
        return (l, r, px * NY + py)

    group = [(lax.rem(l + d % 4, 4), lax.rem(r + d // 4, 4), c) for d in range(1, 16)]
    plane_peers = [(l, r, lax.rem(c + d, NCOL)) for d in range(1, NCOL)]
    sibling = (l + 1 - 2 * core, r, c)

    barrier = pltpu.get_barrier_semaphore()
    for peer in group + plane_peers:
        pl.semaphore_signal(barrier, inc=1, device_id=peer, device_id_type=MESH)

    def remote(a, b, ssem, rsem, peer):
        return pltpu.make_async_remote_copy(
            src_ref=a, dst_ref=b, send_sem=ssem, recv_sem=rsem, device_id=peer, device_id_type=MESH
        )

    for p in range(2):
        S[p] = jnp.sqrt(cond[p])
        V[p] = jnp.sqrt(via[p]) * vmap[p].astype(F32)
    E4[...] = jnp.where(
        iota((COLS, 128), 0) // TILE == lax.rem(iota((COLS, 128), 1), 32), 1.0, 0.0
    ).astype(BF16)

    def tile_row(plane):
        parts = [plane[TILE * a : TILE * a + 8] + plane[TILE * a + 8 : TILE * a + 16] for a in range(4)]
        sums = added(dot(stacked(jnp.concatenate(parts, axis=0)), E4[...]))
        own = iota((32, 128), 0) // 8 == iota((32, 128), 1) // 32
        return jnp.sum(jnp.where(own, sums, 0.0), axis=0, keepdims=True)

    zero_plane = jnp.zeros((ROWS, COLS), F32)

    @pl.when(l == 0)
    def _():
        for rd in range(6):
            HALO[rd, 0] = zero_plane

    @pl.when(l == 3)
    def _():
        for rd in range(6):
            HALO[rd, 1] = zero_plane

    @pl.when(r == 0)
    def _():
        for rd in range(6):
            RIM[rd, 0] = jnp.zeros((2, COLS), F32)

    @pl.when(r == 3)
    def _():
        for rd in range(6):
            RIM[rd, 1] = jnp.zeros((2, COLS), F32)

    @pl.when(c == 0)
    def _():
        for rd in range(6):
            SIDE[rd, 0] = jnp.zeros((1, 128), F32)

    @pl.when(c == NCOL - 1)
    def _():
        for rd in range(6):
            SIDE[rd, 1] = jnp.zeros((1, 128), F32)

    def layer_copies(rd):
        up = remote(HSEND.at[rd, 1], HALO.at[rd, 0], hs.at[rd, 0], hr.at[rd, 0], (lax.rem(l + 1, 4), r, c))
        down = remote(HSEND.at[rd, 0], HALO.at[rd, 1], hs.at[rd, 1], hr.at[rd, 1], (lax.rem(l + 3, 4), r, c))
        return ((l < 3, up, l > 0), (l > 0, down, l < 3))

    def rim_copies(rd):
        south = remote(RSEND.at[rd, 1], RIM.at[rd, 0], hs.at[rd, 2], hr.at[rd, 2], (l, lax.rem(r + 1, 4), c))
        north = remote(RSEND.at[rd, 0], RIM.at[rd, 1], hs.at[rd, 3], hr.at[rd, 3], (l, lax.rem(r + 3, 4), c))
        east = remote(CSEND.at[rd, 1], SIDE.at[rd, 0], hs.at[rd, 4], hr.at[rd, 4], (l, r, lax.rem(c + 1, NCOL)))
        west = remote(
            CSEND.at[rd, 0], SIDE.at[rd, 1], hs.at[rd, 5], hr.at[rd, 5], (l, r, lax.rem(c + NCOL - 1, NCOL))
        )
        return (
            (r < 3, south, r > 0),
            (r > 0, north, r < 3),
            (c < NCOL - 1, east, c > 0),
            (c > 0, west, c < NCOL - 1),
        )

    def start(copies):
        for sends, copy, _ in copies:
            @pl.when(sends)
            def _():
                copy.start()

    def arrive(copies):
        for _, copy, receives in copies:
            @pl.when(receives)
            def _():
                copy.wait_recv()

    def left(copies):
        for sends, copy, _ in copies:
            @pl.when(sends)
            def _():
                copy.wait_send()

    def send_layers(rd, h):
        for p in range(2):
            HSEND[rd, p] = h[p]
        start(layer_copies(rd))

    def send_rims(rd, g):
        for p in range(2):
            RSEND[rd, 0, p : p + 1] = g[p][:1]
            RSEND[rd, 1, p : p + 1] = g[p][ROWS - 1 :]
        first = jnp.concatenate([g[0][:, :128], g[1][:, :128]], axis=0)
        last = jnp.concatenate([g[0][:, COLS - 128 :], g[1][:, COLS - 128 :]], axis=0)
        CSEND[rd, 0] = first.T[:1]
        CSEND[rd, 1] = last.T[127:]
        start(rim_copies(rd))

    def column(rim):
        return jnp.broadcast_to(rim, (128, 128)).T

    row_at = iota((ROWS, COLS), 0)
    col_at = iota((ROWS, 128), 1)

    def from_east(g, side):
        moved = pltpu.roll(g, COLS - 1, 1)
        edge = jnp.where(col_at == 127, side, moved[:, COLS - 128 :])
        return jnp.concatenate([moved[:, : COLS - 128], edge], axis=1)

    def from_west(g, side):
        moved = pltpu.roll(g, 1, 1)
        edge = jnp.where(col_at == 0, side, moved[:, :128])
        return jnp.concatenate([edge, moved[:, 128:]], axis=1)

    def from_south(g, rim):
        return jnp.where(row_at == ROWS - 1, rim, pltpu.roll(g, ROWS - 1, 0))

    def from_north(g, rim):
        return jnp.where(row_at == 0, rim, pltpu.roll(g, 1, 0))

    def plane_sum(g, north, south, west, east):
        west, east = column(west), column(east)
        out = []
        for p in range(2):
            rows = slice(ROWS * p, ROWS * (p + 1))
            out.append(
                from_north(g[p], north[p : p + 1])
                + from_south(g[p], south[p : p + 1])
                + from_west(g[p], west[rows])
                + from_east(g[p], east[rows])
            )
        return out

    def received_sum(rd, g):
        return plane_sum(g, RIM[rd, 0], RIM[rd, 1], SIDE[rd, 0], SIDE[rd, 1])

    def group_copies(it, rows, buf, send):
        slot = r * 4 + l
        return [
            remote(send, buf.at[slot], zs.at[it, d], zr.at[it, d], peer) for d, peer in enumerate(group)
        ]

    def plane_copies(it, send, buf, ss, rs):
        return [remote(send, buf.at[c], ss.at[it, d], rs.at[it, d], peer) for d, peer in enumerate(plane_peers)]

    rim0 = [S[0], S[1]]
    plane = src[0] + src[1]
    ZSEND[0] = tile_row(plane)

    lane_of = []
    for k in range(NPANEL):
        tile = pt[k : k + 1, :]
        arow, acol = tile // 1024, lax.rem(tile, 1024)
        lane = lax.rem(arow, 4) * 32 + lax.rem(acol, 32)
        maprow = (acol // 32) * 4 + arow // 4
        LANES[k] = jnp.where(iota((128, PANEL), 0) == lane, 1.0, 0.0).astype(BF16)
        ROWM[k : k + 1] = maprow

    pl.semaphore_wait(barrier, 15 + 31)

    send_layers(0, [V[0], V[1]])
    send_rims(0, rim0)

    G[core, x, y] = coup[:, pl.ds(pl.multiple_of(core * HALF, HALF), HALF), :]
    mine = G.at[core, x, y]
    copies_y = [
        remote(mine, mine, gys.at[d - 1], gyr.at[d - 1], at_col(x, lax.rem(y + d, NY))) for d in range(1, NY)
    ]

    def copies_x(d):
        piece = G.at[core, x, lax.rem(y + NY - d, NY)]
        return [
            remote(piece, piece, gxs.at[s, d], gxr.at[s, d], at_col(lax.rem(x + step, NX), y))
            for s, step in enumerate((1, 3))
        ]

    turn = 1 - 2 * core

    def copy_forward(d):
        piece = G.at[core, lax.rem(x - turn + NX, NX), lax.rem(y + NY - d, NY)]
        return remote(piece, piece, gfs.at[d], gfr.at[d], at_col(lax.rem(x + turn + NX, NX), y))

    def copy_sibling(j):
        block = G.at[core, lax.rem(x + j, NX)]
        return remote(block, block, gbs.at[j], gbr.at[j], sibling)

    group_first = group_copies(0, 1, Z.at[0], ZSEND.at[0])
    for copy in group_first:
        copy.start()
    for d in (1, 7, 2, 6, 3, 5, 4):
        copies_y[d - 1].start()
    for copy in copies_x(0):
        copy.start()

    def forward_x(*ds):
        for d in ds:
            copies_y[d - 1].wait_recv()
            for copy in copies_x(d):
                copy.start()

    def forward_more(*ds):
        for d in ds:
            for copy in copies_x(d):
                copy.wait_recv()
            copy_forward(d).start()

    arrive(layer_copies(0))
    arrive(rim_copies(0))
    s = [S[0], S[1]]
    v = [V[0], V[1]]
    around = received_sum(0, s)
    top = (l == 3).astype(F32)
    pads = pad_gain * pad[...].astype(F32) * top
    vsum = [HALO[0, 0] + v[1], v[0] + HALO[0, 1]]
    for p in range(2):
        dp = s[p] * around[p]
        if p == 1:
            dp = dp + pads
        inv = 1.0 / (dp + v[p] * vsum[p])
        t = inv * src[p]
        DP[p], INV[p], VS[p], Q[p], T[p], CH[p] = dp, inv, vsum[p], t, t, t
    send_layers(1, [v[p] * T[p] for p in range(2)])
    send_rims(1, [s[p] * T[p] for p in range(2)])

    forward_x(1, 7)

    def gather_plane(it, buf, msg, bufx):
        for q in range(4):
            total = buf[4 * q]
            for k in range(1, 4):
                total = total + buf[4 * q + k]
            msg[q : q + 1] = total
        bufx[c] = msg[...]
        out = plane_copies(it, msg, bufx, xs, xr)
        for copy in out:
            copy.start()
        return out

    Z[0, r * 4 + l] = ZSEND[0]
    for copy in group_first:
        copy.wait_recv()
    plane_first = gather_plane(0, Z.at[0], XM.at[0], X.at[0])

    west_col, east_col = SIDE[0, 0], SIDE[0, 1]
    east_side = column(east_col)
    edge_e = jnp.zeros((ROWS, COLS), F32)
    edge_s = jnp.zeros((ROWS, COLS), F32)
    for p in range(2):
        edge_e = edge_e + s[p] * from_east(s[p], east_side[ROWS * p : ROWS * (p + 1)])
        edge_s = edge_s + s[p] * from_south(s[p], RIM[0, 1, p : p + 1])
    edge_e = jnp.where(lax.rem(iota((ROWS, COLS), 1), TILE) == TILE - 1, edge_e, 0.0)
    edge_s = jnp.where(lax.rem(iota((ROWS, COLS), 0), TILE) == TILE - 1, edge_s, 0.0)
    for k, field in enumerate((pads, edge_e, edge_s)):
        CSND[k : k + 1] = tile_row(field)
    CZ[r * 4 + l] = CSND[...]
    group_coef = group_copies(1, 3, CZ, CSND)
    for copy in group_coef:
        copy.start()

    forward_x(2, 6)

    def sweep(rd, rho, s, v):
        rho_new = 1.0 / (2.0 * sigma - rho)
        t = [T[0], T[1]]
        arrive(rim_copies(rd))
        around = received_sum(rd, [s[p] * t[p] for p in range(2)])
        arrive(layer_copies(rd))
        vert = [HALO[rd, 0] + v[1] * t[1], v[0] * t[0] + HALO[rd, 1]]
        for p in range(2):
            remain = Q[p] - t[p] + INV[p] * (s[p] * around[p] + v[p] * vert[p])
            ch = (rho_new * rho) * CH[p] + (2.0 * rho_new / delta) * remain
            CH[p] = ch
            T[p] = t[p] + ch
        return rho_new

    rho = sweep(1, 1.0 / sigma, s, v)
    send_layers(2, [v[p] * T[p] for p in range(2)])
    send_rims(2, [s[p] * T[p] for p in range(2)])

    forward_x(3, 5, 4)
    copy_sibling(0).start()

    for copy in group_coef:
        copy.wait_recv()
    for q in range(4):
        total = CZ[4 * q]
        for k in range(1, 4):
            total = total + CZ[4 * q + k]
        for k in range(3):
            CXM[k, q : q + 1] = total[k : k + 1]
    CX[c] = CXM[...]
    plane_coef = plane_copies(1, CXM, CX, xs, xr)
    for copy in plane_coef:
        copy.start()

    sweep(2, rho, s, v)
    send_layers(3, [v[p] * T[p] for p in range(2)])
    send_rims(3, [s[p] * T[p] for p in range(2)])

    forward_more(0, 1, 7)

    def tile_map(load):
        return jnp.concatenate([load(k) for k in range(NCOL)], axis=0)

    def row_mask(k):
        return iota((128, PANEL), 0) == ROWM[k : k + 1]

    def select_ports(tiles):
        parts = stacked(tiles)
        out = []
        for k in range(NPANEL):
            picked = added(dot(parts, LANES[k]))
            out.append(
                jnp.sum(jnp.where(row_mask(k), picked, 0.0), axis=0, keepdims=True) * (restrict_scale / TILE)
            )
        return out

    for copy in plane_first:
        copy.wait_recv()
    rhs = select_ports(tile_map(lambda k: X[0, k]))

    arrive(rim_copies(3))
    arrive(layer_copies(3))
    around = received_sum(3, [s[p] * T[p] for p in range(2)])
    vert = [HALO[3, 0] + v[1] * T[1], v[0] * T[0] + HALO[3, 1]]
    for p in range(2):
        t = T[p]
        Q[p] = src[p] - ((DP[p] + v[p] * VS[p]) * t - s[p] * around[p] - v[p] * vert[p])
    ZSEND[1] = tile_row(Q[0] + Q[1])
    Z[1, r * 4 + l] = ZSEND[1]
    group_second = group_copies(2, 1, Z.at[1], ZSEND.at[1])
    for copy in group_second:
        copy.start()

    forward_more(2, 6, 3, 5, 4)
    copy_sibling(1).start()
    copy_sibling(3).start()
    for copy in group_second:
        copy.wait_recv()
    plane_second = gather_plane(2, Z.at[1], XM.at[1], X.at[1])
    for d in range(NY):
        copy_forward(d).wait_recv()
    copy_sibling(2).start()
    for j in range(NX):
        copy_sibling(j).wait_recv()

    def minus(k, f):
        wide = jnp.broadcast_to(f, (8, PANEL))

        def body(i, carry):
            px, py = i // NY, lax.rem(i, NY)
            for h in range(2):
                prod = G[h, px, py, k] * wide
                part = prod[:, :128] + prod[:, 128:256] + prod[:, 256:384] + prod[:, 384:]
                PART[pl.ds(pl.multiple_of(i * SHARE + h * HALF, HALF), HALF)] = part
            return carry

        lax.fori_loop(0, NCOL, body, 0, unroll=8)
        return jnp.concatenate(
            [jnp.sum(PART[128 * j : 128 * (j + 1)].T, axis=0, keepdims=True) for j in range(4)], axis=1
        )

    def minus_transposed(k, f):
        for j in range(4):
            PART[128 * j : 128 * (j + 1)] = column(f[:, 128 * j : 128 * (j + 1)])

        def body(i, acc):
            px, py = i // NY, lax.rem(i, NY)
            for h in range(2):
                w = PART[pl.ds(pl.multiple_of(i * SHARE + h * HALF, HALF), HALF)]
                acc = acc + G[h, px, py, k] * jnp.concatenate([w] * 4, axis=1)
            return acc

        acc = lax.fori_loop(0, NCOL, body, jnp.zeros((8, PANEL), F32), unroll=8)
        return jnp.sum(acc, axis=0, keepdims=True)

    def solve_first(it, rhs):
        forward = [rhs[0]]
        for k in range(1, NPANEL):
            forward.append(rhs[k] - minus(k - 1, forward[-1]))
        rows = []
        for k in range(NPANEL):
            prod = piv[k] * forward[k]
            rows.append(prod[:, :128] + prod[:, 128:256] + prod[:, 256:384] + prod[:, 384:])
        rows.append(jnp.zeros((128 - NPANEL * SHARE, 128), F32))
        SBM[it] = jnp.sum(jnp.concatenate(rows, axis=0).T, axis=0, keepdims=True)
        SB[it, c] = SBM[it]
        copies = plane_copies(it, SBM.at[it], SB.at[it], bs, br)
        for copy in copies:
            copy.start()
        return copies

    def solve_second(it, copies):
        for copy in copies:
            copy.wait_recv()
        got = stacked(jnp.concatenate([SB[it, k] for k in range(NCOL)], axis=0))
        owner = iota((NCOL, PANEL), 1) // SHARE == iota((NCOL, PANEL), 0)
        scaled = []
        for k in range(NPANEL):
            spread = jnp.where(
                iota((128, PANEL), 0) == k * SHARE + lax.rem(iota((128, PANEL), 1), SHARE), 1.0, 0.0
            ).astype(BF16)
            value = added(dot(got, spread))
            scaled.append(jnp.sum(jnp.where(owner, value, 0.0), axis=0, keepdims=True))
        ports = [None] * NPANEL
        ports[NPANEL - 1] = scaled[NPANEL - 1]
        for k in range(NPANEL - 2, -1, -1):
            ports[k] = scaled[k] - minus_transposed(k, ports[k + 1])
        return ports

    def lifted_rows(ports, wanted):
        total = jnp.zeros((24, 128), F32)
        for k in range(NPANEL):
            parts = pieces(ports[k] * prolong_scale)
            masks = [ROWM[k : k + 1] == w for w in wanted]
            masks += [masks[0]] * (8 - len(masks))
            rows = [jnp.where(m, part, 0.0) for part in parts for m in masks]
            total = total + dot_t(jnp.concatenate(rows, axis=0).astype(BF16), LANES[k])
        return added(total)

    lane_row = iota((1, 128), 1)

    def spread_rows(rows):
        return added(dot_t(stacked(rows), E4[...]))

    def field_of(own):
        return jnp.concatenate([jnp.where(lane_row // 32 == min(a, 3), own, 0.0) for a in range(4)], axis=0)

    first = solve_first(0, rhs)
    ports1 = solve_second(0, first)

    own_row = c * 4 + r
    none = jnp.int32(-1)
    wanted = [
        own_row,
        jnp.where(r > 0, own_row - 1, none),
        jnp.where(r < 3, own_row + 1, none),
        jnp.where(c > 0, own_row - 4, none),
        jnp.where(c < NCOL - 1, own_row + 4, none),
    ]
    near = lifted_rows(ports1, wanted)
    level = jnp.concatenate(
        [
            field_of(near[0:1]),
            jnp.where(lane_row // 32 == 3, near[1:2], 0.0),
            jnp.where(lane_row // 32 == 0, near[2:3], 0.0),
            jnp.zeros((2, 128), F32),
        ],
        axis=0,
    )
    level = spread_rows(level)
    lift = jnp.concatenate(
        [jnp.broadcast_to(level[a : a + 1], (TILE, COLS)) for a in range(4)], axis=0
    )
    LIFT[...] = lift
    at_row = lax.rem(iota((128, 128), 1), ROWS) // TILE * 32
    pick_w = jnp.where(iota((128, 128), 0) == at_row + 31, 1.0, 0.0).astype(BF16)
    pick_e = jnp.where(iota((128, 128), 0) == at_row, 1.0, 0.0).astype(BF16)
    side_w = added(dot(stacked(near), pick_w))[3:4]
    side_e = added(dot(stacked(near), pick_e))[4:5]
    lifted_around = plane_sum(
        [s[p] * lift for p in range(2)],
        RIM[0, 0] * level[4:5],
        RIM[0, 1] * level[5:6],
        SIDE[0, 0] * side_w,
        SIDE[0, 1] * side_e,
    )
    for p in range(2):
        t3 = T[p]
        resid = Q[p] - (DP[p] * lift - s[p] * lifted_around[p])
        t = INV[p] * resid
        drop_out[p] = lift + t3
        Q[p], T[p], CH[p] = t, t, t
    send_layers(4, [v[p] * T[p] for p in range(2)])
    send_rims(4, [s[p] * T[p] for p in range(2)])

    lifted_map = jnp.zeros((384, 128), F32)
    for k in range(NPANEL):
        mask = row_mask(k)
        parts = [jnp.where(mask, part, 0.0).astype(BF16) for part in pieces(ports1[k] * prolong_scale)]
        lifted_map = lifted_map + dot_t(jnp.concatenate(parts, axis=0), LANES[k])
    lifted_map = added(lifted_map)
    for copy in plane_coef:
        copy.wait_recv()
    pads_map = tile_map(lambda k: CX[k, 0])
    edge_e = tile_map(lambda k: CX[k, 1])
    edge_s = tile_map(lambda k: CX[k, 2])
    lanes = iota((128, 128), 1)

    def tile_east(a):
        ahead = pltpu.roll(a, 124, 0)
        return jnp.where(lax.rem(lanes, 32) == 31, pltpu.roll(ahead, 31, 1), pltpu.roll(a, 127, 1))

    def tile_west(a):
        behind = pltpu.roll(a, 4, 0)
        return jnp.where(lax.rem(lanes, 32) == 0, pltpu.roll(behind, 97, 1), pltpu.roll(a, 1, 1))

    def tile_south(a):
        below = pltpu.roll(a, 127, 0)
        return jnp.where(lanes // 32 == 3, pltpu.roll(below, 96, 1), pltpu.roll(a, 96, 1))

    def tile_north(a):
        above = pltpu.roll(a, 1, 0)
        return jnp.where(lanes // 32 == 0, pltpu.roll(above, 32, 1), pltpu.roll(a, 32, 1))

    flow_e = edge_e * (lifted_map - tile_east(lifted_map))
    flow_s = edge_s * (lifted_map - tile_south(lifted_map))
    coarse = pads_map * lifted_map + flow_e - tile_west(flow_e) + flow_s - tile_north(flow_s)

    for copy in plane_second:
        copy.wait_recv()
    rhs = select_ports(tile_map(lambda k: X[1, k]) - coarse)
    second = solve_first(1, rhs)

    rho = sweep(4, 1.0 / sigma, s, v)
    send_layers(5, [v[p] * T[p] for p in range(2)])
    send_rims(5, [s[p] * T[p] for p in range(2)])

    ports2 = solve_second(1, second)
    for k in range(NPANEL):
        ports_out[k : k + 1] = ports2[k]
    near = lifted_rows(ports2, [own_row])
    level = spread_rows(jnp.concatenate([field_of(near[0:1])] * 2, axis=0))
    sweep(5, rho, s, v)
    for p in range(2):
        for a in range(4):
            rows = slice(TILE * a, TILE * (a + 1))
            drop_out[p, rows] = drop_out[p, rows] + T[p, rows] + level[a : a + 1]

    for rd in range(6):
        left(layer_copies(rd))
        left(rim_copies(rd))
    for copy in copies_y + group_first + group_coef + group_second:
        copy.wait_send()
    for copy in plane_first + plane_coef + plane_second + first + second:
        copy.wait_send()
    for d in range(NY):
        for copy in copies_x(d):
            copy.wait_send()
        copy_forward(d).wait_send()
    for j in range(NX):
        copy_sibling(j).wait_send()


def shards(*args):
    vmem = pl.BlockSpec(memory_space=pltpu.VMEM)
    field = pltpu.VMEM((2, ROWS, COLS), F32)
    dma = pltpu.SemaphoreType.DMA
    return pl.pallas_call(
        kernel,
        out_shape=(
            jax.ShapeDtypeStruct((2, ROWS, COLS), F32),
            jax.ShapeDtypeStruct((NPANEL, PANEL), F32),
        ),
        in_specs=[vmem] * 8,
        out_specs=(vmem, vmem),
        scratch_shapes=[
            field, field, field, field, field, field, field, field,
            pltpu.VMEM((6, 2, ROWS, COLS), F32),
            pltpu.VMEM((6, 2, ROWS, COLS), F32),
            pltpu.VMEM((6, 2, 2, COLS), F32),
            pltpu.VMEM((6, 2, 2, COLS), F32),
            pltpu.VMEM((6, 2, 1, 128), F32),
            pltpu.VMEM((6, 2, 1, 128), F32),
            pltpu.VMEM((2, NX, NY, NPANEL - 1, HALF, PANEL), F32),
            pltpu.VMEM((PANEL, 128), F32),
            pltpu.VMEM((2, 1, 128), F32),
            pltpu.VMEM((2, 16, 1, 128), F32),
            pltpu.VMEM((2, 4, 128), F32),
            pltpu.VMEM((2, NCOL, 4, 128), F32),
            pltpu.VMEM((3, 128), F32),
            pltpu.VMEM((16, 3, 128), F32),
            pltpu.VMEM((3, 4, 128), F32),
            pltpu.VMEM((NCOL, 3, 4, 128), F32),
            pltpu.VMEM((2, 1, 128), F32),
            pltpu.VMEM((2, NCOL, 1, 128), F32),
            pltpu.VMEM((NPANEL, 128, PANEL), BF16),
            pltpu.VMEM((NPANEL, PANEL), jnp.int32),
            pltpu.VMEM((COLS, 128), BF16),
            pltpu.VMEM((8, 128), F32),
            pltpu.VMEM((ROWS, COLS), F32),
            dma((6, 6)), dma((6, 6)),
            dma((7,)), dma((7,)),
            dma((2, 8)), dma((2, 8)),
            dma((8,)), dma((8,)),
            dma((4,)), dma((4,)),
            dma((3, 15)), dma((3, 15)),
            dma((3, 31)), dma((3, 31)),
            dma((2, 31)), dma((2, 31)),
        ],
        compiler_params=pltpu.CompilerParams(
            collective_id=0, has_side_effects=True, vmem_limit_bytes=48 * 1024 * 1024
        ),
        cost_estimate=pl.CostEstimate(flops=100_000_000, bytes_accessed=2_000_000, transcendentals=300_000),
        name="grid",
    )(*args)


def solution(mesh):
    placed = (
        P("layer", "row", "col"),
        P("layer", "row", "col"),
        P("layer", "row", "col"),
        P("layer", "row", "col"),
        P("row", "col"),
        P(),
        P(None, "col", None),
        P(None, "col", None),
    )
    return jax.shard_map(
        shards,
        mesh=mesh,
        in_specs=placed,
        out_specs=(P("layer", "row", "col"), P()),
        check_vma=False,
    )
```

```python
import jax
import jax.numpy as jnp
from jax import lax
from jax.experimental import pallas as pl
from jax.experimental.pallas import tpu as pltpu
from jax.sharding import PartitionSpec as P

F32 = jnp.float32
BF16 = jnp.bfloat16
MESH = pl.DeviceIdType.MESH

TILE = 16
PANEL = 512
NPANEL = 4
NX, NY = 4, 8
NCOL = NX * NY
ROWS, COLS = 64, 512
SHARE = PANEL // NCOL
HALF = SHARE // 2

pad_gain = 8.0
bound_low = 0.1
bound_high = 1.9
restrict_scale = 0.25
prolong_scale = 0.5
theta = (bound_high + bound_low) / 2.0
delta = (bound_high - bound_low) / 2.0
sigma = theta / delta


def iota(shape, axis):
    return lax.broadcasted_iota(jnp.int32, shape, axis)


def pieces(x):
    high = x.astype(BF16).astype(F32)
    rest = x - high
    mid = rest.astype(BF16).astype(F32)
    return high, mid, rest - mid


def stacked(x):
    return jnp.concatenate(pieces(x), axis=0).astype(BF16)


def added(y):
    n = y.shape[0] // 3
    return y[:n] + y[n : 2 * n] + y[2 * n :]


def dot(a, b):
    return lax.dot_general(a, b, (((1,), (0,)), ((), ())), preferred_element_type=F32)


def dot_t(a, b):
    return lax.dot_general(a, b, (((1,), (1,)), ((), ())), preferred_element_type=F32)


def kernel(
    src_in, cond_in, via_in, vmap_in, pad_in, pt_in, piv_in, coup_in,
    drop_out, ports_out,
    src, cond, via, vmap, pad, pt, piv,
    S, V, INV, DP, VS, Q, T, CH, HSEND, HALO, RSEND, RIM, CSEND, SIDE,
    G, GP, FW, SL, PART, ZSEND, Z, XM, X, CSND, CZ, CXM, CX, SBM, SB, LANES, ROWM, E4, MAPS, LIFT,
    ins, hs, hr, gys, gyr, gxs, gxr, gfs, gfr,
    pys, pyr, pxs, pxr, pfs, pfr, ls, lr, gbs, gbr, zs, zr, xs, xr, bs, br,
):
    l, r, c = lax.axis_index("layer"), lax.axis_index("row"), lax.axis_index("col")
    core = lax.rem(l, 2)
    x, y = c // NY, lax.rem(c, NY)

    def at_col(px, py):
        return (l, r, px * NY + py)

    group = [(lax.rem(l + d % 4, 4), lax.rem(r + d // 4, 4), c) for d in range(1, 16)]
    plane_peers = [(l, r, lax.rem(c + d, NCOL)) for d in range(1, NCOL)]
    sibling = (l + 1 - 2 * core, r, c)

    barrier = pltpu.get_barrier_semaphore()
    for peer in group + plane_peers:
        pl.semaphore_signal(barrier, inc=1, device_id=peer, device_id_type=MESH)

    def remote(a, b, ssem, rsem, peer):
        return pltpu.make_async_remote_copy(
            src_ref=a, dst_ref=b, send_sem=ssem, recv_sem=rsem, device_id=peer, device_id_type=MESH
        )

    inputs = [
        pltpu.make_async_copy(a, b, ins.at[n])
        for n, (a, b) in enumerate(
            (
                (via_in, via),
                (vmap_in, vmap),
                (cond_in, cond),
                (coup_in.at[:, pl.ds(pl.multiple_of(core * HALF, HALF), HALF), :], G.at[core, x, y]),
                (src_in, src),
                (pt_in, pt),
                (pad_in, pad),
                (piv_in, piv),
                (piv_in.at[l], GP.at[x, y]),
            )
        )
    ]
    for copy in inputs:
        copy.start()

    E4[...] = jnp.where(
        iota((COLS, 128), 0) // TILE == lax.rem(iota((COLS, 128), 1), 32), 1.0, 0.0
    ).astype(BF16)

    def tile_row(plane):
        parts = [plane[TILE * a : TILE * a + 8] + plane[TILE * a + 8 : TILE * a + 16] for a in range(4)]
        sums = added(dot(stacked(jnp.concatenate(parts, axis=0)), E4[...]))
        own = iota((32, 128), 0) // 8 == iota((32, 128), 1) // 32
        return jnp.sum(jnp.where(own, sums, 0.0), axis=0, keepdims=True)

    zero_plane = jnp.zeros((ROWS, COLS), F32)

    @pl.when(l == 0)
    def _():
        for rd in range(6):
            HALO[rd, 0] = zero_plane

    @pl.when(l == 3)
    def _():
        for rd in range(6):
            HALO[rd, 1] = zero_plane

    @pl.when(r == 0)
    def _():
        for rd in range(6):
            RIM[rd, 0] = jnp.zeros((2, COLS), F32)

    @pl.when(r == 3)
    def _():
        for rd in range(6):
            RIM[rd, 1] = jnp.zeros((2, COLS), F32)

    @pl.when(c == 0)
    def _():
        for rd in range(6):
            SIDE[rd, 0] = jnp.zeros((1, 128), F32)

    @pl.when(c == NCOL - 1)
    def _():
        for rd in range(6):
            SIDE[rd, 1] = jnp.zeros((1, 128), F32)

    def layer_copies(rd):
        up = remote(HSEND.at[rd, 1], HALO.at[rd, 0], hs.at[rd, 0], hr.at[rd, 0], (lax.rem(l + 1, 4), r, c))
        down = remote(HSEND.at[rd, 0], HALO.at[rd, 1], hs.at[rd, 1], hr.at[rd, 1], (lax.rem(l + 3, 4), r, c))
        return ((l < 3, up, l > 0), (l > 0, down, l < 3))

    def rim_copies(rd):
        south = remote(RSEND.at[rd, 1], RIM.at[rd, 0], hs.at[rd, 2], hr.at[rd, 2], (l, lax.rem(r + 1, 4), c))
        north = remote(RSEND.at[rd, 0], RIM.at[rd, 1], hs.at[rd, 3], hr.at[rd, 3], (l, lax.rem(r + 3, 4), c))
        east = remote(CSEND.at[rd, 1], SIDE.at[rd, 0], hs.at[rd, 4], hr.at[rd, 4], (l, r, lax.rem(c + 1, NCOL)))
        west = remote(
            CSEND.at[rd, 0], SIDE.at[rd, 1], hs.at[rd, 5], hr.at[rd, 5], (l, r, lax.rem(c + NCOL - 1, NCOL))
        )
        return (
            (r < 3, south, r > 0),
            (r > 0, north, r < 3),
            (c < NCOL - 1, east, c > 0),
            (c > 0, west, c < NCOL - 1),
        )

    def start(copies):
        for sends, copy, _ in copies:
            @pl.when(sends)
            def _():
                copy.start()

    def arrive(copies):
        for _, copy, receives in copies:
            @pl.when(receives)
            def _():
                copy.wait_recv()

    def left(copies):
        for sends, copy, _ in copies:
            @pl.when(sends)
            def _():
                copy.wait_send()

    def send_layers(rd, h):
        for p in range(2):
            HSEND[rd, p] = h[p]
        start(layer_copies(rd))

    def send_rims(rd, g):
        for p in range(2):
            RSEND[rd, 0, p : p + 1] = g[p][:1]
            RSEND[rd, 1, p : p + 1] = g[p][ROWS - 1 :]
        first = jnp.concatenate([g[0][:, :128], g[1][:, :128]], axis=0)
        last = jnp.concatenate([g[0][:, COLS - 128 :], g[1][:, COLS - 128 :]], axis=0)
        CSEND[rd, 0] = first.T[:1]
        CSEND[rd, 1] = last.T[127:]
        start(rim_copies(rd))

    def column(rim):
        return jnp.broadcast_to(rim, (128, 128)).T

    row_at = iota((ROWS, COLS), 0)
    col_at = iota((ROWS, 128), 1)

    def from_east(g, side):
        moved = pltpu.roll(g, COLS - 1, 1)
        edge = jnp.where(col_at == 127, side, moved[:, COLS - 128 :])
        return jnp.concatenate([moved[:, : COLS - 128], edge], axis=1)

    def from_west(g, side):
        moved = pltpu.roll(g, 1, 1)
        edge = jnp.where(col_at == 0, side, moved[:, :128])
        return jnp.concatenate([edge, moved[:, 128:]], axis=1)

    def from_south(g, rim):
        return jnp.where(row_at == ROWS - 1, rim, pltpu.roll(g, ROWS - 1, 0))

    def from_north(g, rim):
        return jnp.where(row_at == 0, rim, pltpu.roll(g, 1, 0))

    def plane_sum(g, north, south, west, east):
        west, east = column(west), column(east)
        out = []
        for p in range(2):
            rows = slice(ROWS * p, ROWS * (p + 1))
            out.append(
                from_north(g[p], north[p : p + 1])
                + from_south(g[p], south[p : p + 1])
                + from_west(g[p], west[rows])
                + from_east(g[p], east[rows])
            )
        return out

    def received_sum(rd, g):
        return plane_sum(g, RIM[rd, 0], RIM[rd, 1], SIDE[rd, 0], SIDE[rd, 1])

    def group_copies(it, rows, buf, send):
        slot = r * 4 + l
        return [
            remote(send, buf.at[slot], zs.at[it, d], zr.at[it, d], peer) for d, peer in enumerate(group)
        ]

    def plane_copies(it, send, buf, ss, rs):
        return [remote(send, buf.at[c], ss.at[it, d], rs.at[it, d], peer) for d, peer in enumerate(plane_peers)]

    for copy in inputs[:3]:
        copy.wait()
    for p in range(2):
        S[p] = jnp.sqrt(cond[p])
        V[p] = jnp.sqrt(via[p]) * vmap[p].astype(F32)
    for copy in inputs[3:5]:
        copy.wait()

    pl.semaphore_wait(barrier, 15 + 31)

    send_layers(0, [V[0], V[1]])
    send_rims(0, [S[0], S[1]])

    turn = 1 - 2 * core

    class Ring:
        def __init__(self, slot, ys, yr, xs, xr, fs, fr):
            self.slot, self.xs, self.xr, self.fs, self.fr = slot, xs, xr, fs, fr
            self.along_y = {}
            for d, began, step in (
                (1, 0, 1), (7, 0, NY - 1), (2, 0, 2), (6, 0, NY - 2),
                (3, 1, 2), (5, NY - 1, NY - 2), (4, 2 * turn + NY, 2 * turn + NY),
            ):
                piece = slot(x, lax.rem(y + 2 * NY - began, NY))
                self.along_y[d] = remote(
                    piece, piece, ys.at[d - 1], yr.at[d - 1], at_col(x, lax.rem(y + step, NY))
                )

        def along_x(self, d):
            piece = self.slot(x, lax.rem(y + NY - d, NY))
            return [
                remote(piece, piece, self.xs.at[s, d], self.xr.at[s, d], at_col(lax.rem(x + step, NX), y))
                for s, step in enumerate((1, 3))
            ]

        def onward(self, d):
            piece = self.slot(lax.rem(x - turn + NX, NX), lax.rem(y + NY - d, NY))
            return remote(piece, piece, self.fs.at[d], self.fr.at[d], at_col(lax.rem(x + turn + NX, NX), y))

        def begin(self):
            for d in (1, 7, 2, 6):
                self.along_y[d].start()

        def pass_y(self, *ds):
            for d in ds:
                self.along_y[d].wait_recv()
            for d in ds:
                if d in (1, 7):
                    self.along_y[{1: 3, 7: 5}[d]].start()
            if 2 in ds:
                self.along_y[4].start()

        def send_x(self, *ds):
            for d in ds:
                for copy in self.along_x(d):
                    copy.start()

        def pass_x(self, *ds):
            for d in ds:
                for copy in self.along_x(d):
                    copy.wait_recv()
                self.onward(d).start()

        def end(self):
            for d in range(NY):
                self.onward(d).wait_recv()

        def sent(self):
            for d in range(1, NY):
                self.along_y[d].wait_send()
            for d in range(NY):
                for copy in self.along_x(d):
                    copy.wait_send()
                self.onward(d).wait_send()

    lower = Ring(lambda px, py: G.at[core, px, py], gys, gyr, gxs, gxr, gfs, gfr)
    panel = Ring(lambda px, py: GP.at[px, py], pys, pyr, pxs, pxr, pfs, pfr)

    def copy_sibling(j):
        block = G.at[core, lax.rem(x + j, NX)]
        return remote(block, block, gbs.at[j], gbr.at[j], sibling)

    lower.begin()
    lower.send_x(0)
    ZSEND[0] = tile_row(src[0] + src[1])
    group_first = group_copies(0, 1, Z.at[0], ZSEND.at[0])
    for copy in group_first:
        copy.start()

    for copy in inputs[5:]:
        copy.wait()
    for k in range(NPANEL):
        tile = pt[k : k + 1, :]
        arow, acol = tile // 1024, lax.rem(tile, 1024)
        lane = lax.rem(arow, 4) * 32 + lax.rem(acol, 32)
        LANES[k] = jnp.where(iota((128, PANEL), 0) == lane, 1.0, 0.0).astype(BF16)
        ROWM[k : k + 1] = (acol // 32) * 4 + arow // 4

    arrive(layer_copies(0))
    arrive(rim_copies(0))
    s = [S[0], S[1]]
    v = [V[0], V[1]]
    around = received_sum(0, s)
    top = (l == 3).astype(F32)
    pads = pad_gain * pad[...].astype(F32) * top
    vsum = [HALO[0, 0] + v[1], v[0] + HALO[0, 1]]
    for p in range(2):
        dp = s[p] * around[p]
        if p == 1:
            dp = dp + pads
        inv = 1.0 / (dp + v[p] * vsum[p])
        t = inv * src[p]
        DP[p], INV[p], VS[p], Q[p], T[p], CH[p] = dp, inv, vsum[p], t, t, t
    send_layers(1, [v[p] * T[p] for p in range(2)])
    send_rims(1, [s[p] * T[p] for p in range(2)])

    lower.pass_y(1, 7)
    lower.send_x(1, 7)

    def gather_plane(it, buf, msg, bufx):
        for q in range(4):
            total = buf[4 * q]
            for k in range(1, 4):
                total = total + buf[4 * q + k]
            msg[q : q + 1] = total
        bufx[c] = msg[...]
        out = plane_copies(it, msg, bufx, xs, xr)
        for copy in out:
            copy.start()
        return out

    Z[0, r * 4 + l] = ZSEND[0]
    for copy in group_first:
        copy.wait_recv()
    plane_first = gather_plane(0, Z.at[0], XM.at[0], X.at[0])

    west_col, east_col = SIDE[0, 0], SIDE[0, 1]
    east_side = column(east_col)
    edge_e = jnp.zeros((ROWS, COLS), F32)
    edge_s = jnp.zeros((ROWS, COLS), F32)
    for p in range(2):
        edge_e = edge_e + s[p] * from_east(s[p], east_side[ROWS * p : ROWS * (p + 1)])
        edge_s = edge_s + s[p] * from_south(s[p], RIM[0, 1, p : p + 1])
    edge_e = jnp.where(lax.rem(iota((ROWS, COLS), 1), TILE) == TILE - 1, edge_e, 0.0)
    edge_s = jnp.where(lax.rem(iota((ROWS, COLS), 0), TILE) == TILE - 1, edge_s, 0.0)
    for k, field in enumerate((pads, edge_e, edge_s)):
        CSND[k : k + 1] = tile_row(field)
    CZ[r * 4 + l] = CSND[...]
    group_coef = group_copies(1, 3, CZ, CSND)
    for copy in group_coef:
        copy.start()

    lower.pass_y(2, 6)
    lower.send_x(2, 6)

    def sweep(rd, rho, s, v):
        rho_new = 1.0 / (2.0 * sigma - rho)
        t = [T[0], T[1]]
        arrive(rim_copies(rd))
        around = received_sum(rd, [s[p] * t[p] for p in range(2)])
        arrive(layer_copies(rd))
        vert = [HALO[rd, 0] + v[1] * t[1], v[0] * t[0] + HALO[rd, 1]]
        for p in range(2):
            remain = Q[p] - t[p] + INV[p] * (s[p] * around[p] + v[p] * vert[p])
            ch = (rho_new * rho) * CH[p] + (2.0 * rho_new / delta) * remain
            CH[p] = ch
            T[p] = t[p] + ch
        return rho_new

    rho = sweep(1, 1.0 / sigma, s, v)
    send_layers(2, [v[p] * T[p] for p in range(2)])
    send_rims(2, [s[p] * T[p] for p in range(2)])

    lower.pass_y(3, 5, 4)
    lower.send_x(3, 5, 4)
    panel.begin()
    copy_sibling(0).start()

    for copy in group_coef:
        copy.wait_recv()
    for q in range(4):
        total = CZ[4 * q]
        for k in range(1, 4):
            total = total + CZ[4 * q + k]
        for k in range(3):
            CXM[k, q : q + 1] = total[k : k + 1]
    CX[c] = CXM[...]
    plane_coef = plane_copies(1, CXM, CX, xs, xr)
    for copy in plane_coef:
        copy.start()

    sweep(2, rho, s, v)
    send_layers(3, [v[p] * T[p] for p in range(2)])
    send_rims(3, [s[p] * T[p] for p in range(2)])

    lower.pass_x(0, 1, 7)
    panel.pass_y(1, 7)

    def tile_map(load):
        return jnp.concatenate([load(k) for k in range(NCOL)], axis=0)

    def row_mask(k):
        return iota((128, PANEL), 0) == ROWM[k : k + 1]

    def select_ports(tiles):
        parts = stacked(tiles)
        out = []
        for k in range(NPANEL):
            picked = added(dot(parts, LANES[k]))
            out.append(
                jnp.sum(jnp.where(row_mask(k), picked, 0.0), axis=0, keepdims=True) * (restrict_scale / TILE)
            )
        return out

    for copy in plane_first:
        copy.wait_recv()
    rhs = select_ports(tile_map(lambda k: X[0, k]))

    arrive(rim_copies(3))
    arrive(layer_copies(3))
    around = received_sum(3, [s[p] * T[p] for p in range(2)])
    vert = [HALO[3, 0] + v[1] * T[1], v[0] * T[0] + HALO[3, 1]]
    for p in range(2):
        t = T[p]
        Q[p] = src[p] - ((DP[p] + v[p] * VS[p]) * t - s[p] * around[p] - v[p] * vert[p])
    ZSEND[1] = tile_row(Q[0] + Q[1])
    Z[1, r * 4 + l] = ZSEND[1]
    group_second = group_copies(2, 1, Z.at[1], ZSEND.at[1])
    for copy in group_second:
        copy.start()

    lower.pass_x(2, 6, 3, 5, 4)
    panel.pass_y(2, 6)
    copy_sibling(1).start()
    copy_sibling(3).start()
    for copy in group_second:
        copy.wait_recv()
    plane_second = gather_plane(2, Z.at[1], XM.at[1], X.at[1])
    lower.end()
    copy_sibling(2).start()
    panel.send_x(0, 1, 7, 2, 6)
    panel.pass_y(3, 5, 4)
    panel.send_x(3, 5, 4)
    for j in range(NX):
        copy_sibling(j).wait_recv()

    def times(block, f):
        wide = jnp.broadcast_to(f, (8, PANEL))

        def body(i, carry):
            px, py = i // NY, lax.rem(i, NY)
            for h in range(2):
                prod = block(px, py, h) * wide
                part = prod[:, :128] + prod[:, 128:256] + prod[:, 256:384] + prod[:, 384:]
                PART[pl.ds(pl.multiple_of(i * SHARE + h * HALF, HALF), HALF)] = part
            return carry

        lax.fori_loop(0, NCOL, body, 0, unroll=8)
        return jnp.concatenate(
            [jnp.sum(PART[128 * j : 128 * (j + 1)].T, axis=0, keepdims=True) for j in range(4)], axis=1
        )

    def minus_transposed(k, f):
        for j in range(4):
            PART[128 * j : 128 * (j + 1)] = column(f[:, 128 * j : 128 * (j + 1)])

        def body(i, acc):
            px, py = i // NY, lax.rem(i, NY)
            for h in range(2):
                w = PART[pl.ds(pl.multiple_of(i * SHARE + h * HALF, HALF), HALF)]
                acc = acc + G[h, px, py, k] * jnp.concatenate([w] * 4, axis=1)
            return acc

        acc = lax.fori_loop(0, NCOL, body, jnp.zeros((8, PANEL), F32), unroll=8)
        return jnp.sum(acc, axis=0, keepdims=True)

    def forward_of(rhs):
        forward = [rhs[0]]
        for k in range(1, NPANEL):
            forward.append(rhs[k] - times(lambda px, py, h: G[h, px, py, k - 1], forward[-1]))
        return forward

    def solve_first(it, rhs):
        forward = forward_of(rhs)
        rows = []
        for k in range(NPANEL):
            prod = piv[k] * forward[k]
            rows.append(prod[:, :128] + prod[:, 128:256] + prod[:, 256:384] + prod[:, 384:])
        rows.append(jnp.zeros((128 - NPANEL * SHARE, 128), F32))
        SBM[it] = jnp.sum(jnp.concatenate(rows, axis=0).T, axis=0, keepdims=True)
        SB[it, c] = SBM[it]
        copies = plane_copies(it, SBM.at[it], SB.at[it], bs, br)
        for copy in copies:
            copy.start()
        return copies

    def solve_second(it, copies):
        for copy in copies:
            copy.wait_recv()
        got = stacked(jnp.concatenate([SB[it, k] for k in range(NCOL)], axis=0))
        owner = iota((NCOL, PANEL), 1) // SHARE == iota((NCOL, PANEL), 0)
        scaled = []
        for k in range(NPANEL):
            spread = jnp.where(
                iota((128, PANEL), 0) == k * SHARE + lax.rem(iota((128, PANEL), 1), SHARE), 1.0, 0.0
            ).astype(BF16)
            value = added(dot(got, spread))
            scaled.append(jnp.sum(jnp.where(owner, value, 0.0), axis=0, keepdims=True))
        return backward_of(scaled)

    def backward_of(scaled):
        ports = [None] * NPANEL
        ports[NPANEL - 1] = scaled[NPANEL - 1]
        for k in range(NPANEL - 2, -1, -1):
            ports[k] = scaled[k] - minus_transposed(k, ports[k + 1])
        return ports

    def lifted_rows(ports, wanted):
        total = jnp.zeros((24, 128), F32)
        for k in range(NPANEL):
            parts = pieces(ports[k] * prolong_scale)
            masks = [ROWM[k : k + 1] == w for w in wanted]
            masks += [masks[0]] * (8 - len(masks))
            rows = [jnp.where(m, part, 0.0) for part in parts for m in masks]
            total = total + dot_t(jnp.concatenate(rows, axis=0).astype(BF16), LANES[k])
        return added(total)

    lane_row = iota((1, 128), 1)

    def spread_rows(rows):
        return added(dot_t(stacked(rows), E4[...]))

    def field_of(own):
        return jnp.concatenate([jnp.where(lane_row // 32 == min(a, 3), own, 0.0) for a in range(4)], axis=0)

    first = solve_first(0, rhs)
    panel.pass_x(0, 1, 7)
    ports1 = solve_second(0, first)

    own_row = c * 4 + r
    none = jnp.int32(-1)
    wanted = [
        own_row,
        jnp.where(r > 0, own_row - 1, none),
        jnp.where(r < 3, own_row + 1, none),
        jnp.where(c > 0, own_row - 4, none),
        jnp.where(c < NCOL - 1, own_row + 4, none),
    ]
    near = lifted_rows(ports1, wanted)
    level = jnp.concatenate(
        [
            field_of(near[0:1]),
            jnp.where(lane_row // 32 == 3, near[1:2], 0.0),
            jnp.where(lane_row // 32 == 0, near[2:3], 0.0),
            jnp.zeros((2, 128), F32),
        ],
        axis=0,
    )
    level = spread_rows(level)
    lift = jnp.concatenate(
        [jnp.broadcast_to(level[a : a + 1], (TILE, COLS)) for a in range(4)], axis=0
    )
    LIFT[...] = lift
    at_row = lax.rem(iota((128, 128), 1), ROWS) // TILE * 32
    pick_w = jnp.where(iota((128, 128), 0) == at_row + 31, 1.0, 0.0).astype(BF16)
    pick_e = jnp.where(iota((128, 128), 0) == at_row, 1.0, 0.0).astype(BF16)
    side_w = added(dot(stacked(near), pick_w))[3:4]
    side_e = added(dot(stacked(near), pick_e))[4:5]
    lifted_around = plane_sum(
        [s[p] * lift for p in range(2)],
        RIM[0, 0] * level[4:5],
        RIM[0, 1] * level[5:6],
        SIDE[0, 0] * side_w,
        SIDE[0, 1] * side_e,
    )
    for p in range(2):
        t3 = T[p]
        resid = Q[p] - (DP[p] * lift - s[p] * lifted_around[p])
        t = INV[p] * resid
        drop_out[p] = lift + t3
        Q[p], T[p], CH[p] = t, t, t
    send_layers(4, [v[p] * T[p] for p in range(2)])
    send_rims(4, [s[p] * T[p] for p in range(2)])
    panel.pass_x(2, 6, 3, 5, 4)

    lifted_map = jnp.zeros((384, 128), F32)
    for k in range(NPANEL):
        mask = row_mask(k)
        parts = [jnp.where(mask, part, 0.0).astype(BF16) for part in pieces(ports1[k] * prolong_scale)]
        lifted_map = lifted_map + dot_t(jnp.concatenate(parts, axis=0), LANES[k])
    lifted_map = added(lifted_map)
    for copy in plane_coef:
        copy.wait_recv()
    pads_map = tile_map(lambda k: CX[k, 0])
    edge_e = tile_map(lambda k: CX[k, 1])
    edge_s = tile_map(lambda k: CX[k, 2])
    lanes = iota((128, 128), 1)

    def tile_east(a):
        ahead = pltpu.roll(a, 124, 0)
        return jnp.where(lax.rem(lanes, 32) == 31, pltpu.roll(ahead, 31, 1), pltpu.roll(a, 127, 1))

    def tile_west(a):
        behind = pltpu.roll(a, 4, 0)
        return jnp.where(lax.rem(lanes, 32) == 0, pltpu.roll(behind, 97, 1), pltpu.roll(a, 1, 1))

    def tile_south(a):
        below = pltpu.roll(a, 127, 0)
        return jnp.where(lanes // 32 == 3, pltpu.roll(below, 96, 1), pltpu.roll(a, 96, 1))

    def tile_north(a):
        above = pltpu.roll(a, 1, 0)
        return jnp.where(lanes // 32 == 0, pltpu.roll(above, 32, 1), pltpu.roll(a, 32, 1))

    flow_e = edge_e * (lifted_map - tile_east(lifted_map))
    flow_s = edge_s * (lifted_map - tile_south(lifted_map))
    coarse = pads_map * lifted_map + flow_e - tile_west(flow_e) + flow_s - tile_north(flow_s)

    for copy in plane_second:
        copy.wait_recv()
    rhs = select_ports(tile_map(lambda k: X[1, k]) - coarse)
    forward = forward_of(rhs)
    for k in range(NPANEL):
        FW[k : k + 1] = forward[k]
    panel.end()
    SL[l] = times(
        lambda px, py, h: GP[px, py, HALF * h : HALF * (h + 1)], FW[pl.ds(l, 1)]
    )
    second = [
        remote(SL.at[l], SL.at[l], ls.at[d - 1], lr.at[d - 1], (lax.rem(l + d, 4), r, c)) for d in range(1, 4)
    ]
    for copy in second:
        copy.start()

    rho = sweep(4, 1.0 / sigma, s, v)
    send_layers(5, [v[p] * T[p] for p in range(2)])
    send_rims(5, [s[p] * T[p] for p in range(2)])

    for copy in second:
        copy.wait_recv()
    ports2 = backward_of([SL[k] for k in range(NPANEL)])
    for k in range(NPANEL):
        ports_out[k : k + 1] = ports2[k]
    near = lifted_rows(ports2, [own_row])
    level = spread_rows(jnp.concatenate([field_of(near[0:1])] * 2, axis=0))
    sweep(5, rho, s, v)
    for p in range(2):
        for a in range(4):
            rows = slice(TILE * a, TILE * (a + 1))
            drop_out[p, rows] = drop_out[p, rows] + T[p, rows] + level[a : a + 1]

    for rd in range(6):
        left(layer_copies(rd))
        left(rim_copies(rd))
    lower.sent()
    panel.sent()
    for copy in group_first + group_coef + group_second:
        copy.wait_send()
    for copy in plane_first + plane_coef + plane_second + first + second:
        copy.wait_send()
    for j in range(NX):
        copy_sibling(j).wait_send()


def shards(*args):
    vmem = pl.BlockSpec(memory_space=pltpu.VMEM)
    field = pltpu.VMEM((2, ROWS, COLS), F32)
    dma = pltpu.SemaphoreType.DMA
    return pl.pallas_call(
        kernel,
        out_shape=(
            jax.ShapeDtypeStruct((2, ROWS, COLS), F32),
            jax.ShapeDtypeStruct((NPANEL, PANEL), F32),
        ),
        in_specs=[pl.BlockSpec(memory_space=pl.ANY)] * 8,
        out_specs=(vmem, vmem),
        scratch_shapes=[
            field, field, field,
            pltpu.VMEM((2, ROWS, COLS), jnp.int32),
            pltpu.VMEM((ROWS, COLS), jnp.int32),
            pltpu.VMEM((NPANEL, PANEL), jnp.int32),
            pltpu.VMEM((NPANEL, SHARE, PANEL), F32),
            field, field, field, field, field, field, field, field,
            pltpu.VMEM((6, 2, ROWS, COLS), F32),
            pltpu.VMEM((6, 2, ROWS, COLS), F32),
            pltpu.VMEM((6, 2, 2, COLS), F32),
            pltpu.VMEM((6, 2, 2, COLS), F32),
            pltpu.VMEM((6, 2, 1, 128), F32),
            pltpu.VMEM((6, 2, 1, 128), F32),
            pltpu.VMEM((2, NX, NY, NPANEL - 1, HALF, PANEL), F32),
            pltpu.VMEM((NX, NY, SHARE, PANEL), F32),
            pltpu.VMEM((NPANEL, PANEL), F32),
            pltpu.VMEM((4, 1, PANEL), F32),
            pltpu.VMEM((PANEL, 128), F32),
            pltpu.VMEM((2, 1, 128), F32),
            pltpu.VMEM((2, 16, 1, 128), F32),
            pltpu.VMEM((2, 4, 128), F32),
            pltpu.VMEM((2, NCOL, 4, 128), F32),
            pltpu.VMEM((3, 128), F32),
            pltpu.VMEM((16, 3, 128), F32),
            pltpu.VMEM((3, 4, 128), F32),
            pltpu.VMEM((NCOL, 3, 4, 128), F32),
            pltpu.VMEM((2, 1, 128), F32),
            pltpu.VMEM((2, NCOL, 1, 128), F32),
            pltpu.VMEM((NPANEL, 128, PANEL), BF16),
            pltpu.VMEM((NPANEL, PANEL), jnp.int32),
            pltpu.VMEM((COLS, 128), BF16),
            pltpu.VMEM((8, 128), F32),
            pltpu.VMEM((ROWS, COLS), F32),
            dma((9,)), dma((6, 6)), dma((6, 6)),
            dma((7,)), dma((7,)),
            dma((2, 8)), dma((2, 8)),
            dma((8,)), dma((8,)),
            dma((7,)), dma((7,)),
            dma((2, 8)), dma((2, 8)),
            dma((8,)), dma((8,)),
            dma((3,)), dma((3,)),
            dma((4,)), dma((4,)),
            dma((3, 15)), dma((3, 15)),
            dma((3, 31)), dma((3, 31)),
            dma((2, 31)), dma((2, 31)),
        ],
        compiler_params=pltpu.CompilerParams(
            collective_id=0, has_side_effects=True, vmem_limit_bytes=60 * 1024 * 1024
        ),
        cost_estimate=pl.CostEstimate(flops=100_000_000, bytes_accessed=2_000_000, transcendentals=300_000),
        name="grid",
    )(*args)


def solution(mesh):
    placed = (
        P("layer", "row", "col"),
        P("layer", "row", "col"),
        P("layer", "row", "col"),
        P("layer", "row", "col"),
        P("row", "col"),
        P(),
        P(None, "col", None),
        P(None, "col", None),
    )
    return jax.shard_map(
        shards,
        mesh=mesh,
        in_specs=placed,
        out_specs=(P("layer", "row", "col"), P()),
        check_vma=False,
    )
```

```python
import jax
import jax.numpy as jnp
from jax import lax
from jax.experimental import pallas as pl
from jax.experimental.pallas import tpu as pltpu
from jax.sharding import PartitionSpec as P

F32 = jnp.float32
BF16 = jnp.bfloat16
MESH = pl.DeviceIdType.MESH

TILE = 16
PANEL = 512
NPANEL = 4
NX, NY = 4, 8
NCOL = NX * NY
ROWS, COLS = 64, 512
SHARE = PANEL // NCOL
HALF = SHARE // 2

pad_gain = 8.0
bound_low = 0.1
bound_high = 1.9
restrict_scale = 0.25
prolong_scale = 0.5
theta = (bound_high + bound_low) / 2.0
delta = (bound_high - bound_low) / 2.0
sigma = theta / delta


def iota(shape, axis):
    return lax.broadcasted_iota(jnp.int32, shape, axis)


def pieces(x):
    high = x.astype(BF16).astype(F32)
    rest = x - high
    mid = rest.astype(BF16).astype(F32)
    return high, mid, rest - mid


def stacked(x):
    return jnp.concatenate(pieces(x), axis=0).astype(BF16)


def added(y):
    n = y.shape[0] // 3
    return y[:n] + y[n : 2 * n] + y[2 * n :]


def dot(a, b):
    return lax.dot_general(a, b, (((1,), (0,)), ((), ())), preferred_element_type=F32)


def dot_t(a, b):
    return lax.dot_general(a, b, (((1,), (1,)), ((), ())), preferred_element_type=F32)


def kernel(
    src_in, cond_in, via_in, vmap_in, pad_in, pt_in, piv_in, coup_in,
    drop_out, ports_out,
    src, cond, via, vmap, pad, pt, piv,
    S, V, INV, DP, VS, Q, T, CH, HSEND, HALO, RSEND, RIM, CSEND, SIDE,
    G, GP, FW, SL, PART, ZSEND, Z, XM, X, CSND, CZ, CXM, CX, SBM, SB, LANES, ROWM, E4,
    ins, hs, hr, gys, gyr, gxs, gxr, gfs, gfr,
    pys, pyr, pxs, pxr, pfs, pfr, ls, lr, gbs, gbr, zs, zr, xs, xr, bs, br,
):
    l, r, c = lax.axis_index("layer"), lax.axis_index("row"), lax.axis_index("col")
    core = lax.rem(l, 2)
    x, y = c // NY, lax.rem(c, NY)

    def at_col(px, py):
        return (l, r, px * NY + py)

    group = [(lax.rem(l + d % 4, 4), lax.rem(r + d // 4, 4), c) for d in range(1, 16)]
    plane_peers = [(l, r, lax.rem(c + d, NCOL)) for d in range(1, NCOL)]
    sibling = (l + 1 - 2 * core, r, c)

    barrier = pltpu.get_barrier_semaphore()
    for peer in group + plane_peers:
        pl.semaphore_signal(barrier, inc=1, device_id=peer, device_id_type=MESH)

    def remote(a, b, ssem, rsem, peer):
        return pltpu.make_async_remote_copy(
            src_ref=a, dst_ref=b, send_sem=ssem, recv_sem=rsem, device_id=peer, device_id_type=MESH
        )

    inputs = [
        pltpu.make_async_copy(a, b, ins.at[n])
        for n, (a, b) in enumerate(
            (
                (via_in, via),
                (vmap_in, vmap),
                (cond_in, cond),
                (coup_in.at[:, pl.ds(pl.multiple_of(core * HALF, HALF), HALF), :], G.at[core, x, y]),
                (src_in, src),
                (pt_in, pt),
                (pad_in, pad),
                (piv_in, piv),
                (piv_in.at[l], GP.at[x, y]),
            )
        )
    ]
    for copy in inputs:
        copy.start()

    E4[...] = jnp.where(
        iota((COLS, 128), 0) // TILE == lax.rem(iota((COLS, 128), 1), 32), 1.0, 0.0
    ).astype(BF16)

    def tile_row(plane):
        parts = [plane[TILE * a : TILE * a + 8] + plane[TILE * a + 8 : TILE * a + 16] for a in range(4)]
        sums = added(dot(stacked(jnp.concatenate(parts, axis=0)), E4[...]))
        own = iota((32, 128), 0) // 8 == iota((32, 128), 1) // 32
        return jnp.sum(jnp.where(own, sums, 0.0), axis=0, keepdims=True)

    zero_plane = jnp.zeros((ROWS, COLS), F32)

    @pl.when(l == 0)
    def _():
        for rd in range(6):
            HALO[rd, 0] = zero_plane

    @pl.when(l == 3)
    def _():
        for rd in range(6):
            HALO[rd, 1] = zero_plane

    @pl.when(r == 0)
    def _():
        for rd in range(6):
            RIM[rd, 0] = jnp.zeros((2, COLS), F32)

    @pl.when(r == 3)
    def _():
        for rd in range(6):
            RIM[rd, 1] = jnp.zeros((2, COLS), F32)

    @pl.when(c == 0)
    def _():
        for rd in range(6):
            SIDE[rd, 0] = jnp.zeros((1, 128), F32)

    @pl.when(c == NCOL - 1)
    def _():
        for rd in range(6):
            SIDE[rd, 1] = jnp.zeros((1, 128), F32)

    def layer_copies(rd):
        up = remote(HSEND.at[rd, 1], HALO.at[rd, 0], hs.at[rd, 0], hr.at[rd, 0], (lax.rem(l + 1, 4), r, c))
        down = remote(HSEND.at[rd, 0], HALO.at[rd, 1], hs.at[rd, 1], hr.at[rd, 1], (lax.rem(l + 3, 4), r, c))
        return ((l < 3, up, l > 0), (l > 0, down, l < 3))

    def rim_copies(rd):
        south = remote(RSEND.at[rd, 1], RIM.at[rd, 0], hs.at[rd, 2], hr.at[rd, 2], (l, lax.rem(r + 1, 4), c))
        north = remote(RSEND.at[rd, 0], RIM.at[rd, 1], hs.at[rd, 3], hr.at[rd, 3], (l, lax.rem(r + 3, 4), c))
        east = remote(CSEND.at[rd, 1], SIDE.at[rd, 0], hs.at[rd, 4], hr.at[rd, 4], (l, r, lax.rem(c + 1, NCOL)))
        west = remote(
            CSEND.at[rd, 0], SIDE.at[rd, 1], hs.at[rd, 5], hr.at[rd, 5], (l, r, lax.rem(c + NCOL - 1, NCOL))
        )
        return (
            (r < 3, south, r > 0),
            (r > 0, north, r < 3),
            (c < NCOL - 1, east, c > 0),
            (c > 0, west, c < NCOL - 1),
        )

    def start(copies):
        for sends, copy, _ in copies:
            @pl.when(sends)
            def _():
                copy.start()

    def arrive(copies):
        for _, copy, receives in copies:
            @pl.when(receives)
            def _():
                copy.wait_recv()

    def left(copies):
        for sends, copy, _ in copies:
            @pl.when(sends)
            def _():
                copy.wait_send()

    def send_layers(rd, h):
        for p in range(2):
            HSEND[rd, p] = h[p]
        start(layer_copies(rd))

    def send_rims(rd, g):
        for p in range(2):
            RSEND[rd, 0, p : p + 1] = g[p][:1]
            RSEND[rd, 1, p : p + 1] = g[p][ROWS - 1 :]
        copies = rim_copies(rd)
        start(copies[:2])
        first = jnp.concatenate([g[0][:, :128], g[1][:, :128]], axis=0)
        last = jnp.concatenate([g[0][:, COLS - 128 :], g[1][:, COLS - 128 :]], axis=0)
        CSEND[rd, 0] = first.T[:1]
        CSEND[rd, 1] = last.T[127:]
        start(copies[2:])

    def column(rim):
        return jnp.broadcast_to(rim, (128, 128)).T

    row_at = iota((ROWS, COLS), 0)
    col_at = iota((ROWS, 128), 1)

    def from_east(g, side):
        moved = pltpu.roll(g, COLS - 1, 1)
        edge = jnp.where(col_at == 127, side, moved[:, COLS - 128 :])
        return jnp.concatenate([moved[:, : COLS - 128], edge], axis=1)

    def from_west(g, side):
        moved = pltpu.roll(g, 1, 1)
        edge = jnp.where(col_at == 0, side, moved[:, :128])
        return jnp.concatenate([edge, moved[:, 128:]], axis=1)

    def from_south(g, rim):
        return jnp.where(row_at == ROWS - 1, rim, pltpu.roll(g, ROWS - 1, 0))

    def from_north(g, rim):
        return jnp.where(row_at == 0, rim, pltpu.roll(g, 1, 0))

    def plane_sum(g, north, south, west, east):
        west, east = column(west), column(east)
        out = []
        for p in range(2):
            rows = slice(ROWS * p, ROWS * (p + 1))
            out.append(
                from_north(g[p], north[p : p + 1])
                + from_south(g[p], south[p : p + 1])
                + from_west(g[p], west[rows])
                + from_east(g[p], east[rows])
            )
        return out

    def received_sum(rd, g):
        return plane_sum(g, RIM[rd, 0], RIM[rd, 1], SIDE[rd, 0], SIDE[rd, 1])

    def group_copies(it, rows, buf, send):
        slot = r * 4 + l
        return [
            remote(send, buf.at[slot], zs.at[it, d], zr.at[it, d], peer) for d, peer in enumerate(group)
        ]

    def plane_copies(it, send, buf, ss, rs):
        return [remote(send, buf.at[c], ss.at[it, d], rs.at[it, d], peer) for d, peer in enumerate(plane_peers)]

    for copy in inputs[:3]:
        copy.wait()
    for p in range(2):
        S[p] = jnp.sqrt(cond[p])
        V[p] = jnp.sqrt(via[p]) * vmap[p].astype(F32)
    for copy in inputs[3:5]:
        copy.wait()

    pl.semaphore_wait(barrier, 15 + 31)

    send_layers(0, [V[0], V[1]])
    send_rims(0, [S[0], S[1]])

    turn = 1 - 2 * core

    class Ring:
        def __init__(self, slot, ys, yr, xs, xr, fs, fr):
            self.slot, self.xs, self.xr, self.fs, self.fr = slot, xs, xr, fs, fr
            self.along_y = {}
            for d, began, step in (
                (1, 0, 1), (7, 0, NY - 1), (2, 0, 2), (6, 0, NY - 2),
                (3, 1, 2), (5, NY - 1, NY - 2), (4, 2 * turn + NY, 2 * turn + NY),
            ):
                piece = slot(x, lax.rem(y + 2 * NY - began, NY))
                self.along_y[d] = remote(
                    piece, piece, ys.at[d - 1], yr.at[d - 1], at_col(x, lax.rem(y + step, NY))
                )

        def along_x(self, d):
            piece = self.slot(x, lax.rem(y + NY - d, NY))
            return [
                remote(piece, piece, self.xs.at[s, d], self.xr.at[s, d], at_col(lax.rem(x + step, NX), y))
                for s, step in enumerate((1, 3))
            ]

        def onward(self, d):
            piece = self.slot(lax.rem(x - turn + NX, NX), lax.rem(y + NY - d, NY))
            return remote(piece, piece, self.fs.at[d], self.fr.at[d], at_col(lax.rem(x + turn + NX, NX), y))

        def begin(self):
            for d in (1, 7, 2, 6):
                self.along_y[d].start()

        def pass_y(self, *ds):
            for d in ds:
                self.along_y[d].wait_recv()
            for d in ds:
                if d in (1, 7):
                    self.along_y[{1: 3, 7: 5}[d]].start()
            if 2 in ds:
                self.along_y[4].start()

        def send_x(self, *ds):
            for d in ds:
                for copy in self.along_x(d):
                    copy.start()

        def pass_x(self, *ds):
            for d in ds:
                for copy in self.along_x(d):
                    copy.wait_recv()
                self.onward(d).start()

        def end(self):
            for d in range(NY):
                self.onward(d).wait_recv()

        def sent(self):
            for d in range(1, NY):
                self.along_y[d].wait_send()
            for d in range(NY):
                for copy in self.along_x(d):
                    copy.wait_send()
                self.onward(d).wait_send()

    lower = Ring(lambda px, py: G.at[core, px, py], gys, gyr, gxs, gxr, gfs, gfr)
    panel = Ring(lambda px, py: GP.at[px, py], pys, pyr, pxs, pxr, pfs, pfr)

    def copy_sibling(j):
        block = G.at[core, lax.rem(x + j, NX)]
        return remote(block, block, gbs.at[j], gbr.at[j], sibling)

    lower.begin()
    lower.send_x(0)
    ZSEND[0] = tile_row(src[0] + src[1])
    group_first = group_copies(0, 1, Z.at[0], ZSEND.at[0])
    for copy in group_first:
        copy.start()

    for copy in inputs[5:]:
        copy.wait()
    for k in range(NPANEL):
        tile = pt[k : k + 1, :]
        arow, acol = tile // 1024, lax.rem(tile, 1024)
        lane = lax.rem(arow, 4) * 32 + lax.rem(acol, 32)
        LANES[k] = jnp.where(iota((128, PANEL), 0) == lane, 1.0, 0.0).astype(BF16)
        ROWM[k : k + 1] = (acol // 32) * 4 + arow // 4

    arrive(layer_copies(0))
    arrive(rim_copies(0))
    s = [S[0], S[1]]
    v = [V[0], V[1]]
    around = received_sum(0, s)
    top = (l == 3).astype(F32)
    pads = pad_gain * pad[...].astype(F32) * top
    vsum = [HALO[0, 0] + v[1], v[0] + HALO[0, 1]]
    for p in range(2):
        dp = s[p] * around[p]
        if p == 1:
            dp = dp + pads
        inv = 1.0 / (dp + v[p] * vsum[p])
        t = inv * src[p]
        DP[p], INV[p], VS[p], Q[p], T[p], CH[p] = dp, inv, vsum[p], t, t, t
    send_layers(1, [v[p] * T[p] for p in range(2)])
    send_rims(1, [s[p] * T[p] for p in range(2)])

    lower.pass_y(1, 7)
    lower.send_x(1, 7)
    lower.pass_x(0)

    def gather_plane(it, buf, msg, bufx):
        for q in range(4):
            total = buf[4 * q]
            for k in range(1, 4):
                total = total + buf[4 * q + k]
            msg[q : q + 1] = total
        bufx[c] = msg[...]
        out = plane_copies(it, msg, bufx, xs, xr)
        for copy in out:
            copy.start()
        return out

    Z[0, r * 4 + l] = ZSEND[0]
    for copy in group_first:
        copy.wait_recv()
    plane_first = gather_plane(0, Z.at[0], XM.at[0], X.at[0])

    lower.pass_y(2, 6)
    lower.send_x(2, 6)

    def sweep(rd, rho, s, v):
        rho_new = 1.0 / (2.0 * sigma - rho)
        t = [T[0], T[1]]
        arrive(rim_copies(rd))
        around = received_sum(rd, [s[p] * t[p] for p in range(2)])
        arrive(layer_copies(rd))
        vert = [HALO[rd, 0] + v[1] * t[1], v[0] * t[0] + HALO[rd, 1]]
        for p in range(2):
            remain = Q[p] - t[p] + INV[p] * (s[p] * around[p] + v[p] * vert[p])
            ch = (rho_new * rho) * CH[p] + (2.0 * rho_new / delta) * remain
            CH[p] = ch
            T[p] = t[p] + ch
        return rho_new

    rho = sweep(1, 1.0 / sigma, s, v)
    send_layers(2, [v[p] * T[p] for p in range(2)])
    send_rims(2, [s[p] * T[p] for p in range(2)])

    lower.pass_y(3, 5, 4)
    lower.send_x(3, 5, 4)
    lower.pass_x(1, 7)
    copy_sibling(0).start()

    sweep(2, rho, s, v)
    send_layers(3, [v[p] * T[p] for p in range(2)])
    send_rims(3, [s[p] * T[p] for p in range(2)])

    lower.pass_x(2, 6)
    panel.begin()

    west_col, east_col = SIDE[0, 0], SIDE[0, 1]
    east_side = column(east_col)
    edge_e = jnp.zeros((ROWS, COLS), F32)
    edge_s = jnp.zeros((ROWS, COLS), F32)
    for p in range(2):
        edge_e = edge_e + s[p] * from_east(s[p], east_side[ROWS * p : ROWS * (p + 1)])
        edge_s = edge_s + s[p] * from_south(s[p], RIM[0, 1, p : p + 1])
    edge_e = jnp.where(lax.rem(iota((ROWS, COLS), 1), TILE) == TILE - 1, edge_e, 0.0)
    edge_s = jnp.where(lax.rem(iota((ROWS, COLS), 0), TILE) == TILE - 1, edge_s, 0.0)
    for k, field in enumerate((pads, edge_e, edge_s)):
        CSND[k : k + 1] = tile_row(field)
    CZ[r * 4 + l] = CSND[...]
    group_coef = group_copies(1, 3, CZ, CSND)
    for copy in group_coef:
        copy.start()

    def tile_map(load):
        return jnp.concatenate([load(k) for k in range(NCOL)], axis=0)

    def row_mask(k):
        return iota((128, PANEL), 0) == ROWM[k : k + 1]

    def select_ports(tiles):
        parts = stacked(tiles)
        out = []
        for k in range(NPANEL):
            picked = added(dot(parts, LANES[k]))
            out.append(
                jnp.sum(jnp.where(row_mask(k), picked, 0.0), axis=0, keepdims=True) * (restrict_scale / TILE)
            )
        return out

    for copy in plane_first:
        copy.wait_recv()
    rhs = select_ports(tile_map(lambda k: X[0, k]))

    lower.pass_x(3, 5, 4)
    copy_sibling(1).start()
    copy_sibling(3).start()

    arrive(rim_copies(3))
    around = received_sum(3, [s[p] * T[p] for p in range(2)])
    flat = [src[p] - (DP[p] * T[p] - s[p] * around[p]) for p in range(2)]
    ZSEND[1] = tile_row(flat[0] + flat[1])
    Z[1, r * 4 + l] = ZSEND[1]
    group_second = group_copies(2, 1, Z.at[1], ZSEND.at[1])
    for copy in group_second:
        copy.start()

    arrive(layer_copies(3))
    vert = [HALO[3, 0] + v[1] * T[1], v[0] * T[0] + HALO[3, 1]]
    for p in range(2):
        t = T[p]
        Q[p] = flat[p] - v[p] * (VS[p] * t - vert[p])
    lower.end()
    copy_sibling(2).start()
    panel.pass_y(1, 7, 2, 6)
    for copy in group_coef:
        copy.wait_recv()
    for q in range(4):
        total = CZ[4 * q]
        for k in range(1, 4):
            total = total + CZ[4 * q + k]
        for k in range(3):
            CXM[k, q : q + 1] = total[k : k + 1]
    CX[c] = CXM[...]
    plane_coef = plane_copies(1, CXM, CX, xs, xr)
    for copy in plane_coef:
        copy.start()

    for j in range(NX):
        copy_sibling(j).wait_recv()

    def times(block, f):
        wide = jnp.broadcast_to(f, (8, PANEL))

        def body(i, carry):
            px, py = i // NY, lax.rem(i, NY)
            for h in range(2):
                prod = block(px, py, h) * wide
                part = prod[:, :128] + prod[:, 128:256] + prod[:, 256:384] + prod[:, 384:]
                PART[pl.ds(pl.multiple_of(i * SHARE + h * HALF, HALF), HALF)] = part
            return carry

        lax.fori_loop(0, NCOL, body, 0, unroll=8)
        return jnp.concatenate(
            [jnp.sum(PART[128 * j : 128 * (j + 1)].T, axis=0, keepdims=True) for j in range(4)], axis=1
        )

    def minus_transposed(k, f):
        for j in range(4):
            PART[128 * j : 128 * (j + 1)] = column(f[:, 128 * j : 128 * (j + 1)])

        def body(i, acc):
            px, py = i // NY, lax.rem(i, NY)
            for h in range(2):
                w = PART[pl.ds(pl.multiple_of(i * SHARE + h * HALF, HALF), HALF)]
                acc = acc + G[h, px, py, k] * jnp.concatenate([w] * 4, axis=1)
            return acc

        acc = lax.fori_loop(0, NCOL, body, jnp.zeros((8, PANEL), F32), unroll=8)
        return jnp.sum(acc, axis=0, keepdims=True)

    def forward_of(rhs):
        forward = [rhs[0]]
        for k in range(1, NPANEL):
            forward.append(rhs[k] - times(lambda px, py, h: G[h, px, py, k - 1], forward[-1]))
        return forward

    def solve_first(it, rhs):
        forward = forward_of(rhs)
        rows = []
        for k in range(NPANEL):
            prod = piv[k] * forward[k]
            rows.append(prod[:, :128] + prod[:, 128:256] + prod[:, 256:384] + prod[:, 384:])
        rows.append(jnp.zeros((128 - NPANEL * SHARE, 128), F32))
        SBM[it] = jnp.sum(jnp.concatenate(rows, axis=0).T, axis=0, keepdims=True)
        SB[it, c] = SBM[it]
        copies = plane_copies(it, SBM.at[it], SB.at[it], bs, br)
        for copy in copies:
            copy.start()
        return copies

    def solve_second(it, copies):
        for copy in copies:
            copy.wait_recv()
        got = stacked(jnp.concatenate([SB[it, k] for k in range(NCOL)], axis=0))
        owner = iota((NCOL, PANEL), 1) // SHARE == iota((NCOL, PANEL), 0)
        scaled = []
        for k in range(NPANEL):
            spread = jnp.where(
                iota((128, PANEL), 0) == k * SHARE + lax.rem(iota((128, PANEL), 1), SHARE), 1.0, 0.0
            ).astype(BF16)
            value = added(dot(got, spread))
            scaled.append(jnp.sum(jnp.where(owner, value, 0.0), axis=0, keepdims=True))
        return backward_of(scaled)

    def backward_of(scaled):
        ports = [None] * NPANEL
        ports[NPANEL - 1] = scaled[NPANEL - 1]
        for k in range(NPANEL - 2, -1, -1):
            ports[k] = scaled[k] - minus_transposed(k, ports[k + 1])
        return ports

    def lifted_rows(ports, wanted):
        total = jnp.zeros((24, 128), F32)
        for k in range(NPANEL):
            parts = pieces(ports[k] * prolong_scale)
            masks = [ROWM[k : k + 1] == w for w in wanted]
            masks += [masks[0]] * (8 - len(masks))
            rows = [jnp.where(m, part, 0.0) for part in parts for m in masks]
            total = total + dot_t(jnp.concatenate(rows, axis=0).astype(BF16), LANES[k])
        return added(total)

    lane_row = iota((1, 128), 1)

    def spread_rows(rows):
        return added(dot_t(stacked(rows), E4[...]))

    def field_of(own):
        return jnp.concatenate([jnp.where(lane_row // 32 == min(a, 3), own, 0.0) for a in range(4)], axis=0)

    first = solve_first(0, rhs)
    for copy in group_second:
        copy.wait_recv()
    plane_second = gather_plane(2, Z.at[1], XM.at[1], X.at[1])
    panel.pass_y(3, 5, 4)
    panel.send_x(0, 1, 7, 2, 6, 3, 5, 4)
    ports1 = solve_second(0, first)

    own_row = c * 4 + r
    none = jnp.int32(-1)
    wanted = [
        own_row,
        jnp.where(r > 0, own_row - 1, none),
        jnp.where(r < 3, own_row + 1, none),
        jnp.where(c > 0, own_row - 4, none),
        jnp.where(c < NCOL - 1, own_row + 4, none),
    ]
    near = lifted_rows(ports1, wanted)
    level = jnp.concatenate(
        [
            field_of(near[0:1]),
            jnp.where(lane_row // 32 == 3, near[1:2], 0.0),
            jnp.where(lane_row // 32 == 0, near[2:3], 0.0),
            jnp.zeros((2, 128), F32),
        ],
        axis=0,
    )
    level = spread_rows(level)
    lift = jnp.concatenate(
        [jnp.broadcast_to(level[a : a + 1], (TILE, COLS)) for a in range(4)], axis=0
    )
    at_row = lax.rem(iota((128, 128), 1), ROWS) // TILE * 32
    pick_w = jnp.where(iota((128, 128), 0) == at_row + 31, 1.0, 0.0).astype(BF16)
    pick_e = jnp.where(iota((128, 128), 0) == at_row, 1.0, 0.0).astype(BF16)
    side_w = added(dot(stacked(near), pick_w))[3:4]
    side_e = added(dot(stacked(near), pick_e))[4:5]
    lifted_around = plane_sum(
        [s[p] * lift for p in range(2)],
        RIM[0, 0] * level[4:5],
        RIM[0, 1] * level[5:6],
        SIDE[0, 0] * side_w,
        SIDE[0, 1] * side_e,
    )
    for p in range(2):
        t3 = T[p]
        resid = Q[p] - (DP[p] * lift - s[p] * lifted_around[p])
        t = INV[p] * resid
        drop_out[p] = lift + t3
        Q[p], T[p], CH[p] = t, t, t
    send_layers(4, [v[p] * T[p] for p in range(2)])
    send_rims(4, [s[p] * T[p] for p in range(2)])
    panel.pass_x(0, 1, 7, 2, 6, 3, 5, 4)

    lifted_map = jnp.zeros((384, 128), F32)
    for k in range(NPANEL):
        mask = row_mask(k)
        parts = [jnp.where(mask, part, 0.0).astype(BF16) for part in pieces(ports1[k] * prolong_scale)]
        lifted_map = lifted_map + dot_t(jnp.concatenate(parts, axis=0), LANES[k])
    lifted_map = added(lifted_map)
    for copy in plane_coef:
        copy.wait_recv()
    pads_map = tile_map(lambda k: CX[k, 0])
    edge_e = tile_map(lambda k: CX[k, 1])
    edge_s = tile_map(lambda k: CX[k, 2])
    lanes = iota((128, 128), 1)

    def tile_east(a):
        ahead = pltpu.roll(a, 124, 0)
        return jnp.where(lax.rem(lanes, 32) == 31, pltpu.roll(ahead, 31, 1), pltpu.roll(a, 127, 1))

    def tile_west(a):
        behind = pltpu.roll(a, 4, 0)
        return jnp.where(lax.rem(lanes, 32) == 0, pltpu.roll(behind, 97, 1), pltpu.roll(a, 1, 1))

    def tile_south(a):
        below = pltpu.roll(a, 127, 0)
        return jnp.where(lanes // 32 == 3, pltpu.roll(below, 96, 1), pltpu.roll(a, 96, 1))

    def tile_north(a):
        above = pltpu.roll(a, 1, 0)
        return jnp.where(lanes // 32 == 0, pltpu.roll(above, 32, 1), pltpu.roll(a, 32, 1))

    flow_e = edge_e * (lifted_map - tile_east(lifted_map))
    flow_s = edge_s * (lifted_map - tile_south(lifted_map))
    coarse = pads_map * lifted_map + flow_e - tile_west(flow_e) + flow_s - tile_north(flow_s)

    for copy in plane_second:
        copy.wait_recv()
    rhs = select_ports(tile_map(lambda k: X[1, k]) - coarse)
    forward = forward_of(rhs)
    for k in range(NPANEL):
        FW[k : k + 1] = forward[k]
    panel.end()
    SL[l] = times(
        lambda px, py, h: GP[px, py, HALF * h : HALF * (h + 1)], FW[pl.ds(l, 1)]
    )
    second = [
        remote(SL.at[l], SL.at[l], ls.at[d - 1], lr.at[d - 1], (lax.rem(l + d, 4), r, c)) for d in range(1, 4)
    ]
    for copy in second:
        copy.start()

    rho = sweep(4, 1.0 / sigma, s, v)
    send_layers(5, [v[p] * T[p] for p in range(2)])
    send_rims(5, [s[p] * T[p] for p in range(2)])

    for copy in second:
        copy.wait_recv()
    ports2 = backward_of([SL[k] for k in range(NPANEL)])
    for k in range(NPANEL):
        ports_out[k : k + 1] = ports2[k]
    near = lifted_rows(ports2, [own_row])
    level = spread_rows(jnp.concatenate([field_of(near[0:1])] * 2, axis=0))
    sweep(5, rho, s, v)
    for p in range(2):
        for a in range(4):
            rows = slice(TILE * a, TILE * (a + 1))
            drop_out[p, rows] = drop_out[p, rows] + T[p, rows] + level[a : a + 1]

    for rd in range(6):
        left(layer_copies(rd))
        left(rim_copies(rd))
    lower.sent()
    panel.sent()
    for copy in group_first + group_coef + group_second:
        copy.wait_send()
    for copy in plane_first + plane_coef + plane_second + first + second:
        copy.wait_send()
    for j in range(NX):
        copy_sibling(j).wait_send()


def shards(*args):
    vmem = pl.BlockSpec(memory_space=pltpu.VMEM)
    field = pltpu.VMEM((2, ROWS, COLS), F32)
    dma = pltpu.SemaphoreType.DMA
    return pl.pallas_call(
        kernel,
        out_shape=(
            jax.ShapeDtypeStruct((2, ROWS, COLS), F32),
            jax.ShapeDtypeStruct((NPANEL, PANEL), F32),
        ),
        in_specs=[pl.BlockSpec(memory_space=pl.ANY)] * 8,
        out_specs=(vmem, vmem),
        scratch_shapes=[
            field, field, field,
            pltpu.VMEM((2, ROWS, COLS), jnp.int32),
            pltpu.VMEM((ROWS, COLS), jnp.int32),
            pltpu.VMEM((NPANEL, PANEL), jnp.int32),
            pltpu.VMEM((NPANEL, SHARE, PANEL), F32),
            field, field, field, field, field, field, field, field,
            pltpu.VMEM((6, 2, ROWS, COLS), F32),
            pltpu.VMEM((6, 2, ROWS, COLS), F32),
            pltpu.VMEM((6, 2, 2, COLS), F32),
            pltpu.VMEM((6, 2, 2, COLS), F32),
            pltpu.VMEM((6, 2, 1, 128), F32),
            pltpu.VMEM((6, 2, 1, 128), F32),
            pltpu.VMEM((2, NX, NY, NPANEL - 1, HALF, PANEL), F32),
            pltpu.VMEM((NX, NY, SHARE, PANEL), F32),
            pltpu.VMEM((NPANEL, PANEL), F32),
            pltpu.VMEM((4, 1, PANEL), F32),
            pltpu.VMEM((PANEL, 128), F32),
            pltpu.VMEM((2, 1, 128), F32),
            pltpu.VMEM((2, 16, 1, 128), F32),
            pltpu.VMEM((2, 4, 128), F32),
            pltpu.VMEM((2, NCOL, 4, 128), F32),
            pltpu.VMEM((3, 128), F32),
            pltpu.VMEM((16, 3, 128), F32),
            pltpu.VMEM((3, 4, 128), F32),
            pltpu.VMEM((NCOL, 3, 4, 128), F32),
            pltpu.VMEM((2, 1, 128), F32),
            pltpu.VMEM((2, NCOL, 1, 128), F32),
            pltpu.VMEM((NPANEL, 128, PANEL), BF16),
            pltpu.VMEM((NPANEL, PANEL), jnp.int32),
            pltpu.VMEM((COLS, 128), BF16),
            dma((9,)), dma((6, 6)), dma((6, 6)),
            dma((7,)), dma((7,)),
            dma((2, 8)), dma((2, 8)),
            dma((8,)), dma((8,)),
            dma((7,)), dma((7,)),
            dma((2, 8)), dma((2, 8)),
            dma((8,)), dma((8,)),
            dma((3,)), dma((3,)),
            dma((4,)), dma((4,)),
            dma((3, 15)), dma((3, 15)),
            dma((3, 31)), dma((3, 31)),
            dma((2, 31)), dma((2, 31)),
        ],
        compiler_params=pltpu.CompilerParams(
            collective_id=0, has_side_effects=True, vmem_limit_bytes=60 * 1024 * 1024
        ),
        cost_estimate=pl.CostEstimate(flops=100_000_000, bytes_accessed=2_000_000, transcendentals=300_000),
        name="grid",
    )(*args)


def solution(mesh):
    placed = (
        P("layer", "row", "col"),
        P("layer", "row", "col"),
        P("layer", "row", "col"),
        P("layer", "row", "col"),
        P("row", "col"),
        P(),
        P(None, "col", None),
        P(None, "col", None),
    )
    return jax.shard_map(
        shards,
        mesh=mesh,
        in_specs=placed,
        out_specs=(P("layer", "row", "col"), P()),
        check_vma=False,
    )
```

```python
import jax
import jax.numpy as jnp
from jax import lax
from jax.experimental import pallas as pl
from jax.experimental.pallas import tpu as pltpu
from jax.sharding import PartitionSpec as P

F32 = jnp.float32
BF16 = jnp.bfloat16
MESH = pl.DeviceIdType.MESH

TILE = 16
PANEL = 512
NPANEL = 4
NX, NY = 4, 8
NCOL = NX * NY
ROWS, COLS = 64, 512
SHARE = PANEL // NCOL
HALF = SHARE // 2

pad_gain = 8.0
bound_low = 0.1
bound_high = 1.9
restrict_scale = 0.25
prolong_scale = 0.5
theta = (bound_high + bound_low) / 2.0
delta = (bound_high - bound_low) / 2.0
sigma = theta / delta


def iota(shape, axis):
    return lax.broadcasted_iota(jnp.int32, shape, axis)


def pieces(x):
    high = x.astype(BF16).astype(F32)
    rest = x - high
    mid = rest.astype(BF16).astype(F32)
    return high, mid, rest - mid


def stacked(x):
    return jnp.concatenate(pieces(x), axis=0).astype(BF16)


def added(y):
    n = y.shape[0] // 3
    return y[:n] + y[n : 2 * n] + y[2 * n :]


def dot(a, b):
    return lax.dot_general(a, b, (((1,), (0,)), ((), ())), preferred_element_type=F32)


def dot_t(a, b):
    return lax.dot_general(a, b, (((1,), (1,)), ((), ())), preferred_element_type=F32)


def kernel(
    src_in, cond_in, via_in, vmap_in, pad_in, pt_in, piv_in, coup_in,
    drop_out, ports_out,
    src, cond, via, vmap, pad, pt, piv,
    S, V, INV, DP, VS, Q, T, CH, HSEND, HALO, RSEND, RIM, CSEND, SIDE,
    G, GP, FW, SL, PART, ZSEND, Z, XM, X, CSND, CZ, CXM, CX, SBM, SB, LANES, ROWM, E4,
    ins, hs, hr, gys, gyr, gxs, gxr, gfs, gfr,
    pys, pyr, pxs, pxr, pfs, pfr, ls, lr, gbs, gbr, zs, zr, xs, xr, bs, br,
):
    l, r, c = lax.axis_index("layer"), lax.axis_index("row"), lax.axis_index("col")
    core = lax.rem(l, 2)
    x, y = c // NY, lax.rem(c, NY)

    def at_col(px, py):
        return (l, r, px * NY + py)

    def far(d, n, m):
        i, j = d // m, d % m
        return -(min(i, n - i) + min(j, m - j))

    group = [
        (lax.rem(l + d % 4, 4), lax.rem(r + d // 4, 4), c)
        for d in sorted(range(1, 16), key=lambda d: far(d, 4, 4) - min(d // 4, 4 - d // 4))
    ]
    plane_peers = [
        (l, r, lax.rem(c + d, NCOL)) for d in sorted(range(1, NCOL), key=lambda d: far(d, NX, NY))
    ]
    sibling = (l + 1 - 2 * core, r, c)

    barrier = pltpu.get_barrier_semaphore()
    for peer in plane_peers + group:
        pl.semaphore_signal(barrier, inc=1, device_id=peer, device_id_type=MESH)

    def remote(a, b, ssem, rsem, peer):
        return pltpu.make_async_remote_copy(
            src_ref=a, dst_ref=b, send_sem=ssem, recv_sem=rsem, device_id=peer, device_id_type=MESH
        )

    inputs = [
        pltpu.make_async_copy(a, b, ins.at[n])
        for n, (a, b) in enumerate(
            (
                (via_in, via),
                (vmap_in, vmap),
                (cond_in, cond),
                (coup_in.at[:, pl.ds(pl.multiple_of(core * HALF, HALF), HALF), :], G.at[core, x, y]),
                (src_in, src),
                (pt_in, pt),
                (pad_in, pad),
                (piv_in, piv),
                (piv_in.at[l], GP.at[x, y]),
            )
        )
    ]
    for copy in inputs:
        copy.start()

    E4[...] = jnp.where(
        iota((COLS, 128), 0) // TILE == lax.rem(iota((COLS, 128), 1), 32), 1.0, 0.0
    ).astype(BF16)

    def tile_row(plane):
        parts = [plane[TILE * a : TILE * a + 8] + plane[TILE * a + 8 : TILE * a + 16] for a in range(4)]
        sums = added(dot(stacked(jnp.concatenate(parts, axis=0)), E4[...]))
        own = iota((32, 128), 0) // 8 == iota((32, 128), 1) // 32
        return jnp.sum(jnp.where(own, sums, 0.0), axis=0, keepdims=True)

    zero_plane = jnp.zeros((ROWS, COLS), F32)

    @pl.when(l == 0)
    def _():
        for rd in range(6):
            HALO[rd, 0] = zero_plane

    @pl.when(l == 3)
    def _():
        for rd in range(6):
            HALO[rd, 1] = zero_plane

    @pl.when(r == 0)
    def _():
        for rd in range(6):
            RIM[rd, 0] = jnp.zeros((2, COLS), F32)

    @pl.when(r == 3)
    def _():
        for rd in range(6):
            RIM[rd, 1] = jnp.zeros((2, COLS), F32)

    @pl.when(c == 0)
    def _():
        for rd in range(6):
            SIDE[rd, 0] = jnp.zeros((1, 128), F32)

    @pl.when(c == NCOL - 1)
    def _():
        for rd in range(6):
            SIDE[rd, 1] = jnp.zeros((1, 128), F32)

    def layer_copies(rd):
        up = remote(HSEND.at[rd, 1], HALO.at[rd, 0], hs.at[rd, 0], hr.at[rd, 0], (lax.rem(l + 1, 4), r, c))
        down = remote(HSEND.at[rd, 0], HALO.at[rd, 1], hs.at[rd, 1], hr.at[rd, 1], (lax.rem(l + 3, 4), r, c))
        return ((l < 3, up, l > 0), (l > 0, down, l < 3))

    def rim_copies(rd):
        south = remote(RSEND.at[rd, 1], RIM.at[rd, 0], hs.at[rd, 2], hr.at[rd, 2], (l, lax.rem(r + 1, 4), c))
        north = remote(RSEND.at[rd, 0], RIM.at[rd, 1], hs.at[rd, 3], hr.at[rd, 3], (l, lax.rem(r + 3, 4), c))
        east = remote(CSEND.at[rd, 1], SIDE.at[rd, 0], hs.at[rd, 4], hr.at[rd, 4], (l, r, lax.rem(c + 1, NCOL)))
        west = remote(
            CSEND.at[rd, 0], SIDE.at[rd, 1], hs.at[rd, 5], hr.at[rd, 5], (l, r, lax.rem(c + NCOL - 1, NCOL))
        )
        return (
            (r < 3, south, r > 0),
            (r > 0, north, r < 3),
            (c < NCOL - 1, east, c > 0),
            (c > 0, west, c < NCOL - 1),
        )

    def start(copies):
        for sends, copy, _ in copies:
            @pl.when(sends)
            def _():
                copy.start()

    def arrive(copies):
        for _, copy, receives in copies:
            @pl.when(receives)
            def _():
                copy.wait_recv()

    def left(copies):
        for sends, copy, _ in copies:
            @pl.when(sends)
            def _():
                copy.wait_send()

    def send_layers(rd, h):
        for p in range(2):
            HSEND[rd, p] = h[p]
        start(layer_copies(rd))

    def send_rims(rd, g):
        for p in range(2):
            RSEND[rd, 0, p : p + 1] = g[p][:1]
            RSEND[rd, 1, p : p + 1] = g[p][ROWS - 1 :]
        copies = rim_copies(rd)
        start(copies[:2])
        first = jnp.concatenate([g[0][:, :128], g[1][:, :128]], axis=0)
        last = jnp.concatenate([g[0][:, COLS - 128 :], g[1][:, COLS - 128 :]], axis=0)
        CSEND[rd, 0] = first.T[:1]
        CSEND[rd, 1] = last.T[127:]
        start(copies[2:])

    def column(rim):
        return jnp.broadcast_to(rim, (128, 128)).T

    row_at = iota((ROWS, COLS), 0)
    col_at = iota((ROWS, 128), 1)

    def from_east(g, side):
        moved = pltpu.roll(g, COLS - 1, 1)
        edge = jnp.where(col_at == 127, side, moved[:, COLS - 128 :])
        return jnp.concatenate([moved[:, : COLS - 128], edge], axis=1)

    def from_west(g, side):
        moved = pltpu.roll(g, 1, 1)
        edge = jnp.where(col_at == 0, side, moved[:, :128])
        return jnp.concatenate([edge, moved[:, 128:]], axis=1)

    def from_south(g, rim):
        return jnp.where(row_at == ROWS - 1, rim, pltpu.roll(g, ROWS - 1, 0))

    def from_north(g, rim):
        return jnp.where(row_at == 0, rim, pltpu.roll(g, 1, 0))

    def plane_sum(g, north, south, west, east):
        west, east = column(west), column(east)
        out = []
        for p in range(2):
            rows = slice(ROWS * p, ROWS * (p + 1))
            out.append(
                from_north(g[p], north[p : p + 1])
                + from_south(g[p], south[p : p + 1])
                + from_west(g[p], west[rows])
                + from_east(g[p], east[rows])
            )
        return out

    def received_sum(rd, g):
        return plane_sum(g, RIM[rd, 0], RIM[rd, 1], SIDE[rd, 0], SIDE[rd, 1])

    def group_copies(it, rows, buf, send):
        slot = r * 4 + l
        return [
            remote(send, buf.at[slot], zs.at[it, d], zr.at[it, d], peer) for d, peer in enumerate(group)
        ]

    def plane_copies(it, send, buf, ss, rs):
        return [remote(send, buf.at[c], ss.at[it, d], rs.at[it, d], peer) for d, peer in enumerate(plane_peers)]

    for copy in inputs[:3]:
        copy.wait()
    for p in range(2):
        S[p] = jnp.sqrt(cond[p])
        V[p] = jnp.sqrt(via[p]) * vmap[p].astype(F32)
    for copy in inputs[3:5]:
        copy.wait()

    pl.semaphore_wait(barrier, 15 + 31)

    send_layers(0, [V[0], V[1]])
    send_rims(0, [S[0], S[1]])

    turn = 1 - 2 * core

    class Ring:
        def __init__(self, slot, ys, yr, xs, xr, fs, fr):
            self.slot, self.xs, self.xr, self.fs, self.fr = slot, xs, xr, fs, fr
            self.along_y = {}
            for d, began, step in (
                (1, 0, 1), (7, 0, NY - 1), (2, 0, 2), (6, 0, NY - 2),
                (3, 1, 2), (5, NY - 1, NY - 2), (4, 2 * turn + NY, 2 * turn + NY),
            ):
                piece = slot(x, lax.rem(y + 2 * NY - began, NY))
                self.along_y[d] = remote(
                    piece, piece, ys.at[d - 1], yr.at[d - 1], at_col(x, lax.rem(y + step, NY))
                )

        def along_x(self, d):
            piece = self.slot(x, lax.rem(y + NY - d, NY))
            return [
                remote(piece, piece, self.xs.at[s, d], self.xr.at[s, d], at_col(lax.rem(x + step, NX), y))
                for s, step in enumerate((1, 3))
            ]

        def onward(self, d):
            piece = self.slot(lax.rem(x - turn + NX, NX), lax.rem(y + NY - d, NY))
            return remote(piece, piece, self.fs.at[d], self.fr.at[d], at_col(lax.rem(x + turn + NX, NX), y))

        def begin(self):
            for d in (1, 7, 2, 6):
                self.along_y[d].start()

        def pass_y(self, *ds):
            for d in ds:
                self.along_y[d].wait_recv()
            for d in ds:
                if d in (1, 7):
                    self.along_y[{1: 3, 7: 5}[d]].start()
            if 2 in ds:
                self.along_y[4].start()

        def send_x(self, *ds):
            for d in ds:
                for copy in self.along_x(d):
                    copy.start()

        def pass_x(self, *ds):
            for d in ds:
                for copy in self.along_x(d):
                    copy.wait_recv()
                self.onward(d).start()

        def end(self):
            for d in range(NY):
                self.onward(d).wait_recv()

        def sent(self):
            for d in range(1, NY):
                self.along_y[d].wait_send()
            for d in range(NY):
                for copy in self.along_x(d):
                    copy.wait_send()
                self.onward(d).wait_send()

    lower = Ring(lambda px, py: G.at[core, px, py], gys, gyr, gxs, gxr, gfs, gfr)
    panel = Ring(lambda px, py: GP.at[px, py], pys, pyr, pxs, pxr, pfs, pfr)

    def copy_sibling(j):
        block = G.at[core, lax.rem(x + j, NX)]
        return remote(block, block, gbs.at[j], gbr.at[j], sibling)

    lower.begin()
    lower.send_x(0)
    ZSEND[0] = tile_row(src[0] + src[1])
    group_first = group_copies(0, 1, Z.at[0], ZSEND.at[0])
    for copy in group_first:
        copy.start()

    for copy in inputs[5:]:
        copy.wait()
    for k in range(NPANEL):
        tile = pt[k : k + 1, :]
        arow, acol = tile // 1024, lax.rem(tile, 1024)
        lane = lax.rem(arow, 4) * 32 + lax.rem(acol, 32)
        LANES[k] = jnp.where(iota((128, PANEL), 0) == lane, 1.0, 0.0).astype(BF16)
        ROWM[k : k + 1] = (acol // 32) * 4 + arow // 4

    arrive(rim_copies(0))
    lower.pass_y(1, 7)
    lower.send_x(1, 7)
    arrive(layer_copies(0))
    s = [S[0], S[1]]
    v = [V[0], V[1]]
    around = received_sum(0, s)
    top = (l == 3).astype(F32)
    pads = pad_gain * pad[...].astype(F32) * top
    vsum = [HALO[0, 0] + v[1], v[0] + HALO[0, 1]]
    for p in range(2):
        dp = s[p] * around[p]
        if p == 1:
            dp = dp + pads
        inv = 1.0 / (dp + v[p] * vsum[p])
        t = inv * src[p]
        DP[p], INV[p], VS[p], Q[p], T[p], CH[p] = dp, inv, vsum[p], t, t, t
    send_layers(1, [v[p] * T[p] for p in range(2)])
    send_rims(1, [s[p] * T[p] for p in range(2)])

    lower.pass_y(2, 6)
    lower.send_x(2, 6)

    def gather_plane(it, buf, msg, bufx):
        for q in range(4):
            total = buf[4 * q]
            for k in range(1, 4):
                total = total + buf[4 * q + k]
            msg[q : q + 1] = total
        bufx[c] = msg[...]
        out = plane_copies(it, msg, bufx, xs, xr)
        for copy in out:
            copy.start()
        return out

    Z[0, r * 4 + l] = ZSEND[0]
    for copy in group_first:
        copy.wait_recv()
    plane_first = gather_plane(0, Z.at[0], XM.at[0], X.at[0])

    lower.pass_x(0)
    lower.pass_y(3, 5, 4)
    lower.send_x(3, 5, 4)

    def sweep(rd, rho, s, v):
        rho_new = 1.0 / (2.0 * sigma - rho)
        t = [T[0], T[1]]
        arrive(rim_copies(rd))
        around = received_sum(rd, [s[p] * t[p] for p in range(2)])
        arrive(layer_copies(rd))
        vert = [HALO[rd, 0] + v[1] * t[1], v[0] * t[0] + HALO[rd, 1]]
        for p in range(2):
            remain = Q[p] - t[p] + INV[p] * (s[p] * around[p] + v[p] * vert[p])
            ch = (rho_new * rho) * CH[p] + (2.0 * rho_new / delta) * remain
            CH[p] = ch
            T[p] = t[p] + ch
        return rho_new

    rho = sweep(1, 1.0 / sigma, s, v)
    send_layers(2, [v[p] * T[p] for p in range(2)])
    send_rims(2, [s[p] * T[p] for p in range(2)])

    lower.pass_x(1, 7, 2, 6)
    copy_sibling(0).start()

    sweep(2, rho, s, v)
    send_layers(3, [v[p] * T[p] for p in range(2)])
    send_rims(3, [s[p] * T[p] for p in range(2)])

    lower.pass_x(3, 5, 4)
    copy_sibling(1).start()
    copy_sibling(3).start()
    panel.begin()

    west_col, east_col = SIDE[0, 0], SIDE[0, 1]
    east_side = column(east_col)
    edge_e = jnp.zeros((ROWS, COLS), F32)
    edge_s = jnp.zeros((ROWS, COLS), F32)
    for p in range(2):
        edge_e = edge_e + s[p] * from_east(s[p], east_side[ROWS * p : ROWS * (p + 1)])
        edge_s = edge_s + s[p] * from_south(s[p], RIM[0, 1, p : p + 1])
    edge_e = jnp.where(lax.rem(iota((ROWS, COLS), 1), TILE) == TILE - 1, edge_e, 0.0)
    edge_s = jnp.where(lax.rem(iota((ROWS, COLS), 0), TILE) == TILE - 1, edge_s, 0.0)
    for k, field in enumerate((pads, edge_e, edge_s)):
        CSND[k : k + 1] = tile_row(field)
    CZ[r * 4 + l] = CSND[...]
    group_coef = group_copies(1, 3, CZ, CSND)
    for copy in group_coef:
        copy.start()

    def tile_map(load):
        return jnp.concatenate([load(k) for k in range(NCOL)], axis=0)

    def row_mask(k):
        return iota((128, PANEL), 0) == ROWM[k : k + 1]

    def select_ports(tiles):
        parts = stacked(tiles)
        out = []
        for k in range(NPANEL):
            picked = added(dot(parts, LANES[k]))
            out.append(
                jnp.sum(jnp.where(row_mask(k), picked, 0.0), axis=0, keepdims=True) * (restrict_scale / TILE)
            )
        return out

    for copy in plane_first:
        copy.wait_recv()
    rhs = select_ports(tile_map(lambda k: X[0, k]))

    lower.end()
    copy_sibling(2).start()
    panel.pass_y(1, 7, 2, 6)

    arrive(rim_copies(3))
    around = received_sum(3, [s[p] * T[p] for p in range(2)])
    flat = [src[p] - (DP[p] * T[p] - s[p] * around[p]) for p in range(2)]
    ZSEND[1] = tile_row(flat[0] + flat[1])
    Z[1, r * 4 + l] = ZSEND[1]
    group_second = group_copies(2, 1, Z.at[1], ZSEND.at[1])
    for copy in group_second:
        copy.start()

    def times(block, f):
        wide = jnp.broadcast_to(f, (8, PANEL))

        def body(i, carry):
            px, py = i // NY, lax.rem(i, NY)
            for h in range(2):
                prod = block(px, py, h) * wide
                part = prod[:, :128] + prod[:, 128:256] + prod[:, 256:384] + prod[:, 384:]
                PART[pl.ds(pl.multiple_of(i * SHARE + h * HALF, HALF), HALF)] = part
            return carry

        lax.fori_loop(0, NCOL, body, 0, unroll=8)
        return jnp.concatenate(
            [jnp.sum(PART[128 * j : 128 * (j + 1)].T, axis=0, keepdims=True) for j in range(4)], axis=1
        )

    def minus_transposed(k, f):
        for j in range(4):
            PART[128 * j : 128 * (j + 1)] = column(f[:, 128 * j : 128 * (j + 1)])

        def body(i, acc):
            px, py = i // NY, lax.rem(i, NY)
            for h in range(2):
                w = PART[pl.ds(pl.multiple_of(i * SHARE + h * HALF, HALF), HALF)]
                acc = acc + G[h, px, py, k] * jnp.concatenate([w] * 4, axis=1)
            return acc

        acc = lax.fori_loop(0, NCOL, body, jnp.zeros((8, PANEL), F32), unroll=8)
        return jnp.sum(acc, axis=0, keepdims=True)

    def forward_of(rhs):
        forward = [rhs[0]]
        for k in range(1, NPANEL):
            forward.append(rhs[k] - times(lambda px, py, h: G[h, px, py, k - 1], forward[-1]))
        return forward

    def solve_first(it, rhs):
        forward = forward_of(rhs)
        rows = []
        for k in range(NPANEL):
            prod = piv[k] * forward[k]
            rows.append(prod[:, :128] + prod[:, 128:256] + prod[:, 256:384] + prod[:, 384:])
        rows.append(jnp.zeros((128 - NPANEL * SHARE, 128), F32))
        SBM[it] = jnp.sum(jnp.concatenate(rows, axis=0).T, axis=0, keepdims=True)
        SB[it, c] = SBM[it]
        copies = plane_copies(it, SBM.at[it], SB.at[it], bs, br)
        for copy in copies:
            copy.start()
        return copies

    def solve_second(it, copies):
        for copy in copies:
            copy.wait_recv()
        got = stacked(jnp.concatenate([SB[it, k] for k in range(NCOL)], axis=0))
        owner = iota((NCOL, PANEL), 1) // SHARE == iota((NCOL, PANEL), 0)
        scaled = []
        for k in range(NPANEL):
            spread = jnp.where(
                iota((128, PANEL), 0) == k * SHARE + lax.rem(iota((128, PANEL), 1), SHARE), 1.0, 0.0
            ).astype(BF16)
            value = added(dot(got, spread))
            scaled.append(jnp.sum(jnp.where(owner, value, 0.0), axis=0, keepdims=True))
        return backward_of(scaled)

    def backward_of(scaled):
        ports = [None] * NPANEL
        ports[NPANEL - 1] = scaled[NPANEL - 1]
        for k in range(NPANEL - 2, -1, -1):
            ports[k] = scaled[k] - minus_transposed(k, ports[k + 1])
        return ports

    def lifted_rows(ports, wanted):
        total = jnp.zeros((24, 128), F32)
        for k in range(NPANEL):
            parts = pieces(ports[k] * prolong_scale)
            masks = [ROWM[k : k + 1] == w for w in wanted]
            masks += [masks[0]] * (8 - len(masks))
            rows = [jnp.where(m, part, 0.0) for part in parts for m in masks]
            total = total + dot_t(jnp.concatenate(rows, axis=0).astype(BF16), LANES[k])
        return added(total)

    lane_row = iota((1, 128), 1)

    def spread_rows(rows):
        return added(dot_t(stacked(rows), E4[...]))

    def field_of(own):
        return jnp.concatenate([jnp.where(lane_row // 32 == min(a, 3), own, 0.0) for a in range(4)], axis=0)

    for j in range(NX):
        copy_sibling(j).wait_recv()
    first = solve_first(0, rhs)

    arrive(layer_copies(3))
    vert = [HALO[3, 0] + v[1] * T[1], v[0] * T[0] + HALO[3, 1]]
    for p in range(2):
        t = T[p]
        Q[p] = flat[p] - v[p] * (VS[p] * t - vert[p])
    for copy in group_coef:
        copy.wait_recv()
    for q in range(4):
        total = CZ[4 * q]
        for k in range(1, 4):
            total = total + CZ[4 * q + k]
        for k in range(3):
            CXM[k, q : q + 1] = total[k : k + 1]
    CX[c] = CXM[...]
    plane_coef = plane_copies(1, CXM, CX, xs, xr)
    for copy in plane_coef:
        copy.start()


    for copy in group_second:
        copy.wait_recv()
    plane_second = gather_plane(2, Z.at[1], XM.at[1], X.at[1])
    panel.pass_y(3, 5, 4)
    panel.send_x(0, 1, 7, 2, 6, 3, 5, 4)
    ports1 = solve_second(0, first)

    own_row = c * 4 + r
    none = jnp.int32(-1)
    wanted = [
        own_row,
        jnp.where(r > 0, own_row - 1, none),
        jnp.where(r < 3, own_row + 1, none),
        jnp.where(c > 0, own_row - 4, none),
        jnp.where(c < NCOL - 1, own_row + 4, none),
    ]
    near = lifted_rows(ports1, wanted)
    level = jnp.concatenate(
        [
            field_of(near[0:1]),
            jnp.where(lane_row // 32 == 3, near[1:2], 0.0),
            jnp.where(lane_row // 32 == 0, near[2:3], 0.0),
            jnp.zeros((2, 128), F32),
        ],
        axis=0,
    )
    level = spread_rows(level)
    lift = jnp.concatenate(
        [jnp.broadcast_to(level[a : a + 1], (TILE, COLS)) for a in range(4)], axis=0
    )
    at_row = lax.rem(iota((128, 128), 1), ROWS) // TILE * 32
    pick_w = jnp.where(iota((128, 128), 0) == at_row + 31, 1.0, 0.0).astype(BF16)
    pick_e = jnp.where(iota((128, 128), 0) == at_row, 1.0, 0.0).astype(BF16)
    side_w = added(dot(stacked(near), pick_w))[3:4]
    side_e = added(dot(stacked(near), pick_e))[4:5]
    lifted_around = plane_sum(
        [s[p] * lift for p in range(2)],
        RIM[0, 0] * level[4:5],
        RIM[0, 1] * level[5:6],
        SIDE[0, 0] * side_w,
        SIDE[0, 1] * side_e,
    )
    for p in range(2):
        t3 = T[p]
        resid = Q[p] - (DP[p] * lift - s[p] * lifted_around[p])
        t = INV[p] * resid
        drop_out[p] = lift + t3
        Q[p], T[p], CH[p] = t, t, t
    send_layers(4, [v[p] * T[p] for p in range(2)])
    send_rims(4, [s[p] * T[p] for p in range(2)])
    panel.pass_x(0, 1, 7, 2, 6)

    lifted_map = jnp.zeros((384, 128), F32)
    for k in range(NPANEL):
        mask = row_mask(k)
        parts = [jnp.where(mask, part, 0.0).astype(BF16) for part in pieces(ports1[k] * prolong_scale)]
        lifted_map = lifted_map + dot_t(jnp.concatenate(parts, axis=0), LANES[k])
    lifted_map = added(lifted_map)
    for copy in plane_coef:
        copy.wait_recv()
    pads_map = tile_map(lambda k: CX[k, 0])
    edge_e = tile_map(lambda k: CX[k, 1])
    edge_s = tile_map(lambda k: CX[k, 2])
    lanes = iota((128, 128), 1)

    def tile_east(a):
        ahead = pltpu.roll(a, 124, 0)
        return jnp.where(lax.rem(lanes, 32) == 31, pltpu.roll(ahead, 31, 1), pltpu.roll(a, 127, 1))

    def tile_west(a):
        behind = pltpu.roll(a, 4, 0)
        return jnp.where(lax.rem(lanes, 32) == 0, pltpu.roll(behind, 97, 1), pltpu.roll(a, 1, 1))

    def tile_south(a):
        below = pltpu.roll(a, 127, 0)
        return jnp.where(lanes // 32 == 3, pltpu.roll(below, 96, 1), pltpu.roll(a, 96, 1))

    def tile_north(a):
        above = pltpu.roll(a, 1, 0)
        return jnp.where(lanes // 32 == 0, pltpu.roll(above, 32, 1), pltpu.roll(a, 32, 1))

    flow_e = edge_e * (lifted_map - tile_east(lifted_map))
    flow_s = edge_s * (lifted_map - tile_south(lifted_map))
    coarse = pads_map * lifted_map + flow_e - tile_west(flow_e) + flow_s - tile_north(flow_s)

    panel.pass_x(3, 5, 4)
    for copy in plane_second:
        copy.wait_recv()
    rhs = select_ports(tile_map(lambda k: X[1, k]) - coarse)
    rho = sweep(4, 1.0 / sigma, s, v)
    send_layers(5, [v[p] * T[p] for p in range(2)])
    send_rims(5, [s[p] * T[p] for p in range(2)])

    forward = forward_of(rhs)
    for k in range(NPANEL):
        FW[k : k + 1] = forward[k]
    panel.end()
    SL[l] = times(
        lambda px, py, h: GP[px, py, HALF * h : HALF * (h + 1)], FW[pl.ds(l, 1)]
    )
    second = [
        remote(SL.at[l], SL.at[l], ls.at[d - 1], lr.at[d - 1], (lax.rem(l + d, 4), r, c)) for d in range(1, 4)
    ]
    for copy in second:
        copy.start()

    for copy in second:
        copy.wait_recv()
    ports2 = backward_of([SL[k] for k in range(NPANEL)])
    for k in range(NPANEL):
        ports_out[k : k + 1] = ports2[k]
    near = lifted_rows(ports2, [own_row])
    level = spread_rows(jnp.concatenate([field_of(near[0:1])] * 2, axis=0))
    sweep(5, rho, s, v)
    for p in range(2):
        for a in range(4):
            rows = slice(TILE * a, TILE * (a + 1))
            drop_out[p, rows] = drop_out[p, rows] + T[p, rows] + level[a : a + 1]

    for rd in range(6):
        left(layer_copies(rd))
        left(rim_copies(rd))
    lower.sent()
    panel.sent()
    for copy in group_first + group_coef + group_second:
        copy.wait_send()
    for copy in plane_first + plane_coef + plane_second + first + second:
        copy.wait_send()
    for j in range(NX):
        copy_sibling(j).wait_send()


def shards(*args):
    vmem = pl.BlockSpec(memory_space=pltpu.VMEM)
    field = pltpu.VMEM((2, ROWS, COLS), F32)
    dma = pltpu.SemaphoreType.DMA
    return pl.pallas_call(
        kernel,
        out_shape=(
            jax.ShapeDtypeStruct((2, ROWS, COLS), F32),
            jax.ShapeDtypeStruct((NPANEL, PANEL), F32),
        ),
        in_specs=[pl.BlockSpec(memory_space=pl.ANY)] * 8,
        out_specs=(vmem, vmem),
        scratch_shapes=[
            field, field, field,
            pltpu.VMEM((2, ROWS, COLS), jnp.int32),
            pltpu.VMEM((ROWS, COLS), jnp.int32),
            pltpu.VMEM((NPANEL, PANEL), jnp.int32),
            pltpu.VMEM((NPANEL, SHARE, PANEL), F32),
            field, field, field, field, field, field, field, field,
            pltpu.VMEM((6, 2, ROWS, COLS), F32),
            pltpu.VMEM((6, 2, ROWS, COLS), F32),
            pltpu.VMEM((6, 2, 2, COLS), F32),
            pltpu.VMEM((6, 2, 2, COLS), F32),
            pltpu.VMEM((6, 2, 1, 128), F32),
            pltpu.VMEM((6, 2, 1, 128), F32),
            pltpu.VMEM((2, NX, NY, NPANEL - 1, HALF, PANEL), F32),
            pltpu.VMEM((NX, NY, SHARE, PANEL), F32),
            pltpu.VMEM((NPANEL, PANEL), F32),
            pltpu.VMEM((4, 1, PANEL), F32),
            pltpu.VMEM((PANEL, 128), F32),
            pltpu.VMEM((2, 1, 128), F32),
            pltpu.VMEM((2, 16, 1, 128), F32),
            pltpu.VMEM((2, 4, 128), F32),
            pltpu.VMEM((2, NCOL, 4, 128), F32),
            pltpu.VMEM((3, 128), F32),
            pltpu.VMEM((16, 3, 128), F32),
            pltpu.VMEM((3, 4, 128), F32),
            pltpu.VMEM((NCOL, 3, 4, 128), F32),
            pltpu.VMEM((2, 1, 128), F32),
            pltpu.VMEM((2, NCOL, 1, 128), F32),
            pltpu.VMEM((NPANEL, 128, PANEL), BF16),
            pltpu.VMEM((NPANEL, PANEL), jnp.int32),
            pltpu.VMEM((COLS, 128), BF16),
            dma((9,)), dma((6, 6)), dma((6, 6)),
            dma((7,)), dma((7,)),
            dma((2, 8)), dma((2, 8)),
            dma((8,)), dma((8,)),
            dma((7,)), dma((7,)),
            dma((2, 8)), dma((2, 8)),
            dma((8,)), dma((8,)),
            dma((3,)), dma((3,)),
            dma((4,)), dma((4,)),
            dma((3, 15)), dma((3, 15)),
            dma((3, 31)), dma((3, 31)),
            dma((2, 31)), dma((2, 31)),
        ],
        compiler_params=pltpu.CompilerParams(
            collective_id=0, has_side_effects=True, vmem_limit_bytes=60 * 1024 * 1024
        ),
        cost_estimate=pl.CostEstimate(flops=100_000_000, bytes_accessed=2_000_000, transcendentals=300_000),
        name="grid",
    )(*args)


def solution(mesh):
    placed = (
        P("layer", "row", "col"),
        P("layer", "row", "col"),
        P("layer", "row", "col"),
        P("layer", "row", "col"),
        P("row", "col"),
        P(),
        P(None, "col", None),
        P(None, "col", None),
    )
    return jax.shard_map(
        shards,
        mesh=mesh,
        in_specs=placed,
        out_specs=(P("layer", "row", "col"), P()),
        check_vma=False,
    )
```

```python
import jax
import jax.numpy as jnp
from jax import lax
from jax.experimental import pallas as pl
from jax.experimental.pallas import tpu as pltpu
from jax.sharding import PartitionSpec as P

F32 = jnp.float32
BF16 = jnp.bfloat16
MESH = pl.DeviceIdType.MESH

TILE = 16
PANEL = 512
NPANEL = 4
NX, NY = 4, 8
NCOL = NX * NY
ROWS, COLS = 64, 512
SHARE = PANEL // NCOL
HALF = SHARE // 2

pad_gain = 8.0
bound_low = 0.1
bound_high = 1.9
restrict_scale = 0.25
prolong_scale = 0.5
theta = (bound_high + bound_low) / 2.0
delta = (bound_high - bound_low) / 2.0
sigma = theta / delta


def iota(shape, axis):
    return lax.broadcasted_iota(jnp.int32, shape, axis)


def pieces(x):
    high = x.astype(BF16).astype(F32)
    rest = x - high
    mid = rest.astype(BF16).astype(F32)
    return high, mid, rest - mid


def stacked(x):
    return jnp.concatenate(pieces(x), axis=0).astype(BF16)


def added(y):
    n = y.shape[0] // 3
    return y[:n] + y[n : 2 * n] + y[2 * n :]


def dot(a, b):
    return lax.dot_general(a, b, (((1,), (0,)), ((), ())), preferred_element_type=F32)


def dot_t(a, b):
    return lax.dot_general(a, b, (((1,), (1,)), ((), ())), preferred_element_type=F32)


def kernel(
    src_in, cond_in, via_in, vmap_in, pad_in, pt_in, piv_in, coup_in,
    drop_out, ports_out,
    src, cond, via, vmap, pad, pt, piv,
    S, V, INV, DP, VS, Q, T, CH, HSEND, HALO, RSEND, RIM, CSEND, SIDE,
    G, GP, FW, SL, PART, ZSEND, Z, XM, X, CSND, CZ, CXM, CX, SBM, SB, LANES, ROWM, E4,
    ins, hs, hr, gys, gyr, gxs, gxr, gfs, gfr,
    pys, pyr, pxs, pxr, pfs, pfr, ls, lr, gbs, gbr, zs, zr, xs, xr, bs, br,
):
    l, r, c = lax.axis_index("layer"), lax.axis_index("row"), lax.axis_index("col")
    core = lax.rem(l, 2)
    x, y = c // NY, lax.rem(c, NY)

    def at_col(px, py):
        return (l, r, px * NY + py)

    def far(d, n, m):
        i, j = d // m, d % m
        return -(min(i, n - i) + min(j, m - j))

    group = [
        (lax.rem(l + d % 4, 4), lax.rem(r + d // 4, 4), c)
        for d in sorted(range(1, 16), key=lambda d: far(d, 4, 4) - min(d // 4, 4 - d // 4))
    ]
    plane_peers = [
        (l, r, lax.rem(c + d, NCOL)) for d in sorted(range(1, NCOL), key=lambda d: far(d, NX, NY))
    ]
    sibling = (l + 1 - 2 * core, r, c)

    barrier = pltpu.get_barrier_semaphore()
    for peer in plane_peers + group:
        pl.semaphore_signal(barrier, inc=1, device_id=peer, device_id_type=MESH)

    def remote(a, b, ssem, rsem, peer):
        return pltpu.make_async_remote_copy(
            src_ref=a, dst_ref=b, send_sem=ssem, recv_sem=rsem, device_id=peer, device_id_type=MESH
        )

    inputs = [
        pltpu.make_async_copy(a, b, ins.at[n])
        for n, (a, b) in enumerate(
            (
                (via_in, via),
                (vmap_in, vmap),
                (cond_in, cond),
                (coup_in.at[:, pl.ds(pl.multiple_of(core * HALF, HALF), HALF), :], G.at[core, x, y]),
                (src_in, src),
                (pt_in, pt),
                (pad_in, pad),
                (piv_in, piv),
                (piv_in.at[l], GP.at[x, y]),
            )
        )
    ]
    for copy in inputs:
        copy.start()

    E4[...] = jnp.where(
        iota((COLS, 128), 0) // TILE == lax.rem(iota((COLS, 128), 1), 32), 1.0, 0.0
    ).astype(BF16)

    def tile_row(plane):
        parts = [plane[TILE * a : TILE * a + 8] + plane[TILE * a + 8 : TILE * a + 16] for a in range(4)]
        sums = added(dot(stacked(jnp.concatenate(parts, axis=0)), E4[...]))
        own = iota((32, 128), 0) // 8 == iota((32, 128), 1) // 32
        return jnp.sum(jnp.where(own, sums, 0.0), axis=0, keepdims=True)

    zero_plane = jnp.zeros((ROWS, COLS), F32)

    @pl.when(l == 0)
    def _():
        for rd in range(6):
            HALO[rd, 0] = zero_plane

    @pl.when(l == 3)
    def _():
        for rd in range(6):
            HALO[rd, 1] = zero_plane

    @pl.when(r == 0)
    def _():
        for rd in range(6):
            RIM[rd, 0] = jnp.zeros((2, COLS), F32)

    @pl.when(r == 3)
    def _():
        for rd in range(6):
            RIM[rd, 1] = jnp.zeros((2, COLS), F32)

    @pl.when(c == 0)
    def _():
        for rd in range(6):
            SIDE[rd, 0] = jnp.zeros((1, 128), F32)

    @pl.when(c == NCOL - 1)
    def _():
        for rd in range(6):
            SIDE[rd, 1] = jnp.zeros((1, 128), F32)

    def layer_copies(rd):
        up = remote(HSEND.at[rd, 1], HALO.at[rd, 0], hs.at[rd, 0], hr.at[rd, 0], (lax.rem(l + 1, 4), r, c))
        down = remote(HSEND.at[rd, 0], HALO.at[rd, 1], hs.at[rd, 1], hr.at[rd, 1], (lax.rem(l + 3, 4), r, c))
        return ((l < 3, up, l > 0), (l > 0, down, l < 3))

    def rim_copies(rd):
        south = remote(RSEND.at[rd, 1], RIM.at[rd, 0], hs.at[rd, 2], hr.at[rd, 2], (l, lax.rem(r + 1, 4), c))
        north = remote(RSEND.at[rd, 0], RIM.at[rd, 1], hs.at[rd, 3], hr.at[rd, 3], (l, lax.rem(r + 3, 4), c))
        east = remote(CSEND.at[rd, 1], SIDE.at[rd, 0], hs.at[rd, 4], hr.at[rd, 4], (l, r, lax.rem(c + 1, NCOL)))
        west = remote(
            CSEND.at[rd, 0], SIDE.at[rd, 1], hs.at[rd, 5], hr.at[rd, 5], (l, r, lax.rem(c + NCOL - 1, NCOL))
        )
        return (
            (r < 3, south, r > 0),
            (r > 0, north, r < 3),
            (c < NCOL - 1, east, c > 0),
            (c > 0, west, c < NCOL - 1),
        )

    def start(copies):
        for sends, copy, _ in copies:
            @pl.when(sends)
            def _():
                copy.start()

    def arrive(copies):
        for _, copy, receives in copies:
            @pl.when(receives)
            def _():
                copy.wait_recv()

    def left(copies):
        for sends, copy, _ in copies:
            @pl.when(sends)
            def _():
                copy.wait_send()

    def send_round(rd, g, h):
        rims = rim_copies(rd)
        for p in range(2):
            RSEND[rd, 0, p : p + 1] = g[p][:1]
            RSEND[rd, 1, p : p + 1] = g[p][ROWS - 1 :]
        start(rims[:2])
        for p in range(2):
            HSEND[rd, p] = h[p]
        start(layer_copies(rd))
        first = jnp.concatenate([g[0][:, :128], g[1][:, :128]], axis=0)
        last = jnp.concatenate([g[0][:, COLS - 128 :], g[1][:, COLS - 128 :]], axis=0)
        CSEND[rd, 0] = first.T[:1]
        CSEND[rd, 1] = last.T[127:]
        start(rims[2:])

    def column(rim):
        return jnp.broadcast_to(rim, (128, 128)).T

    row_at = iota((ROWS, COLS), 0)
    col_at = iota((ROWS, 128), 1)

    def from_east(g, side):
        moved = pltpu.roll(g, COLS - 1, 1)
        edge = jnp.where(col_at == 127, side, moved[:, COLS - 128 :])
        return jnp.concatenate([moved[:, : COLS - 128], edge], axis=1)

    def from_west(g, side):
        moved = pltpu.roll(g, 1, 1)
        edge = jnp.where(col_at == 0, side, moved[:, :128])
        return jnp.concatenate([edge, moved[:, 128:]], axis=1)

    def from_south(g, rim):
        return jnp.where(row_at == ROWS - 1, rim, pltpu.roll(g, ROWS - 1, 0))

    def from_north(g, rim):
        return jnp.where(row_at == 0, rim, pltpu.roll(g, 1, 0))

    def plane_sum(g, north, south, west, east):
        west, east = column(west), column(east)
        out = []
        for p in range(2):
            rows = slice(ROWS * p, ROWS * (p + 1))
            out.append(
                from_north(g[p], north[p : p + 1])
                + from_south(g[p], south[p : p + 1])
                + from_west(g[p], west[rows])
                + from_east(g[p], east[rows])
            )
        return out

    def received_sum(rd, g):
        return plane_sum(g, RIM[rd, 0], RIM[rd, 1], SIDE[rd, 0], SIDE[rd, 1])

    def group_copies(it, rows, buf, send):
        slot = r * 4 + l
        return [
            remote(send, buf.at[slot], zs.at[it, d], zr.at[it, d], peer) for d, peer in enumerate(group)
        ]

    def plane_copies(it, send, buf, ss, rs):
        return [remote(send, buf.at[c], ss.at[it, d], rs.at[it, d], peer) for d, peer in enumerate(plane_peers)]

    for copy in inputs[:3]:
        copy.wait()
    for p in range(2):
        S[p] = jnp.sqrt(cond[p])
        V[p] = jnp.sqrt(via[p]) * vmap[p].astype(F32)
    for copy in inputs[3:5]:
        copy.wait()

    pl.semaphore_wait(barrier, 15 + 31)

    send_round(0, [S[0], S[1]], [V[0], V[1]])

    turn = 1 - 2 * core

    class Ring:
        def __init__(self, slot, ys, yr, xs, xr, fs, fr):
            self.slot, self.xs, self.xr, self.fs, self.fr = slot, xs, xr, fs, fr
            self.along_y = {}
            for d, began, step in (
                (1, 0, 1), (7, 0, NY - 1), (2, 0, 2), (6, 0, NY - 2),
                (3, 1, 2), (5, NY - 1, NY - 2), (4, 2 * turn + NY, 2 * turn + NY),
            ):
                piece = slot(x, lax.rem(y + 2 * NY - began, NY))
                self.along_y[d] = remote(
                    piece, piece, ys.at[d - 1], yr.at[d - 1], at_col(x, lax.rem(y + step, NY))
                )

        def along_x(self, d):
            piece = self.slot(x, lax.rem(y + NY - d, NY))
            return [
                remote(piece, piece, self.xs.at[s, d], self.xr.at[s, d], at_col(lax.rem(x + step, NX), y))
                for s, step in enumerate((1, 3))
            ]

        def onward(self, d):
            piece = self.slot(lax.rem(x - turn + NX, NX), lax.rem(y + NY - d, NY))
            return remote(piece, piece, self.fs.at[d], self.fr.at[d], at_col(lax.rem(x + turn + NX, NX), y))

        def begin(self):
            for d in (1, 7, 2, 6):
                self.along_y[d].start()

        def pass_y(self, *ds):
            for d in ds:
                self.along_y[d].wait_recv()
            for d in ds:
                if d in (1, 7):
                    self.along_y[{1: 3, 7: 5}[d]].start()
            if 2 in ds:
                self.along_y[4].start()

        def send_x(self, *ds):
            for d in ds:
                for copy in self.along_x(d):
                    copy.start()

        def pass_x(self, *ds):
            for d in ds:
                for copy in self.along_x(d):
                    copy.wait_recv()
                self.onward(d).start()

        def end(self):
            for d in range(NY):
                self.onward(d).wait_recv()

        def sent(self):
            for d in range(1, NY):
                self.along_y[d].wait_send()
            for d in range(NY):
                for copy in self.along_x(d):
                    copy.wait_send()
                self.onward(d).wait_send()

    lower = Ring(lambda px, py: G.at[core, px, py], gys, gyr, gxs, gxr, gfs, gfr)
    panel = Ring(lambda px, py: GP.at[px, py], pys, pyr, pxs, pxr, pfs, pfr)

    def copy_sibling(j):
        block = G.at[core, lax.rem(x + j, NX)]
        return remote(block, block, gbs.at[j], gbr.at[j], sibling)

    lower.begin()
    lower.send_x(0)
    ZSEND[0] = tile_row(src[0] + src[1])
    group_first = group_copies(0, 1, Z.at[0], ZSEND.at[0])
    for copy in group_first:
        copy.start()

    for copy in inputs[5:]:
        copy.wait()
    for k in range(NPANEL):
        tile = pt[k : k + 1, :]
        arow, acol = tile // 1024, lax.rem(tile, 1024)
        lane = lax.rem(arow, 4) * 32 + lax.rem(acol, 32)
        LANES[k] = jnp.where(iota((128, PANEL), 0) == lane, 1.0, 0.0).astype(BF16)
        ROWM[k : k + 1] = (acol // 32) * 4 + arow // 4

    arrive(rim_copies(0))
    lower.pass_y(1, 7)
    lower.send_x(1, 7)
    arrive(layer_copies(0))
    s = [S[0], S[1]]
    v = [V[0], V[1]]
    around = received_sum(0, s)
    top = (l == 3).astype(F32)
    pads = pad_gain * pad[...].astype(F32) * top
    vsum = [HALO[0, 0] + v[1], v[0] + HALO[0, 1]]
    for p in range(2):
        dp = s[p] * around[p]
        if p == 1:
            dp = dp + pads
        inv = 1.0 / (dp + v[p] * vsum[p])
        t = inv * src[p]
        DP[p], INV[p], VS[p], Q[p], T[p], CH[p] = dp, inv, vsum[p], t, t, t
    send_round(1, [s[p] * T[p] for p in range(2)], [v[p] * T[p] for p in range(2)])

    lower.pass_y(2, 6)
    lower.send_x(2, 6)

    def gather_plane(it, buf, msg, bufx):
        for q in range(4):
            total = buf[4 * q]
            for k in range(1, 4):
                total = total + buf[4 * q + k]
            msg[q : q + 1] = total
        bufx[c] = msg[...]
        out = plane_copies(it, msg, bufx, xs, xr)
        for copy in out:
            copy.start()
        return out

    Z[0, r * 4 + l] = ZSEND[0]
    for copy in group_first:
        copy.wait_recv()
    plane_first = gather_plane(0, Z.at[0], XM.at[0], X.at[0])

    lower.pass_y(3, 5, 4)
    lower.send_x(3, 5, 4)
    lower.pass_x(0, 1, 7)

    def sweep(rd, rho, s, v):
        rho_new = 1.0 / (2.0 * sigma - rho)
        t = [T[0], T[1]]
        arrive(rim_copies(rd))
        around = received_sum(rd, [s[p] * t[p] for p in range(2)])
        arrive(layer_copies(rd))
        vert = [HALO[rd, 0] + v[1] * t[1], v[0] * t[0] + HALO[rd, 1]]
        for p in range(2):
            remain = Q[p] - t[p] + INV[p] * (s[p] * around[p] + v[p] * vert[p])
            ch = (rho_new * rho) * CH[p] + (2.0 * rho_new / delta) * remain
            CH[p] = ch
            T[p] = t[p] + ch
        return rho_new

    rho = sweep(1, 1.0 / sigma, s, v)
    send_round(2, [s[p] * T[p] for p in range(2)], [v[p] * T[p] for p in range(2)])

    lower.pass_x(2, 6)
    copy_sibling(0).start()

    sweep(2, rho, s, v)
    send_round(3, [s[p] * T[p] for p in range(2)], [v[p] * T[p] for p in range(2)])

    lower.pass_x(3, 5, 4)
    copy_sibling(1).start()
    copy_sibling(3).start()
    panel.begin()

    west_col, east_col = SIDE[0, 0], SIDE[0, 1]
    east_side = column(east_col)
    edge_e = jnp.zeros((ROWS, COLS), F32)
    edge_s = jnp.zeros((ROWS, COLS), F32)
    for p in range(2):
        edge_e = edge_e + s[p] * from_east(s[p], east_side[ROWS * p : ROWS * (p + 1)])
        edge_s = edge_s + s[p] * from_south(s[p], RIM[0, 1, p : p + 1])
    edge_e = jnp.where(lax.rem(iota((ROWS, COLS), 1), TILE) == TILE - 1, edge_e, 0.0)
    edge_s = jnp.where(lax.rem(iota((ROWS, COLS), 0), TILE) == TILE - 1, edge_s, 0.0)
    for k, field in enumerate((pads, edge_e, edge_s)):
        CSND[k : k + 1] = tile_row(field)
    CZ[r * 4 + l] = CSND[...]
    group_coef = group_copies(1, 3, CZ, CSND)
    for copy in group_coef:
        copy.start()

    def tile_map(load):
        return jnp.concatenate([load(k) for k in range(NCOL)], axis=0)

    def row_mask(k):
        return iota((128, PANEL), 0) == ROWM[k : k + 1]

    def select_ports(tiles):
        parts = stacked(tiles)
        out = []
        for k in range(NPANEL):
            picked = added(dot(parts, LANES[k]))
            out.append(
                jnp.sum(jnp.where(row_mask(k), picked, 0.0), axis=0, keepdims=True) * (restrict_scale / TILE)
            )
        return out

    for copy in plane_first:
        copy.wait_recv()
    rhs = select_ports(tile_map(lambda k: X[0, k]))

    lower.end()
    copy_sibling(2).start()
    panel.pass_y(1, 7, 2, 6)

    arrive(rim_copies(3))
    around = received_sum(3, [s[p] * T[p] for p in range(2)])
    flat = [src[p] - (DP[p] * T[p] - s[p] * around[p]) for p in range(2)]
    ZSEND[1] = tile_row(flat[0] + flat[1])
    Z[1, r * 4 + l] = ZSEND[1]
    group_second = group_copies(2, 1, Z.at[1], ZSEND.at[1])
    for copy in group_second:
        copy.start()

    def times(block, f):
        wide = jnp.broadcast_to(f, (8, PANEL))

        def body(i, carry):
            px, py = i // NY, lax.rem(i, NY)
            for h in range(2):
                prod = block(px, py, h) * wide
                part = prod[:, :128] + prod[:, 128:256] + prod[:, 256:384] + prod[:, 384:]
                PART[pl.ds(pl.multiple_of(i * SHARE + h * HALF, HALF), HALF)] = part
            return carry

        lax.fori_loop(0, NCOL, body, 0, unroll=NCOL)
        return jnp.concatenate(
            [jnp.sum(PART[128 * j : 128 * (j + 1)].T, axis=0, keepdims=True) for j in range(4)], axis=1
        )

    def minus_transposed(k, f):
        for j in range(4):
            PART[128 * j : 128 * (j + 1)] = column(f[:, 128 * j : 128 * (j + 1)])

        def body(i, acc):
            px, py = i // NY, lax.rem(i, NY)
            for h in range(2):
                w = PART[pl.ds(pl.multiple_of(i * SHARE + h * HALF, HALF), HALF)]
                acc = acc + G[h, px, py, k] * jnp.concatenate([w] * 4, axis=1)
            return acc

        acc = lax.fori_loop(0, NCOL, body, jnp.zeros((8, PANEL), F32), unroll=NCOL)
        return jnp.sum(acc, axis=0, keepdims=True)

    def forward_of(rhs):
        forward = [rhs[0]]
        for k in range(1, NPANEL):
            forward.append(rhs[k] - times(lambda px, py, h: G[h, px, py, k - 1], forward[-1]))
        return forward

    def solve_first(it, rhs):
        forward = forward_of(rhs)
        rows = []
        for k in range(NPANEL):
            prod = piv[k] * forward[k]
            rows.append(prod[:, :128] + prod[:, 128:256] + prod[:, 256:384] + prod[:, 384:])
        rows.append(jnp.zeros((128 - NPANEL * SHARE, 128), F32))
        SBM[it] = jnp.sum(jnp.concatenate(rows, axis=0).T, axis=0, keepdims=True)
        SB[it, c] = SBM[it]
        copies = plane_copies(it, SBM.at[it], SB.at[it], bs, br)
        for copy in copies:
            copy.start()
        return copies

    def solve_second(it, copies):
        for copy in copies:
            copy.wait_recv()
        got = stacked(jnp.concatenate([SB[it, k] for k in range(NCOL)], axis=0))
        owner = iota((NCOL, PANEL), 1) // SHARE == iota((NCOL, PANEL), 0)
        scaled = []
        for k in range(NPANEL):
            spread = jnp.where(
                iota((128, PANEL), 0) == k * SHARE + lax.rem(iota((128, PANEL), 1), SHARE), 1.0, 0.0
            ).astype(BF16)
            value = added(dot(got, spread))
            scaled.append(jnp.sum(jnp.where(owner, value, 0.0), axis=0, keepdims=True))
        return backward_of(scaled)

    def backward_of(scaled):
        ports = [None] * NPANEL
        ports[NPANEL - 1] = scaled[NPANEL - 1]
        for k in range(NPANEL - 2, -1, -1):
            ports[k] = scaled[k] - minus_transposed(k, ports[k + 1])
        return ports

    def lifted_rows(ports, wanted):
        total = jnp.zeros((24, 128), F32)
        for k in range(NPANEL):
            parts = pieces(ports[k] * prolong_scale)
            masks = [ROWM[k : k + 1] == w for w in wanted]
            masks += [masks[0]] * (8 - len(masks))
            rows = [jnp.where(m, part, 0.0) for part in parts for m in masks]
            total = total + dot_t(jnp.concatenate(rows, axis=0).astype(BF16), LANES[k])
        return added(total)

    lane_row = iota((1, 128), 1)

    def spread_rows(rows):
        return added(dot_t(stacked(rows), E4[...]))

    def field_of(own):
        return jnp.concatenate([jnp.where(lane_row // 32 == min(a, 3), own, 0.0) for a in range(4)], axis=0)

    for j in range(NX):
        copy_sibling(j).wait_recv()
    first = solve_first(0, rhs)

    arrive(layer_copies(3))
    vert = [HALO[3, 0] + v[1] * T[1], v[0] * T[0] + HALO[3, 1]]
    for p in range(2):
        t = T[p]
        Q[p] = flat[p] - v[p] * (VS[p] * t - vert[p])
    for copy in group_coef:
        copy.wait_recv()
    for q in range(4):
        total = CZ[4 * q]
        for k in range(1, 4):
            total = total + CZ[4 * q + k]
        for k in range(3):
            CXM[k, q : q + 1] = total[k : k + 1]
    CX[c] = CXM[...]
    plane_coef = plane_copies(1, CXM, CX, xs, xr)
    for copy in plane_coef:
        copy.start()


    for copy in group_second:
        copy.wait_recv()
    plane_second = gather_plane(2, Z.at[1], XM.at[1], X.at[1])
    panel.pass_y(3, 5, 4)
    panel.send_x(0, 1, 7, 2, 6, 3, 5, 4)
    ports1 = solve_second(0, first)

    own_row = c * 4 + r
    none = jnp.int32(-1)
    wanted = [
        own_row,
        jnp.where(r > 0, own_row - 1, none),
        jnp.where(r < 3, own_row + 1, none),
        jnp.where(c > 0, own_row - 4, none),
        jnp.where(c < NCOL - 1, own_row + 4, none),
    ]
    near = lifted_rows(ports1, wanted)
    level = jnp.concatenate(
        [
            field_of(near[0:1]),
            jnp.where(lane_row // 32 == 3, near[1:2], 0.0),
            jnp.where(lane_row // 32 == 0, near[2:3], 0.0),
            jnp.zeros((2, 128), F32),
        ],
        axis=0,
    )
    level = spread_rows(level)
    lift = jnp.concatenate(
        [jnp.broadcast_to(level[a : a + 1], (TILE, COLS)) for a in range(4)], axis=0
    )
    at_row = lax.rem(iota((128, 128), 1), ROWS) // TILE * 32
    pick_w = jnp.where(iota((128, 128), 0) == at_row + 31, 1.0, 0.0).astype(BF16)
    pick_e = jnp.where(iota((128, 128), 0) == at_row, 1.0, 0.0).astype(BF16)
    side_w = added(dot(stacked(near), pick_w))[3:4]
    side_e = added(dot(stacked(near), pick_e))[4:5]
    lifted_around = plane_sum(
        [s[p] * lift for p in range(2)],
        RIM[0, 0] * level[4:5],
        RIM[0, 1] * level[5:6],
        SIDE[0, 0] * side_w,
        SIDE[0, 1] * side_e,
    )
    for p in range(2):
        t3 = T[p]
        resid = Q[p] - (DP[p] * lift - s[p] * lifted_around[p])
        t = INV[p] * resid
        drop_out[p] = lift + t3
        Q[p], T[p], CH[p] = t, t, t
    send_round(4, [s[p] * T[p] for p in range(2)], [v[p] * T[p] for p in range(2)])
    panel.pass_x(0, 1, 7, 2, 6)

    lifted_map = jnp.zeros((384, 128), F32)
    for k in range(NPANEL):
        mask = row_mask(k)
        parts = [jnp.where(mask, part, 0.0).astype(BF16) for part in pieces(ports1[k] * prolong_scale)]
        lifted_map = lifted_map + dot_t(jnp.concatenate(parts, axis=0), LANES[k])
    lifted_map = added(lifted_map)
    for copy in plane_coef:
        copy.wait_recv()
    pads_map = tile_map(lambda k: CX[k, 0])
    edge_e = tile_map(lambda k: CX[k, 1])
    edge_s = tile_map(lambda k: CX[k, 2])
    lanes = iota((128, 128), 1)

    def tile_east(a):
        ahead = pltpu.roll(a, 124, 0)
        return jnp.where(lax.rem(lanes, 32) == 31, pltpu.roll(ahead, 31, 1), pltpu.roll(a, 127, 1))

    def tile_west(a):
        behind = pltpu.roll(a, 4, 0)
        return jnp.where(lax.rem(lanes, 32) == 0, pltpu.roll(behind, 97, 1), pltpu.roll(a, 1, 1))

    def tile_south(a):
        below = pltpu.roll(a, 127, 0)
        return jnp.where(lanes // 32 == 3, pltpu.roll(below, 96, 1), pltpu.roll(a, 96, 1))

    def tile_north(a):
        above = pltpu.roll(a, 1, 0)
        return jnp.where(lanes // 32 == 0, pltpu.roll(above, 32, 1), pltpu.roll(a, 32, 1))

    flow_e = edge_e * (lifted_map - tile_east(lifted_map))
    flow_s = edge_s * (lifted_map - tile_south(lifted_map))
    coarse = pads_map * lifted_map + flow_e - tile_west(flow_e) + flow_s - tile_north(flow_s)

    panel.pass_x(3, 5, 4)
    for copy in plane_second:
        copy.wait_recv()
    rhs = select_ports(tile_map(lambda k: X[1, k]) - coarse)
    rho = sweep(4, 1.0 / sigma, s, v)
    send_round(5, [s[p] * T[p] for p in range(2)], [v[p] * T[p] for p in range(2)])

    forward = forward_of(rhs)
    for k in range(NPANEL):
        FW[k : k + 1] = forward[k]
    panel.end()
    SL[l] = times(
        lambda px, py, h: GP[px, py, HALF * h : HALF * (h + 1)], FW[pl.ds(l, 1)]
    )
    second = [
        remote(SL.at[l], SL.at[l], ls.at[d - 1], lr.at[d - 1], (lax.rem(l + d, 4), r, c)) for d in range(1, 4)
    ]
    for copy in second:
        copy.start()

    for copy in second:
        copy.wait_recv()
    ports2 = backward_of([SL[k] for k in range(NPANEL)])
    for k in range(NPANEL):
        ports_out[k : k + 1] = ports2[k]
    near = lifted_rows(ports2, [own_row])
    level = spread_rows(jnp.concatenate([field_of(near[0:1])] * 2, axis=0))
    sweep(5, rho, s, v)
    for p in range(2):
        for a in range(4):
            rows = slice(TILE * a, TILE * (a + 1))
            drop_out[p, rows] = drop_out[p, rows] + T[p, rows] + level[a : a + 1]

    for rd in range(6):
        left(layer_copies(rd))
        left(rim_copies(rd))
    lower.sent()
    panel.sent()
    for copy in group_first + group_coef + group_second:
        copy.wait_send()
    for copy in plane_first + plane_coef + plane_second + first + second:
        copy.wait_send()
    for j in range(NX):
        copy_sibling(j).wait_send()


def shards(*args):
    vmem = pl.BlockSpec(memory_space=pltpu.VMEM)
    field = pltpu.VMEM((2, ROWS, COLS), F32)
    dma = pltpu.SemaphoreType.DMA
    return pl.pallas_call(
        kernel,
        out_shape=(
            jax.ShapeDtypeStruct((2, ROWS, COLS), F32),
            jax.ShapeDtypeStruct((NPANEL, PANEL), F32),
        ),
        in_specs=[pl.BlockSpec(memory_space=pl.ANY)] * 8,
        out_specs=(vmem, vmem),
        scratch_shapes=[
            field, field, field,
            pltpu.VMEM((2, ROWS, COLS), jnp.int32),
            pltpu.VMEM((ROWS, COLS), jnp.int32),
            pltpu.VMEM((NPANEL, PANEL), jnp.int32),
            pltpu.VMEM((NPANEL, SHARE, PANEL), F32),
            field, field, field, field, field, field, field, field,
            pltpu.VMEM((6, 2, ROWS, COLS), F32),
            pltpu.VMEM((6, 2, ROWS, COLS), F32),
            pltpu.VMEM((6, 2, 2, COLS), F32),
            pltpu.VMEM((6, 2, 2, COLS), F32),
            pltpu.VMEM((6, 2, 1, 128), F32),
            pltpu.VMEM((6, 2, 1, 128), F32),
            pltpu.VMEM((2, NX, NY, NPANEL - 1, HALF, PANEL), F32),
            pltpu.VMEM((NX, NY, SHARE, PANEL), F32),
            pltpu.VMEM((NPANEL, PANEL), F32),
            pltpu.VMEM((4, 1, PANEL), F32),
            pltpu.VMEM((PANEL, 128), F32),
            pltpu.VMEM((2, 1, 128), F32),
            pltpu.VMEM((2, 16, 1, 128), F32),
            pltpu.VMEM((2, 4, 128), F32),
            pltpu.VMEM((2, NCOL, 4, 128), F32),
            pltpu.VMEM((3, 128), F32),
            pltpu.VMEM((16, 3, 128), F32),
            pltpu.VMEM((3, 4, 128), F32),
            pltpu.VMEM((NCOL, 3, 4, 128), F32),
            pltpu.VMEM((2, 1, 128), F32),
            pltpu.VMEM((2, NCOL, 1, 128), F32),
            pltpu.VMEM((NPANEL, 128, PANEL), BF16),
            pltpu.VMEM((NPANEL, PANEL), jnp.int32),
            pltpu.VMEM((COLS, 128), BF16),
            dma((9,)), dma((6, 6)), dma((6, 6)),
            dma((7,)), dma((7,)),
            dma((2, 8)), dma((2, 8)),
            dma((8,)), dma((8,)),
            dma((7,)), dma((7,)),
            dma((2, 8)), dma((2, 8)),
            dma((8,)), dma((8,)),
            dma((3,)), dma((3,)),
            dma((4,)), dma((4,)),
            dma((3, 15)), dma((3, 15)),
            dma((3, 31)), dma((3, 31)),
            dma((2, 31)), dma((2, 31)),
        ],
        compiler_params=pltpu.CompilerParams(
            collective_id=0, has_side_effects=True, vmem_limit_bytes=60 * 1024 * 1024
        ),
        cost_estimate=pl.CostEstimate(flops=100_000_000, bytes_accessed=2_000_000, transcendentals=300_000),
        name="grid",
    )(*args)


def solution(mesh):
    placed = (
        P("layer", "row", "col"),
        P("layer", "row", "col"),
        P("layer", "row", "col"),
        P("layer", "row", "col"),
        P("row", "col"),
        P(),
        P(None, "col", None),
        P(None, "col", None),
    )
    return jax.shard_map(
        shards,
        mesh=mesh,
        in_specs=placed,
        out_specs=(P("layer", "row", "col"), P()),
        check_vma=False,
    )
```

```python
import jax
import jax.numpy as jnp
from jax import lax
from jax.experimental import pallas as pl
from jax.experimental.pallas import tpu as pltpu
from jax.sharding import PartitionSpec as P

F32 = jnp.float32
BF16 = jnp.bfloat16
MESH = pl.DeviceIdType.MESH

TILE = 16
PANEL = 512
NPANEL = 4
NX, NY = 4, 8
NCOL = NX * NY
ROWS, COLS = 64, 512
SHARE = PANEL // NCOL
HALF = SHARE // 2

pad_gain = 8.0
bound_low = 0.1
bound_high = 1.9
restrict_scale = 0.25
prolong_scale = 0.5
theta = (bound_high + bound_low) / 2.0
delta = (bound_high - bound_low) / 2.0
sigma = theta / delta


def iota(shape, axis):
    return lax.broadcasted_iota(jnp.int32, shape, axis)


def pieces(x):
    high = x.astype(BF16).astype(F32)
    rest = x - high
    mid = rest.astype(BF16).astype(F32)
    return high, mid, rest - mid


def stacked(x):
    return jnp.concatenate(pieces(x), axis=0).astype(BF16)


def added(y):
    n = y.shape[0] // 3
    return y[:n] + y[n : 2 * n] + y[2 * n :]


def dot(a, b):
    return lax.dot_general(a, b, (((1,), (0,)), ((), ())), preferred_element_type=F32)


def dot_t(a, b):
    return lax.dot_general(a, b, (((1,), (1,)), ((), ())), preferred_element_type=F32)


def kernel(
    src_in, cond_in, via_in, vmap_in, pad_in, pt_in, piv_in, coup_in,
    drop_out, ports_out,
    src, cond, via, vmap, pad, pt, piv,
    S, V, INV, DP, VS, Q, T, CH, HSEND, HALO, RSEND, RIM, CSEND, SIDE,
    G, GP, FW, SL, PART, ZSEND, Z, XM, X, CSND, CZ, CXM, CX, SBM, SB, LANES, ROWM, E4,
    ins, hs, hr, gys, gyr, gxs, gxr, gfs, gfr,
    pys, pyr, pxs, pxr, pfs, pfr, ls, lr, gbs, gbr, zs, zr, xs, xr, bs, br,
):
    l, r, c = lax.axis_index("layer"), lax.axis_index("row"), lax.axis_index("col")
    core = lax.rem(l, 2)
    x, y = c // NY, lax.rem(c, NY)

    def at_col(px, py):
        return (l, r, px * NY + py)

    def far(d, n, m):
        i, j = d // m, d % m
        return -(min(i, n - i) + min(j, m - j))

    group = [
        (lax.rem(l + d % 4, 4), lax.rem(r + d // 4, 4), c)
        for d in sorted(range(1, 16), key=lambda d: far(d, 4, 4) - min(d // 4, 4 - d // 4))
    ]
    plane_peers = [
        (l, r, lax.rem(c + d, NCOL)) for d in sorted(range(1, NCOL), key=lambda d: far(d, NX, NY))
    ]
    sibling = (l + 1 - 2 * core, r, c)

    barrier = pltpu.get_barrier_semaphore()
    for peer in plane_peers + group:
        pl.semaphore_signal(barrier, inc=1, device_id=peer, device_id_type=MESH)

    def remote(a, b, ssem, rsem, peer):
        return pltpu.make_async_remote_copy(
            src_ref=a, dst_ref=b, send_sem=ssem, recv_sem=rsem, device_id=peer, device_id_type=MESH
        )

    inputs = [
        pltpu.make_async_copy(a, b, ins.at[n])
        for n, (a, b) in enumerate(
            (
                (via_in, via),
                (vmap_in, vmap),
                (cond_in, cond),
                (coup_in.at[:, pl.ds(pl.multiple_of(core * HALF, HALF), HALF), :], G.at[core, x, y]),
                (src_in, src),
                (pt_in, pt),
                (pad_in, pad),
                (piv_in, piv),
                (piv_in.at[l], GP.at[x, y]),
            )
        )
    ]
    for copy in inputs:
        copy.start()

    E4[...] = jnp.where(
        iota((COLS, 128), 0) // TILE == lax.rem(iota((COLS, 128), 1), 32), 1.0, 0.0
    ).astype(BF16)

    def tile_row(plane):
        parts = [plane[TILE * a : TILE * a + 8] + plane[TILE * a + 8 : TILE * a + 16] for a in range(4)]
        sums = added(dot(stacked(jnp.concatenate(parts, axis=0)), E4[...]))
        own = iota((32, 128), 0) // 8 == iota((32, 128), 1) // 32
        return jnp.sum(jnp.where(own, sums, 0.0), axis=0, keepdims=True)

    zero_plane = jnp.zeros((ROWS, COLS), F32)

    @pl.when(l == 0)
    def _():
        for rd in range(6):
            HALO[rd, 0] = zero_plane

    @pl.when(l == 3)
    def _():
        for rd in range(6):
            HALO[rd, 1] = zero_plane

    @pl.when(r == 0)
    def _():
        for rd in range(6):
            RIM[rd, 0] = jnp.zeros((2, COLS), F32)

    @pl.when(r == 3)
    def _():
        for rd in range(6):
            RIM[rd, 1] = jnp.zeros((2, COLS), F32)

    @pl.when(c == 0)
    def _():
        for rd in range(6):
            SIDE[rd, 0] = jnp.zeros((1, 128), F32)

    @pl.when(c == NCOL - 1)
    def _():
        for rd in range(6):
            SIDE[rd, 1] = jnp.zeros((1, 128), F32)

    def layer_copies(rd):
        up = remote(HSEND.at[rd, 1], HALO.at[rd, 0], hs.at[rd, 0], hr.at[rd, 0], (lax.rem(l + 1, 4), r, c))
        down = remote(HSEND.at[rd, 0], HALO.at[rd, 1], hs.at[rd, 1], hr.at[rd, 1], (lax.rem(l + 3, 4), r, c))
        return ((l < 3, up, l > 0), (l > 0, down, l < 3))

    def rim_copies(rd):
        south = remote(RSEND.at[rd, 1], RIM.at[rd, 0], hs.at[rd, 2], hr.at[rd, 2], (l, lax.rem(r + 1, 4), c))
        north = remote(RSEND.at[rd, 0], RIM.at[rd, 1], hs.at[rd, 3], hr.at[rd, 3], (l, lax.rem(r + 3, 4), c))
        east = remote(CSEND.at[rd, 1], SIDE.at[rd, 0], hs.at[rd, 4], hr.at[rd, 4], (l, r, lax.rem(c + 1, NCOL)))
        west = remote(
            CSEND.at[rd, 0], SIDE.at[rd, 1], hs.at[rd, 5], hr.at[rd, 5], (l, r, lax.rem(c + NCOL - 1, NCOL))
        )
        return (
            (r < 3, south, r > 0),
            (r > 0, north, r < 3),
            (c < NCOL - 1, east, c > 0),
            (c > 0, west, c < NCOL - 1),
        )

    def start(copies):
        for sends, copy, _ in copies:
            @pl.when(sends)
            def _():
                copy.start()

    def arrive(copies):
        for _, copy, receives in copies:
            @pl.when(receives)
            def _():
                copy.wait_recv()

    def left(copies):
        for sends, copy, _ in copies:
            @pl.when(sends)
            def _():
                copy.wait_send()

    def send_round(rd, g, h):
        rims = rim_copies(rd)
        for p in range(2):
            RSEND[rd, 0, p : p + 1] = g[p][:1]
            RSEND[rd, 1, p : p + 1] = g[p][ROWS - 1 :]
        start(rims[:2])
        for p in range(2):
            HSEND[rd, p] = h[p]
        start(layer_copies(rd))
        first = jnp.concatenate([g[0][:, :128], g[1][:, :128]], axis=0)
        last = jnp.concatenate([g[0][:, COLS - 128 :], g[1][:, COLS - 128 :]], axis=0)
        CSEND[rd, 0] = first.T[:1]
        CSEND[rd, 1] = last.T[127:]
        start(rims[2:])

    def column(rim):
        return jnp.broadcast_to(rim, (128, 128)).T

    row_at = iota((ROWS, COLS), 0)
    col_at = iota((ROWS, 128), 1)

    def from_east(g, side):
        moved = pltpu.roll(g, COLS - 1, 1)
        edge = jnp.where(col_at == 127, side, moved[:, COLS - 128 :])
        return jnp.concatenate([moved[:, : COLS - 128], edge], axis=1)

    def from_west(g, side):
        moved = pltpu.roll(g, 1, 1)
        edge = jnp.where(col_at == 0, side, moved[:, :128])
        return jnp.concatenate([edge, moved[:, 128:]], axis=1)

    def from_south(g, rim):
        return jnp.where(row_at == ROWS - 1, rim, pltpu.roll(g, ROWS - 1, 0))

    def from_north(g, rim):
        return jnp.where(row_at == 0, rim, pltpu.roll(g, 1, 0))

    def plane_sum(g, north, south, west, east):
        west, east = column(west), column(east)
        out = []
        for p in range(2):
            rows = slice(ROWS * p, ROWS * (p + 1))
            out.append(
                from_north(g[p], north[p : p + 1])
                + from_south(g[p], south[p : p + 1])
                + from_west(g[p], west[rows])
                + from_east(g[p], east[rows])
            )
        return out

    def received_sum(rd, g):
        return plane_sum(g, RIM[rd, 0], RIM[rd, 1], SIDE[rd, 0], SIDE[rd, 1])

    def group_copies(it, rows, buf, send):
        slot = r * 4 + l
        return [
            remote(send, buf.at[slot], zs.at[it, d], zr.at[it, d], peer) for d, peer in enumerate(group)
        ]

    def plane_copies(it, send, buf, ss, rs):
        return [remote(send, buf.at[c], ss.at[it, d], rs.at[it, d], peer) for d, peer in enumerate(plane_peers)]

    for copy in inputs[:3]:
        copy.wait()
    for p in range(2):
        S[p] = jnp.sqrt(cond[p])
        V[p] = jnp.sqrt(via[p]) * vmap[p].astype(F32)
    for copy in inputs[3:5]:
        copy.wait()

    pl.semaphore_wait(barrier, 15 + 31)

    send_round(0, [S[0], S[1]], [V[0], V[1]])

    turn = 1 - 2 * core

    class Ring:
        def __init__(self, slot, ys, yr, xs, xr, fs, fr):
            self.slot, self.xs, self.xr, self.fs, self.fr = slot, xs, xr, fs, fr
            self.along_y = {}
            for d, began, step in (
                (1, 0, 1), (7, 0, NY - 1), (2, 0, 2), (6, 0, NY - 2),
                (3, 1, 2), (5, NY - 1, NY - 2), (4, 2 * turn + NY, 2 * turn + NY),
            ):
                piece = slot(x, lax.rem(y + 2 * NY - began, NY))
                self.along_y[d] = remote(
                    piece, piece, ys.at[d - 1], yr.at[d - 1], at_col(x, lax.rem(y + step, NY))
                )

        def along_x(self, d):
            piece = self.slot(x, lax.rem(y + NY - d, NY))
            return [
                remote(piece, piece, self.xs.at[s, d], self.xr.at[s, d], at_col(lax.rem(x + step, NX), y))
                for s, step in enumerate((1, 3))
            ]

        def onward(self, d):
            piece = self.slot(lax.rem(x - turn + NX, NX), lax.rem(y + NY - d, NY))
            return remote(piece, piece, self.fs.at[d], self.fr.at[d], at_col(lax.rem(x + turn + NX, NX), y))

        def begin(self):
            for d in (1, 7, 2, 6):
                self.along_y[d].start()

        def pass_y(self, *ds):
            for d in ds:
                self.along_y[d].wait_recv()
            for d in ds:
                if d in (1, 7):
                    self.along_y[{1: 3, 7: 5}[d]].start()
            if 2 in ds:
                self.along_y[4].start()

        def send_x(self, *ds):
            for d in ds:
                for copy in self.along_x(d):
                    copy.start()

        def pass_x(self, *ds):
            for d in ds:
                for copy in self.along_x(d):
                    copy.wait_recv()
                self.onward(d).start()

        def end(self):
            for d in range(NY):
                self.onward(d).wait_recv()

        def sent(self):
            for d in range(1, NY):
                self.along_y[d].wait_send()
            for d in range(NY):
                for copy in self.along_x(d):
                    copy.wait_send()
                self.onward(d).wait_send()

    lower = Ring(lambda px, py: G.at[core, px, py], gys, gyr, gxs, gxr, gfs, gfr)
    panel = Ring(lambda px, py: GP.at[px, py], pys, pyr, pxs, pxr, pfs, pfr)

    def copy_sibling(j):
        block = G.at[core, lax.rem(x + j, NX)]
        return remote(block, block, gbs.at[j], gbr.at[j], sibling)

    lower.begin()
    lower.send_x(0)
    ZSEND[0] = tile_row(src[0] + src[1])
    group_first = group_copies(0, 1, Z.at[0], ZSEND.at[0])
    for copy in group_first:
        copy.start()

    for copy in inputs[5:]:
        copy.wait()
    for k in range(NPANEL):
        tile = pt[k : k + 1, :]
        arow, acol = tile // 1024, lax.rem(tile, 1024)
        lane = lax.rem(arow, 4) * 32 + lax.rem(acol, 32)
        LANES[k] = jnp.where(iota((128, PANEL), 0) == lane, 1.0, 0.0).astype(BF16)
        ROWM[k : k + 1] = (acol // 32) * 4 + arow // 4

    arrive(rim_copies(0))
    lower.pass_y(1, 7)
    lower.send_x(1, 7)
    arrive(layer_copies(0))
    s = [S[0], S[1]]
    v = [V[0], V[1]]
    around = received_sum(0, s)
    top = (l == 3).astype(F32)
    pads = pad_gain * pad[...].astype(F32) * top
    vsum = [HALO[0, 0] + v[1], v[0] + HALO[0, 1]]
    for p in range(2):
        dp = s[p] * around[p]
        if p == 1:
            dp = dp + pads
        inv = 1.0 / (dp + v[p] * vsum[p])
        t = inv * src[p]
        DP[p], INV[p], VS[p], Q[p], T[p], CH[p] = dp, inv, vsum[p], t, t, t
    send_round(1, [s[p] * T[p] for p in range(2)], [v[p] * T[p] for p in range(2)])

    lower.pass_y(2, 6)
    lower.send_x(2, 6)

    def gather_plane(it, buf, msg, bufx):
        for q in range(4):
            total = buf[4 * q]
            for k in range(1, 4):
                total = total + buf[4 * q + k]
            msg[q : q + 1] = total
        bufx[c] = msg[...]
        out = plane_copies(it, msg, bufx, xs, xr)
        for copy in out:
            copy.start()
        return out

    Z[0, r * 4 + l] = ZSEND[0]
    for copy in group_first:
        copy.wait_recv()
    plane_first = gather_plane(0, Z.at[0], XM.at[0], X.at[0])

    west_col, east_col = SIDE[0, 0], SIDE[0, 1]
    east_side = column(east_col)
    edge_e = jnp.zeros((ROWS, COLS), F32)
    edge_s = jnp.zeros((ROWS, COLS), F32)
    for p in range(2):
        edge_e = edge_e + s[p] * from_east(s[p], east_side[ROWS * p : ROWS * (p + 1)])
        edge_s = edge_s + s[p] * from_south(s[p], RIM[0, 1, p : p + 1])
    edge_e = jnp.where(lax.rem(iota((ROWS, COLS), 1), TILE) == TILE - 1, edge_e, 0.0)
    edge_s = jnp.where(lax.rem(iota((ROWS, COLS), 0), TILE) == TILE - 1, edge_s, 0.0)
    for k, field in enumerate((pads, edge_e, edge_s)):
        CSND[k : k + 1] = tile_row(field)
    CZ[r * 4 + l] = CSND[...]
    group_coef = group_copies(1, 3, CZ, CSND)
    for copy in group_coef:
        copy.start()


    lower.pass_y(3, 5, 4)
    lower.send_x(3, 5, 4)
    lower.pass_x(0, 1, 7)

    def sweep(rd, rho, s, v):
        rho_new = 1.0 / (2.0 * sigma - rho)
        t = [T[0], T[1]]
        arrive(rim_copies(rd))
        around = received_sum(rd, [s[p] * t[p] for p in range(2)])
        arrive(layer_copies(rd))
        vert = [HALO[rd, 0] + v[1] * t[1], v[0] * t[0] + HALO[rd, 1]]
        for p in range(2):
            remain = Q[p] - t[p] + INV[p] * (s[p] * around[p] + v[p] * vert[p])
            ch = (rho_new * rho) * CH[p] + (2.0 * rho_new / delta) * remain
            CH[p] = ch
            T[p] = t[p] + ch
        return rho_new

    rho = sweep(1, 1.0 / sigma, s, v)
    send_round(2, [s[p] * T[p] for p in range(2)], [v[p] * T[p] for p in range(2)])

    lower.pass_x(2, 6)
    copy_sibling(0).start()
    for copy in group_coef:
        copy.wait_recv()
    for q in range(4):
        total = CZ[4 * q]
        for k in range(1, 4):
            total = total + CZ[4 * q + k]
        for k in range(3):
            CXM[k, q : q + 1] = total[k : k + 1]
    CX[c] = CXM[...]
    plane_coef = plane_copies(1, CXM, CX, xs, xr)
    for copy in plane_coef:
        copy.start()

    sweep(2, rho, s, v)
    send_round(3, [s[p] * T[p] for p in range(2)], [v[p] * T[p] for p in range(2)])

    lower.pass_x(3, 5, 4)
    copy_sibling(1).start()
    copy_sibling(3).start()
    panel.begin()

    def tile_map(load):
        return jnp.concatenate([load(k) for k in range(NCOL)], axis=0)

    def row_mask(k):
        return iota((128, PANEL), 0) == ROWM[k : k + 1]

    def select_ports(tiles):
        parts = stacked(tiles)
        out = []
        for k in range(NPANEL):
            picked = added(dot(parts, LANES[k]))
            out.append(
                jnp.sum(jnp.where(row_mask(k), picked, 0.0), axis=0, keepdims=True) * (restrict_scale / TILE)
            )
        return out

    for copy in plane_first:
        copy.wait_recv()
    rhs = select_ports(tile_map(lambda k: X[0, k]))

    lower.end()
    copy_sibling(2).start()
    panel.pass_y(1, 7, 2, 6)

    arrive(rim_copies(3))
    around = received_sum(3, [s[p] * T[p] for p in range(2)])
    flat = [src[p] - (DP[p] * T[p] - s[p] * around[p]) for p in range(2)]
    ZSEND[1] = tile_row(flat[0] + flat[1])
    Z[1, r * 4 + l] = ZSEND[1]
    group_second = group_copies(2, 1, Z.at[1], ZSEND.at[1])
    for copy in group_second:
        copy.start()

    def times(block, f):
        wide = jnp.broadcast_to(f, (8, PANEL))

        def body(i, carry):
            px, py = i // NY, lax.rem(i, NY)
            for h in range(2):
                prod = block(px, py, h) * wide
                part = prod[:, :128] + prod[:, 128:256] + prod[:, 256:384] + prod[:, 384:]
                PART[pl.ds(pl.multiple_of(i * SHARE + h * HALF, HALF), HALF)] = part
            return carry

        lax.fori_loop(0, NCOL, body, 0, unroll=NCOL)
        return jnp.concatenate(
            [jnp.sum(PART[128 * j : 128 * (j + 1)].T, axis=0, keepdims=True) for j in range(4)], axis=1
        )

    def minus_transposed(k, f):
        for j in range(4):
            PART[128 * j : 128 * (j + 1)] = column(f[:, 128 * j : 128 * (j + 1)])

        def body(i, acc):
            px, py = i // NY, lax.rem(i, NY)
            for h in range(2):
                w = PART[pl.ds(pl.multiple_of(i * SHARE + h * HALF, HALF), HALF)]
                acc = acc + G[h, px, py, k] * jnp.concatenate([w] * 4, axis=1)
            return acc

        acc = lax.fori_loop(0, NCOL, body, jnp.zeros((8, PANEL), F32), unroll=NCOL)
        return jnp.sum(acc, axis=0, keepdims=True)

    def forward_of(rhs):
        forward = [rhs[0]]
        for k in range(1, NPANEL):
            forward.append(rhs[k] - times(lambda px, py, h: G[h, px, py, k - 1], forward[-1]))
        return forward

    def solve_first(it, rhs):
        forward = forward_of(rhs)
        rows = []
        for k in range(NPANEL):
            prod = piv[k] * forward[k]
            rows.append(prod[:, :128] + prod[:, 128:256] + prod[:, 256:384] + prod[:, 384:])
        rows.append(jnp.zeros((128 - NPANEL * SHARE, 128), F32))
        SBM[it] = jnp.sum(jnp.concatenate(rows, axis=0).T, axis=0, keepdims=True)
        SB[it, c] = SBM[it]
        copies = plane_copies(it, SBM.at[it], SB.at[it], bs, br)
        for copy in copies:
            copy.start()
        return copies

    def solve_second(it, copies):
        for copy in copies:
            copy.wait_recv()
        got = stacked(jnp.concatenate([SB[it, k] for k in range(NCOL)], axis=0))
        owner = iota((NCOL, PANEL), 1) // SHARE == iota((NCOL, PANEL), 0)
        scaled = []
        for k in range(NPANEL):
            spread = jnp.where(
                iota((128, PANEL), 0) == k * SHARE + lax.rem(iota((128, PANEL), 1), SHARE), 1.0, 0.0
            ).astype(BF16)
            value = added(dot(got, spread))
            scaled.append(jnp.sum(jnp.where(owner, value, 0.0), axis=0, keepdims=True))
        return backward_of(scaled)

    def backward_of(scaled):
        ports = [None] * NPANEL
        ports[NPANEL - 1] = scaled[NPANEL - 1]
        for k in range(NPANEL - 2, -1, -1):
            ports[k] = scaled[k] - minus_transposed(k, ports[k + 1])
        return ports

    def lifted_rows(ports, wanted):
        total = jnp.zeros((24, 128), F32)
        for k in range(NPANEL):
            parts = pieces(ports[k] * prolong_scale)
            masks = [ROWM[k : k + 1] == w for w in wanted]
            masks += [masks[0]] * (8 - len(masks))
            rows = [jnp.where(m, part, 0.0) for part in parts for m in masks]
            total = total + dot_t(jnp.concatenate(rows, axis=0).astype(BF16), LANES[k])
        return added(total)

    lane_row = iota((1, 128), 1)

    def spread_rows(rows):
        return added(dot_t(stacked(rows), E4[...]))

    def field_of(own):
        return jnp.concatenate([jnp.where(lane_row // 32 == min(a, 3), own, 0.0) for a in range(4)], axis=0)

    for j in range(NX):
        copy_sibling(j).wait_recv()
    first = solve_first(0, rhs)

    arrive(layer_copies(3))
    vert = [HALO[3, 0] + v[1] * T[1], v[0] * T[0] + HALO[3, 1]]
    for p in range(2):
        t = T[p]
        Q[p] = flat[p] - v[p] * (VS[p] * t - vert[p])
    for copy in group_second:
        copy.wait_recv()
    plane_second = gather_plane(2, Z.at[1], XM.at[1], X.at[1])
    panel.pass_y(3, 5, 4)
    panel.send_x(0, 1, 7, 2, 6, 3, 5, 4)
    ports1 = solve_second(0, first)

    own_row = c * 4 + r
    none = jnp.int32(-1)
    wanted = [
        own_row,
        jnp.where(r > 0, own_row - 1, none),
        jnp.where(r < 3, own_row + 1, none),
        jnp.where(c > 0, own_row - 4, none),
        jnp.where(c < NCOL - 1, own_row + 4, none),
    ]
    near = lifted_rows(ports1, wanted)
    level = jnp.concatenate(
        [
            field_of(near[0:1]),
            jnp.where(lane_row // 32 == 3, near[1:2], 0.0),
            jnp.where(lane_row // 32 == 0, near[2:3], 0.0),
            jnp.zeros((2, 128), F32),
        ],
        axis=0,
    )
    level = spread_rows(level)
    lift = jnp.concatenate(
        [jnp.broadcast_to(level[a : a + 1], (TILE, COLS)) for a in range(4)], axis=0
    )
    at_row = lax.rem(iota((128, 128), 1), ROWS) // TILE * 32
    pick_w = jnp.where(iota((128, 128), 0) == at_row + 31, 1.0, 0.0).astype(BF16)
    pick_e = jnp.where(iota((128, 128), 0) == at_row, 1.0, 0.0).astype(BF16)
    side_w = added(dot(stacked(near), pick_w))[3:4]
    side_e = added(dot(stacked(near), pick_e))[4:5]
    lifted_around = plane_sum(
        [s[p] * lift for p in range(2)],
        RIM[0, 0] * level[4:5],
        RIM[0, 1] * level[5:6],
        SIDE[0, 0] * side_w,
        SIDE[0, 1] * side_e,
    )
    for p in range(2):
        t3 = T[p]
        resid = Q[p] - (DP[p] * lift - s[p] * lifted_around[p])
        t = INV[p] * resid
        drop_out[p] = lift + t3
        Q[p], T[p], CH[p] = t, t, t
    send_round(4, [s[p] * T[p] for p in range(2)], [v[p] * T[p] for p in range(2)])
    panel.pass_x(0, 1, 7, 2, 6)

    lifted_map = jnp.zeros((384, 128), F32)
    for k in range(NPANEL):
        mask = row_mask(k)
        parts = [jnp.where(mask, part, 0.0).astype(BF16) for part in pieces(ports1[k] * prolong_scale)]
        lifted_map = lifted_map + dot_t(jnp.concatenate(parts, axis=0), LANES[k])
    lifted_map = added(lifted_map)
    for copy in plane_coef:
        copy.wait_recv()
    pads_map = tile_map(lambda k: CX[k, 0])
    edge_e = tile_map(lambda k: CX[k, 1])
    edge_s = tile_map(lambda k: CX[k, 2])
    lanes = iota((128, 128), 1)

    def tile_east(a):
        ahead = pltpu.roll(a, 124, 0)
        return jnp.where(lax.rem(lanes, 32) == 31, pltpu.roll(ahead, 31, 1), pltpu.roll(a, 127, 1))

    def tile_west(a):
        behind = pltpu.roll(a, 4, 0)
        return jnp.where(lax.rem(lanes, 32) == 0, pltpu.roll(behind, 97, 1), pltpu.roll(a, 1, 1))

    def tile_south(a):
        below = pltpu.roll(a, 127, 0)
        return jnp.where(lanes // 32 == 3, pltpu.roll(below, 96, 1), pltpu.roll(a, 96, 1))

    def tile_north(a):
        above = pltpu.roll(a, 1, 0)
        return jnp.where(lanes // 32 == 0, pltpu.roll(above, 32, 1), pltpu.roll(a, 32, 1))

    flow_e = edge_e * (lifted_map - tile_east(lifted_map))
    flow_s = edge_s * (lifted_map - tile_south(lifted_map))
    coarse = pads_map * lifted_map + flow_e - tile_west(flow_e) + flow_s - tile_north(flow_s)

    panel.pass_x(3, 5, 4)
    for copy in plane_second:
        copy.wait_recv()
    rhs = select_ports(tile_map(lambda k: X[1, k]) - coarse)
    rho = sweep(4, 1.0 / sigma, s, v)
    send_round(5, [s[p] * T[p] for p in range(2)], [v[p] * T[p] for p in range(2)])

    forward = forward_of(rhs)
    for k in range(NPANEL):
        FW[k : k + 1] = forward[k]
    panel.end()
    SL[l] = times(
        lambda px, py, h: GP[px, py, HALF * h : HALF * (h + 1)], FW[pl.ds(l, 1)]
    )
    second = [
        remote(SL.at[l], SL.at[l], ls.at[d - 1], lr.at[d - 1], (lax.rem(l + d, 4), r, c)) for d in range(1, 4)
    ]
    for copy in second:
        copy.start()

    for rd in range(5):
        left(layer_copies(rd))
        left(rim_copies(rd))
    lower.sent()
    panel.sent()
    for copy in group_first + group_coef + group_second:
        copy.wait_send()
    for copy in plane_first + plane_coef + plane_second + first:
        copy.wait_send()
    for j in range(NX):
        copy_sibling(j).wait_send()
    for copy in second:
        copy.wait_recv()
    ports2 = backward_of([SL[k] for k in range(NPANEL)])
    for k in range(NPANEL):
        ports_out[k : k + 1] = ports2[k]
    near = lifted_rows(ports2, [own_row])
    level = spread_rows(jnp.concatenate([field_of(near[0:1])] * 2, axis=0))
    sweep(5, rho, s, v)
    for p in range(2):
        for a in range(4):
            rows = slice(TILE * a, TILE * (a + 1))
            drop_out[p, rows] = drop_out[p, rows] + T[p, rows] + level[a : a + 1]

    left(layer_copies(5))
    left(rim_copies(5))
    for copy in second:
        copy.wait_send()


def shards(*args):
    vmem = pl.BlockSpec(memory_space=pltpu.VMEM)
    field = pltpu.VMEM((2, ROWS, COLS), F32)
    dma = pltpu.SemaphoreType.DMA
    return pl.pallas_call(
        kernel,
        out_shape=(
            jax.ShapeDtypeStruct((2, ROWS, COLS), F32),
            jax.ShapeDtypeStruct((NPANEL, PANEL), F32),
        ),
        in_specs=[pl.BlockSpec(memory_space=pl.ANY)] * 8,
        out_specs=(vmem, vmem),
        scratch_shapes=[
            field, field, field,
            pltpu.VMEM((2, ROWS, COLS), jnp.int32),
            pltpu.VMEM((ROWS, COLS), jnp.int32),
            pltpu.VMEM((NPANEL, PANEL), jnp.int32),
            pltpu.VMEM((NPANEL, SHARE, PANEL), F32),
            field, field, field, field, field, field, field, field,
            pltpu.VMEM((6, 2, ROWS, COLS), F32),
            pltpu.VMEM((6, 2, ROWS, COLS), F32),
            pltpu.VMEM((6, 2, 2, COLS), F32),
            pltpu.VMEM((6, 2, 2, COLS), F32),
            pltpu.VMEM((6, 2, 1, 128), F32),
            pltpu.VMEM((6, 2, 1, 128), F32),
            pltpu.VMEM((2, NX, NY, NPANEL - 1, HALF, PANEL), F32),
            pltpu.VMEM((NX, NY, SHARE, PANEL), F32),
            pltpu.VMEM((NPANEL, PANEL), F32),
            pltpu.VMEM((4, 1, PANEL), F32),
            pltpu.VMEM((PANEL, 128), F32),
            pltpu.VMEM((2, 1, 128), F32),
            pltpu.VMEM((2, 16, 1, 128), F32),
            pltpu.VMEM((2, 4, 128), F32),
            pltpu.VMEM((2, NCOL, 4, 128), F32),
            pltpu.VMEM((3, 128), F32),
            pltpu.VMEM((16, 3, 128), F32),
            pltpu.VMEM((3, 4, 128), F32),
            pltpu.VMEM((NCOL, 3, 4, 128), F32),
            pltpu.VMEM((2, 1, 128), F32),
            pltpu.VMEM((2, NCOL, 1, 128), F32),
            pltpu.VMEM((NPANEL, 128, PANEL), BF16),
            pltpu.VMEM((NPANEL, PANEL), jnp.int32),
            pltpu.VMEM((COLS, 128), BF16),
            dma((9,)), dma((6, 6)), dma((6, 6)),
            dma((7,)), dma((7,)),
            dma((2, 8)), dma((2, 8)),
            dma((8,)), dma((8,)),
            dma((7,)), dma((7,)),
            dma((2, 8)), dma((2, 8)),
            dma((8,)), dma((8,)),
            dma((3,)), dma((3,)),
            dma((4,)), dma((4,)),
            dma((3, 15)), dma((3, 15)),
            dma((3, 31)), dma((3, 31)),
            dma((2, 31)), dma((2, 31)),
        ],
        compiler_params=pltpu.CompilerParams(
            collective_id=0, has_side_effects=True, vmem_limit_bytes=60 * 1024 * 1024
        ),
        cost_estimate=pl.CostEstimate(flops=100_000_000, bytes_accessed=2_000_000, transcendentals=300_000),
        name="grid",
    )(*args)


def solution(mesh):
    placed = (
        P("layer", "row", "col"),
        P("layer", "row", "col"),
        P("layer", "row", "col"),
        P("layer", "row", "col"),
        P("row", "col"),
        P(),
        P(None, "col", None),
        P(None, "col", None),
    )
    return jax.shard_map(
        shards,
        mesh=mesh,
        in_specs=placed,
        out_specs=(P("layer", "row", "col"), P()),
        check_vma=False,
    )
```

```python
import jax
import jax.numpy as jnp
from jax import lax
from jax.experimental import pallas as pl
from jax.experimental.pallas import tpu as pltpu
from jax.sharding import PartitionSpec as P

F32 = jnp.float32
BF16 = jnp.bfloat16
MESH = pl.DeviceIdType.MESH

TILE = 16
PANEL = 512
NPANEL = 4
NX, NY = 4, 8
NCOL = NX * NY
ROWS, COLS = 64, 512
SHARE = PANEL // NCOL
HALF = SHARE // 2

pad_gain = 8.0
bound_low = 0.1
bound_high = 1.9
restrict_scale = 0.25
prolong_scale = 0.5
theta = (bound_high + bound_low) / 2.0
delta = (bound_high - bound_low) / 2.0
sigma = theta / delta


def iota(shape, axis):
    return lax.broadcasted_iota(jnp.int32, shape, axis)


def pieces(x):
    high = x.astype(BF16).astype(F32)
    rest = x - high
    mid = rest.astype(BF16).astype(F32)
    return high, mid, rest - mid


def stacked(x):
    return jnp.concatenate(pieces(x), axis=0).astype(BF16)


def added(y):
    n = y.shape[0] // 3
    return y[:n] + y[n : 2 * n] + y[2 * n :]


def dot(a, b):
    return lax.dot_general(a, b, (((1,), (0,)), ((), ())), preferred_element_type=F32)


def dot_t(a, b):
    return lax.dot_general(a, b, (((1,), (1,)), ((), ())), preferred_element_type=F32)


def kernel(
    src_in, cond_in, via_in, vmap_in, pad_in, pt_in, piv_in, coup_in,
    drop_out, ports_out,
    src, cond, via, vmap, pad, pt, piv,
    S, V, INV, DP, VS, Q, T, CH, HSEND, HALO, RSEND, RIM, CSEND, SIDE,
    G, GP, FW, SL, PART, ZSEND, Z, XM, X, CSND, CZ, CXM, CX, SBM, SB, LANES, ROWM, E4,
    ins, hs, hr, gys, gyr, gxs, gxr, gfs, gfr,
    pys, pyr, pxs, pxr, pfs, pfr, ls, lr, gbs, gbr, zs, zr, xs, xr, bs, br,
):
    l, r, c = lax.axis_index("layer"), lax.axis_index("row"), lax.axis_index("col")
    core = lax.rem(l, 2)
    x, y = c // NY, lax.rem(c, NY)

    def at_col(px, py):
        return (l, r, px * NY + py)

    def far(d, n, m):
        i, j = d // m, d % m
        return -(min(i, n - i) + min(j, m - j))

    group = [
        (lax.rem(l + d % 4, 4), lax.rem(r + d // 4, 4), c)
        for d in sorted(range(1, 16), key=lambda d: far(d, 4, 4) - min(d // 4, 4 - d // 4))
    ]
    plane_peers = [
        (l, r, lax.rem(c + d, NCOL)) for d in sorted(range(1, NCOL), key=lambda d: far(d, NX, NY))
    ]
    sibling = (l + 1 - 2 * core, r, c)

    barrier = pltpu.get_barrier_semaphore()
    for peer in plane_peers + group:
        pl.semaphore_signal(barrier, inc=1, device_id=peer, device_id_type=MESH)

    def remote(a, b, ssem, rsem, peer):
        return pltpu.make_async_remote_copy(
            src_ref=a, dst_ref=b, send_sem=ssem, recv_sem=rsem, device_id=peer, device_id_type=MESH
        )

    inputs = [
        pltpu.make_async_copy(a, b, ins.at[n])
        for n, (a, b) in enumerate(
            (
                (via_in, via),
                (vmap_in, vmap),
                (cond_in, cond),
                (coup_in.at[:, pl.ds(pl.multiple_of(core * HALF, HALF), HALF), :], G.at[core, x, y]),
                (src_in, src),
                (pt_in, pt),
                (pad_in, pad),
                (piv_in, piv),
                (piv_in.at[l], GP.at[x, y]),
            )
        )
    ]
    for copy in inputs:
        copy.start()

    E4[...] = jnp.where(
        iota((COLS, 128), 0) // TILE == lax.rem(iota((COLS, 128), 1), 32), 1.0, 0.0
    ).astype(BF16)

    def tile_row(plane):
        parts = [plane[TILE * a : TILE * a + 8] + plane[TILE * a + 8 : TILE * a + 16] for a in range(4)]
        sums = added(dot(stacked(jnp.concatenate(parts, axis=0)), E4[...]))
        own = iota((32, 128), 0) // 8 == iota((32, 128), 1) // 32
        return jnp.sum(jnp.where(own, sums, 0.0), axis=0, keepdims=True)

    zero_plane = jnp.zeros((ROWS, COLS), F32)

    @pl.when(l == 0)
    def _():
        for rd in range(6):
            HALO[rd, 0] = zero_plane

    @pl.when(l == 3)
    def _():
        for rd in range(6):
            HALO[rd, 1] = zero_plane

    @pl.when(r == 0)
    def _():
        for rd in range(6):
            RIM[rd, 0] = jnp.zeros((2, COLS), F32)

    @pl.when(r == 3)
    def _():
        for rd in range(6):
            RIM[rd, 1] = jnp.zeros((2, COLS), F32)

    @pl.when(c == 0)
    def _():
        for rd in range(6):
            SIDE[rd, 0] = jnp.zeros((1, 128), F32)

    @pl.when(c == NCOL - 1)
    def _():
        for rd in range(6):
            SIDE[rd, 1] = jnp.zeros((1, 128), F32)

    def layer_copies(rd):
        up = remote(HSEND.at[rd, 1], HALO.at[rd, 0], hs.at[rd, 0], hr.at[rd, 0], (lax.rem(l + 1, 4), r, c))
        down = remote(HSEND.at[rd, 0], HALO.at[rd, 1], hs.at[rd, 1], hr.at[rd, 1], (lax.rem(l + 3, 4), r, c))
        return ((l < 3, up, l > 0), (l > 0, down, l < 3))

    def rim_copies(rd):
        south = remote(RSEND.at[rd, 1], RIM.at[rd, 0], hs.at[rd, 2], hr.at[rd, 2], (l, lax.rem(r + 1, 4), c))
        north = remote(RSEND.at[rd, 0], RIM.at[rd, 1], hs.at[rd, 3], hr.at[rd, 3], (l, lax.rem(r + 3, 4), c))
        east = remote(CSEND.at[rd, 1], SIDE.at[rd, 0], hs.at[rd, 4], hr.at[rd, 4], (l, r, lax.rem(c + 1, NCOL)))
        west = remote(
            CSEND.at[rd, 0], SIDE.at[rd, 1], hs.at[rd, 5], hr.at[rd, 5], (l, r, lax.rem(c + NCOL - 1, NCOL))
        )
        return (
            (r < 3, south, r > 0),
            (r > 0, north, r < 3),
            (c < NCOL - 1, east, c > 0),
            (c > 0, west, c < NCOL - 1),
        )

    def start(copies):
        for sends, copy, _ in copies:
            @pl.when(sends)
            def _():
                copy.start()

    def arrive(copies):
        for _, copy, receives in copies:
            @pl.when(receives)
            def _():
                copy.wait_recv()

    def left(copies):
        for sends, copy, _ in copies:
            @pl.when(sends)
            def _():
                copy.wait_send()

    def send_round(rd, g, h):
        rims = rim_copies(rd)
        for p in range(2):
            RSEND[rd, 0, p : p + 1] = g[p][:1]
            RSEND[rd, 1, p : p + 1] = g[p][ROWS - 1 :]
        start(rims[:2])
        for p in range(2):
            HSEND[rd, p] = h[p]
        start(layer_copies(rd))
        first = jnp.concatenate([g[0][:, :128], g[1][:, :128]], axis=0)
        last = jnp.concatenate([g[0][:, COLS - 128 :], g[1][:, COLS - 128 :]], axis=0)
        CSEND[rd, 0] = first.T[:1]
        CSEND[rd, 1] = last.T[127:]
        start(rims[2:])

    def column(rim):
        return jnp.broadcast_to(rim, (128, 128)).T

    row_at = iota((ROWS, COLS), 0)
    col_at = iota((ROWS, 128), 1)

    def from_east(g, side):
        moved = pltpu.roll(g, COLS - 1, 1)
        edge = jnp.where(col_at == 127, side, moved[:, COLS - 128 :])
        return jnp.concatenate([moved[:, : COLS - 128], edge], axis=1)

    def from_west(g, side):
        moved = pltpu.roll(g, 1, 1)
        edge = jnp.where(col_at == 0, side, moved[:, :128])
        return jnp.concatenate([edge, moved[:, 128:]], axis=1)

    def from_south(g, rim):
        return jnp.where(row_at == ROWS - 1, rim, pltpu.roll(g, ROWS - 1, 0))

    def from_north(g, rim):
        return jnp.where(row_at == 0, rim, pltpu.roll(g, 1, 0))

    def plane_sum(g, north, south, west, east):
        west, east = column(west), column(east)
        out = []
        for p in range(2):
            rows = slice(ROWS * p, ROWS * (p + 1))
            out.append(
                from_north(g[p], north[p : p + 1])
                + from_south(g[p], south[p : p + 1])
                + from_west(g[p], west[rows])
                + from_east(g[p], east[rows])
            )
        return out

    def received_sum(rd, g):
        return plane_sum(g, RIM[rd, 0], RIM[rd, 1], SIDE[rd, 0], SIDE[rd, 1])

    def group_copies(it, rows, buf, send):
        slot = r * 4 + l
        return [
            remote(send, buf.at[slot], zs.at[it, d], zr.at[it, d], peer) for d, peer in enumerate(group)
        ]

    def plane_copies(it, send, buf, ss, rs):
        return [remote(send, buf.at[c], ss.at[it, d], rs.at[it, d], peer) for d, peer in enumerate(plane_peers)]

    for copy in inputs[:3]:
        copy.wait()
    for p in range(2):
        S[p] = jnp.sqrt(cond[p])
        V[p] = jnp.sqrt(via[p]) * vmap[p].astype(F32)
    for copy in inputs[3:5]:
        copy.wait()

    pl.semaphore_wait(barrier, 15 + 31)

    send_round(0, [S[0], S[1]], [V[0], V[1]])

    turn = 1 - 2 * core

    class Ring:
        def __init__(self, slot, ys, yr, xs, xr, fs, fr):
            self.slot, self.xs, self.xr, self.fs, self.fr = slot, xs, xr, fs, fr
            self.along_y = {}
            for d, began, step in (
                (1, 0, 1), (7, 0, NY - 1), (2, 0, 2), (6, 0, NY - 2),
                (3, 1, 2), (5, NY - 1, NY - 2), (4, 2 * turn + NY, 2 * turn + NY),
            ):
                piece = slot(x, lax.rem(y + 2 * NY - began, NY))
                self.along_y[d] = remote(
                    piece, piece, ys.at[d - 1], yr.at[d - 1], at_col(x, lax.rem(y + step, NY))
                )

        def along_x(self, d):
            piece = self.slot(x, lax.rem(y + NY - d, NY))
            return [
                remote(piece, piece, self.xs.at[s, d], self.xr.at[s, d], at_col(lax.rem(x + step, NX), y))
                for s, step in enumerate((1, 3))
            ]

        def onward(self, d):
            piece = self.slot(lax.rem(x - turn + NX, NX), lax.rem(y + NY - d, NY))
            return remote(piece, piece, self.fs.at[d], self.fr.at[d], at_col(lax.rem(x + turn + NX, NX), y))

        def begin(self):
            for d in (1, 7, 2, 6):
                self.along_y[d].start()

        def pass_y(self, *ds):
            for d in ds:
                self.along_y[d].wait_recv()
            for d in ds:
                if d in (1, 7):
                    self.along_y[{1: 3, 7: 5}[d]].start()
            if 2 in ds:
                self.along_y[4].start()

        def send_x(self, *ds):
            for d in ds:
                for copy in self.along_x(d):
                    copy.start()

        def pass_x(self, *ds):
            for d in ds:
                for copy in self.along_x(d):
                    copy.wait_recv()
                self.onward(d).start()

        def end(self):
            for d in range(NY):
                self.onward(d).wait_recv()

        def sent(self):
            for d in range(1, NY):
                self.along_y[d].wait_send()
            for d in range(NY):
                for copy in self.along_x(d):
                    copy.wait_send()
                self.onward(d).wait_send()

    lower = Ring(lambda px, py: G.at[core, px, py], gys, gyr, gxs, gxr, gfs, gfr)
    panel = Ring(lambda px, py: GP.at[px, py], pys, pyr, pxs, pxr, pfs, pfr)

    def copy_sibling(j):
        block = G.at[core, lax.rem(x + j, NX)]
        return remote(block, block, gbs.at[j], gbr.at[j], sibling)

    lower.begin()
    lower.send_x(0)
    ZSEND[0] = tile_row(src[0] + src[1])
    group_first = group_copies(0, 1, Z.at[0], ZSEND.at[0])
    for copy in group_first:
        copy.start()

    for copy in inputs[5:]:
        copy.wait()
    for k in range(NPANEL):
        tile = pt[k : k + 1, :]
        arow, acol = tile // 1024, lax.rem(tile, 1024)
        lane = lax.rem(arow, 4) * 32 + lax.rem(acol, 32)
        LANES[k] = jnp.where(iota((128, PANEL), 0) == lane, 1.0, 0.0).astype(BF16)
        ROWM[k : k + 1] = (acol // 32) * 4 + arow // 4

    arrive(rim_copies(0))
    lower.pass_y(1, 7)
    lower.send_x(1, 7)
    arrive(layer_copies(0))
    s = [S[0], S[1]]
    v = [V[0], V[1]]
    around = received_sum(0, s)
    top = (l == 3).astype(F32)
    pads = pad_gain * pad[...].astype(F32) * top
    vsum = [HALO[0, 0] + v[1], v[0] + HALO[0, 1]]
    for p in range(2):
        dp = s[p] * around[p]
        if p == 1:
            dp = dp + pads
        inv = 1.0 / (dp + v[p] * vsum[p])
        t = inv * src[p]
        DP[p], INV[p], VS[p], Q[p], T[p], CH[p] = dp, inv, vsum[p], t, t, t
    send_round(1, [s[p] * T[p] for p in range(2)], [v[p] * T[p] for p in range(2)])

    lower.pass_y(2, 6)
    lower.send_x(2, 6)

    def gather_plane(it, buf, msg, bufx):
        for q in range(4):
            total = buf[4 * q]
            for k in range(1, 4):
                total = total + buf[4 * q + k]
            msg[q : q + 1] = total
        bufx[c] = msg[...]
        out = plane_copies(it, msg, bufx, xs, xr)
        for copy in out:
            copy.start()
        return out

    Z[0, r * 4 + l] = ZSEND[0]
    for copy in group_first:
        copy.wait_recv()
    plane_first = gather_plane(0, Z.at[0], XM.at[0], X.at[0])

    west_col, east_col = SIDE[0, 0], SIDE[0, 1]
    east_side = column(east_col)
    edge_e = jnp.zeros((ROWS, COLS), F32)
    edge_s = jnp.zeros((ROWS, COLS), F32)
    for p in range(2):
        edge_e = edge_e + s[p] * from_east(s[p], east_side[ROWS * p : ROWS * (p + 1)])
        edge_s = edge_s + s[p] * from_south(s[p], RIM[0, 1, p : p + 1])
    edge_e = jnp.where(lax.rem(iota((ROWS, COLS), 1), TILE) == TILE - 1, edge_e, 0.0)
    edge_s = jnp.where(lax.rem(iota((ROWS, COLS), 0), TILE) == TILE - 1, edge_s, 0.0)
    for k, field in enumerate((pads, edge_e, edge_s)):
        CSND[k : k + 1] = tile_row(field)
    CZ[r * 4 + l] = CSND[...]
    group_coef = group_copies(1, 3, CZ, CSND)
    for copy in group_coef:
        copy.start()


    lower.pass_y(3, 5, 4)
    lower.send_x(3, 5, 4)
    lower.pass_x(0, 1, 7)

    def sweep(rd, rho, s, v):
        rho_new = 1.0 / (2.0 * sigma - rho)
        t = [T[0], T[1]]
        arrive(rim_copies(rd))
        around = received_sum(rd, [s[p] * t[p] for p in range(2)])
        arrive(layer_copies(rd))
        vert = [HALO[rd, 0] + v[1] * t[1], v[0] * t[0] + HALO[rd, 1]]
        for p in range(2):
            remain = Q[p] - t[p] + INV[p] * (s[p] * around[p] + v[p] * vert[p])
            ch = (rho_new * rho) * CH[p] + (2.0 * rho_new / delta) * remain
            CH[p] = ch
            T[p] = t[p] + ch
        return rho_new

    rho = sweep(1, 1.0 / sigma, s, v)
    send_round(2, [s[p] * T[p] for p in range(2)], [v[p] * T[p] for p in range(2)])

    lower.pass_x(2, 6)
    copy_sibling(0).start()
    for copy in group_coef:
        copy.wait_recv()
    for q in range(4):
        total = CZ[4 * q]
        for k in range(1, 4):
            total = total + CZ[4 * q + k]
        for k in range(3):
            CXM[k, q : q + 1] = total[k : k + 1]
    CX[c] = CXM[...]
    plane_coef = plane_copies(1, CXM, CX, xs, xr)
    for copy in plane_coef:
        copy.start()
    lower.pass_x(3, 5, 4)
    copy_sibling(1).start()
    copy_sibling(3).start()

    sweep(2, rho, s, v)
    send_round(3, [s[p] * T[p] for p in range(2)], [v[p] * T[p] for p in range(2)])

    panel.begin()

    def tile_map(load):
        return jnp.concatenate([load(k) for k in range(NCOL)], axis=0)

    def row_mask(k):
        return iota((128, PANEL), 0) == ROWM[k : k + 1]

    def select_ports(tiles):
        parts = stacked(tiles)
        out = []
        for k in range(NPANEL):
            picked = added(dot(parts, LANES[k]))
            out.append(
                jnp.sum(jnp.where(row_mask(k), picked, 0.0), axis=0, keepdims=True) * (restrict_scale / TILE)
            )
        return out

    for copy in plane_first:
        copy.wait_recv()
    rhs = select_ports(tile_map(lambda k: X[0, k]))

    lower.end()
    copy_sibling(2).start()
    panel.pass_y(1, 7, 2, 6)

    arrive(rim_copies(3))
    around = received_sum(3, [s[p] * T[p] for p in range(2)])
    flat = [src[p] - (DP[p] * T[p] - s[p] * around[p]) for p in range(2)]
    ZSEND[1] = tile_row(flat[0] + flat[1])
    Z[1, r * 4 + l] = ZSEND[1]
    group_second = group_copies(2, 1, Z.at[1], ZSEND.at[1])
    for copy in group_second:
        copy.start()

    def times(block, f):
        wide = jnp.broadcast_to(f, (8, PANEL))

        def body(i, carry):
            px, py = i // NY, lax.rem(i, NY)
            for h in range(2):
                prod = block(px, py, h) * wide
                part = prod[:, :128] + prod[:, 128:256] + prod[:, 256:384] + prod[:, 384:]
                PART[pl.ds(pl.multiple_of(i * SHARE + h * HALF, HALF), HALF)] = part
            return carry

        lax.fori_loop(0, NCOL, body, 0, unroll=NCOL)
        return jnp.concatenate(
            [jnp.sum(PART[128 * j : 128 * (j + 1)].T, axis=0, keepdims=True) for j in range(4)], axis=1
        )

    def minus_transposed(k, f):
        for j in range(4):
            PART[128 * j : 128 * (j + 1)] = column(f[:, 128 * j : 128 * (j + 1)])

        def body(i, acc):
            px, py = i // NY, lax.rem(i, NY)
            for h in range(2):
                w = PART[pl.ds(pl.multiple_of(i * SHARE + h * HALF, HALF), HALF)]
                acc = acc + G[h, px, py, k] * jnp.concatenate([w] * 4, axis=1)
            return acc

        acc = lax.fori_loop(0, NCOL, body, jnp.zeros((8, PANEL), F32), unroll=NCOL)
        return jnp.sum(acc, axis=0, keepdims=True)

    def forward_of(rhs):
        forward = [rhs[0]]
        for k in range(1, NPANEL):
            forward.append(rhs[k] - times(lambda px, py, h: G[h, px, py, k - 1], forward[-1]))
        return forward

    def solve_first(it, rhs):
        forward = forward_of(rhs)
        rows = []
        for k in range(NPANEL):
            prod = piv[k] * forward[k]
            rows.append(prod[:, :128] + prod[:, 128:256] + prod[:, 256:384] + prod[:, 384:])
        rows.append(jnp.zeros((128 - NPANEL * SHARE, 128), F32))
        SBM[it] = jnp.sum(jnp.concatenate(rows, axis=0).T, axis=0, keepdims=True)
        SB[it, c] = SBM[it]
        copies = plane_copies(it, SBM.at[it], SB.at[it], bs, br)
        for copy in copies:
            copy.start()
        return copies

    def solve_second(it, copies):
        for copy in copies:
            copy.wait_recv()
        got = stacked(jnp.concatenate([SB[it, k] for k in range(NCOL)], axis=0))
        owner = iota((NCOL, PANEL), 1) // SHARE == iota((NCOL, PANEL), 0)
        scaled = []
        for k in range(NPANEL):
            spread = jnp.where(
                iota((128, PANEL), 0) == k * SHARE + lax.rem(iota((128, PANEL), 1), SHARE), 1.0, 0.0
            ).astype(BF16)
            value = added(dot(got, spread))
            scaled.append(jnp.sum(jnp.where(owner, value, 0.0), axis=0, keepdims=True))
        return backward_of(scaled)

    def backward_of(scaled):
        ports = [None] * NPANEL
        ports[NPANEL - 1] = scaled[NPANEL - 1]
        for k in range(NPANEL - 2, -1, -1):
            ports[k] = scaled[k] - minus_transposed(k, ports[k + 1])
        return ports

    def lifted_rows(ports, wanted):
        total = jnp.zeros((24, 128), F32)
        for k in range(NPANEL):
            parts = pieces(ports[k] * prolong_scale)
            masks = [ROWM[k : k + 1] == w for w in wanted]
            masks += [masks[0]] * (8 - len(masks))
            rows = [jnp.where(m, part, 0.0) for part in parts for m in masks]
            total = total + dot_t(jnp.concatenate(rows, axis=0).astype(BF16), LANES[k])
        return added(total)

    lane_row = iota((1, 128), 1)

    def spread_rows(rows):
        return added(dot_t(stacked(rows), E4[...]))

    def field_of(own):
        return jnp.concatenate([jnp.where(lane_row // 32 == min(a, 3), own, 0.0) for a in range(4)], axis=0)

    for j in range(NX):
        copy_sibling(j).wait_recv()
    first = solve_first(0, rhs)

    arrive(layer_copies(3))
    vert = [HALO[3, 0] + v[1] * T[1], v[0] * T[0] + HALO[3, 1]]
    for p in range(2):
        t = T[p]
        Q[p] = flat[p] - v[p] * (VS[p] * t - vert[p])
    for copy in group_second:
        copy.wait_recv()
    plane_second = gather_plane(2, Z.at[1], XM.at[1], X.at[1])
    panel.pass_y(3, 5, 4)
    panel.send_x(0, 1, 7, 2, 6, 3, 5, 4)
    ports1 = solve_second(0, first)

    own_row = c * 4 + r
    none = jnp.int32(-1)
    wanted = [
        own_row,
        jnp.where(r > 0, own_row - 1, none),
        jnp.where(r < 3, own_row + 1, none),
        jnp.where(c > 0, own_row - 4, none),
        jnp.where(c < NCOL - 1, own_row + 4, none),
    ]
    near = lifted_rows(ports1, wanted)
    level = jnp.concatenate(
        [
            field_of(near[0:1]),
            jnp.where(lane_row // 32 == 3, near[1:2], 0.0),
            jnp.where(lane_row // 32 == 0, near[2:3], 0.0),
            jnp.zeros((2, 128), F32),
        ],
        axis=0,
    )
    level = spread_rows(level)
    lift = jnp.concatenate(
        [jnp.broadcast_to(level[a : a + 1], (TILE, COLS)) for a in range(4)], axis=0
    )
    at_row = lax.rem(iota((128, 128), 1), ROWS) // TILE * 32
    pick_w = jnp.where(iota((128, 128), 0) == at_row + 31, 1.0, 0.0).astype(BF16)
    pick_e = jnp.where(iota((128, 128), 0) == at_row, 1.0, 0.0).astype(BF16)
    side_w = added(dot(stacked(near), pick_w))[3:4]
    side_e = added(dot(stacked(near), pick_e))[4:5]
    lifted_around = plane_sum(
        [s[p] * lift for p in range(2)],
        RIM[0, 0] * level[4:5],
        RIM[0, 1] * level[5:6],
        SIDE[0, 0] * side_w,
        SIDE[0, 1] * side_e,
    )
    for p in range(2):
        t3 = T[p]
        resid = Q[p] - (DP[p] * lift - s[p] * lifted_around[p])
        t = INV[p] * resid
        drop_out[p] = lift + t3
        Q[p], T[p], CH[p] = t, t, t
    send_round(4, [s[p] * T[p] for p in range(2)], [v[p] * T[p] for p in range(2)])
    panel.pass_x(0, 1, 7, 2, 6)

    lifted_map = jnp.zeros((384, 128), F32)
    for k in range(NPANEL):
        mask = row_mask(k)
        parts = [jnp.where(mask, part, 0.0).astype(BF16) for part in pieces(ports1[k] * prolong_scale)]
        lifted_map = lifted_map + dot_t(jnp.concatenate(parts, axis=0), LANES[k])
    lifted_map = added(lifted_map)
    for copy in plane_coef:
        copy.wait_recv()
    pads_map = tile_map(lambda k: CX[k, 0])
    edge_e = tile_map(lambda k: CX[k, 1])
    edge_s = tile_map(lambda k: CX[k, 2])
    lanes = iota((128, 128), 1)

    def tile_east(a):
        ahead = pltpu.roll(a, 124, 0)
        return jnp.where(lax.rem(lanes, 32) == 31, pltpu.roll(ahead, 31, 1), pltpu.roll(a, 127, 1))

    def tile_west(a):
        behind = pltpu.roll(a, 4, 0)
        return jnp.where(lax.rem(lanes, 32) == 0, pltpu.roll(behind, 97, 1), pltpu.roll(a, 1, 1))

    def tile_south(a):
        below = pltpu.roll(a, 127, 0)
        return jnp.where(lanes // 32 == 3, pltpu.roll(below, 96, 1), pltpu.roll(a, 96, 1))

    def tile_north(a):
        above = pltpu.roll(a, 1, 0)
        return jnp.where(lanes // 32 == 0, pltpu.roll(above, 32, 1), pltpu.roll(a, 32, 1))

    flow_e = edge_e * (lifted_map - tile_east(lifted_map))
    flow_s = edge_s * (lifted_map - tile_south(lifted_map))
    coarse = pads_map * lifted_map + flow_e - tile_west(flow_e) + flow_s - tile_north(flow_s)

    panel.pass_x(3, 5, 4)
    for copy in plane_second:
        copy.wait_recv()
    rhs = select_ports(tile_map(lambda k: X[1, k]) - coarse)
    rho = sweep(4, 1.0 / sigma, s, v)
    send_round(5, [s[p] * T[p] for p in range(2)], [v[p] * T[p] for p in range(2)])

    forward = forward_of(rhs)
    for k in range(NPANEL):
        FW[k : k + 1] = forward[k]
    panel.end()
    SL[l] = times(
        lambda px, py, h: GP[px, py, HALF * h : HALF * (h + 1)], FW[pl.ds(l, 1)]
    )
    second = [
        remote(SL.at[l], SL.at[l], ls.at[d - 1], lr.at[d - 1], (lax.rem(l + d, 4), r, c)) for d in range(1, 4)
    ]
    for copy in second:
        copy.start()

    for rd in range(5):
        left(layer_copies(rd))
        left(rim_copies(rd))
    lower.sent()
    panel.sent()
    for copy in group_first + group_coef + group_second:
        copy.wait_send()
    for copy in plane_first + plane_coef + plane_second + first:
        copy.wait_send()
    for j in range(NX):
        copy_sibling(j).wait_send()
    for copy in second:
        copy.wait_recv()
    ports2 = backward_of([SL[k] for k in range(NPANEL)])
    for k in range(NPANEL):
        ports_out[k : k + 1] = ports2[k]
    near = lifted_rows(ports2, [own_row])
    level = spread_rows(jnp.concatenate([field_of(near[0:1])] * 2, axis=0))
    sweep(5, rho, s, v)
    for p in range(2):
        for a in range(4):
            rows = slice(TILE * a, TILE * (a + 1))
            drop_out[p, rows] = drop_out[p, rows] + T[p, rows] + level[a : a + 1]

    left(layer_copies(5))
    left(rim_copies(5))
    for copy in second:
        copy.wait_send()


def shards(*args):
    vmem = pl.BlockSpec(memory_space=pltpu.VMEM)
    field = pltpu.VMEM((2, ROWS, COLS), F32)
    dma = pltpu.SemaphoreType.DMA
    return pl.pallas_call(
        kernel,
        out_shape=(
            jax.ShapeDtypeStruct((2, ROWS, COLS), F32),
            jax.ShapeDtypeStruct((NPANEL, PANEL), F32),
        ),
        in_specs=[pl.BlockSpec(memory_space=pl.ANY)] * 8,
        out_specs=(vmem, vmem),
        scratch_shapes=[
            field, field, field,
            pltpu.VMEM((2, ROWS, COLS), jnp.int32),
            pltpu.VMEM((ROWS, COLS), jnp.int32),
            pltpu.VMEM((NPANEL, PANEL), jnp.int32),
            pltpu.VMEM((NPANEL, SHARE, PANEL), F32),
            field, field, field, field, field, field, field, field,
            pltpu.VMEM((6, 2, ROWS, COLS), F32),
            pltpu.VMEM((6, 2, ROWS, COLS), F32),
            pltpu.VMEM((6, 2, 2, COLS), F32),
            pltpu.VMEM((6, 2, 2, COLS), F32),
            pltpu.VMEM((6, 2, 1, 128), F32),
            pltpu.VMEM((6, 2, 1, 128), F32),
            pltpu.VMEM((2, NX, NY, NPANEL - 1, HALF, PANEL), F32),
            pltpu.VMEM((NX, NY, SHARE, PANEL), F32),
            pltpu.VMEM((NPANEL, PANEL), F32),
            pltpu.VMEM((4, 1, PANEL), F32),
            pltpu.VMEM((PANEL, 128), F32),
            pltpu.VMEM((2, 1, 128), F32),
            pltpu.VMEM((2, 16, 1, 128), F32),
            pltpu.VMEM((2, 4, 128), F32),
            pltpu.VMEM((2, NCOL, 4, 128), F32),
            pltpu.VMEM((3, 128), F32),
            pltpu.VMEM((16, 3, 128), F32),
            pltpu.VMEM((3, 4, 128), F32),
            pltpu.VMEM((NCOL, 3, 4, 128), F32),
            pltpu.VMEM((2, 1, 128), F32),
            pltpu.VMEM((2, NCOL, 1, 128), F32),
            pltpu.VMEM((NPANEL, 128, PANEL), BF16),
            pltpu.VMEM((NPANEL, PANEL), jnp.int32),
            pltpu.VMEM((COLS, 128), BF16),
            dma((9,)), dma((6, 6)), dma((6, 6)),
            dma((7,)), dma((7,)),
            dma((2, 8)), dma((2, 8)),
            dma((8,)), dma((8,)),
            dma((7,)), dma((7,)),
            dma((2, 8)), dma((2, 8)),
            dma((8,)), dma((8,)),
            dma((3,)), dma((3,)),
            dma((4,)), dma((4,)),
            dma((3, 15)), dma((3, 15)),
            dma((3, 31)), dma((3, 31)),
            dma((2, 31)), dma((2, 31)),
        ],
        compiler_params=pltpu.CompilerParams(
            collective_id=0, has_side_effects=True, vmem_limit_bytes=60 * 1024 * 1024
        ),
        cost_estimate=pl.CostEstimate(flops=100_000_000, bytes_accessed=2_000_000, transcendentals=300_000),
        name="grid",
    )(*args)


def solution(mesh):
    placed = (
        P("layer", "row", "col"),
        P("layer", "row", "col"),
        P("layer", "row", "col"),
        P("layer", "row", "col"),
        P("row", "col"),
        P(),
        P(None, "col", None),
        P(None, "col", None),
    )
    return jax.shard_map(
        shards,
        mesh=mesh,
        in_specs=placed,
        out_specs=(P("layer", "row", "col"), P()),
        check_vma=False,
    )
```
